256 devices in a mesh: shot: 8 (over y, x_hi), lat: 32 (over z, x_lo, core).
Axes of the slice: x: 4 (x_hi: 2, x_lo: 2; x = x_hi * 2 + x_lo), y: 4, z: 8, core: 2. Of those that a mesh axis runs over, the one named last changes fastest.
Arguments:
- partials: bfloat16 [16, 8, 2048, 2048], P('shot', None, 'lat'), may hold values from -2.5 to 2.5
- wedges: int32 [2048, 2048], P('lat'), may hold values from 0 to 15
- levels: float32 [16], replicated, may hold values from 0.25 to 1.5
Outputs:
- filtered: float32 [8, 2048, 2048], P('shot', 'lat')
The draws below stay inside these ranges and needn't reach their ends.
All inputs are finite; a program needn't handle non-finite values.
Results may differ from the reference program's by a relative error of at most 0.03.
Values may be sent and summed in bfloat16 or wider, within the bound.
A program may use at most 64 MiB of HBM per device.

```python
import math
import jax
import jax.numpy as jnp
from jax import lax

NX = 2048
NY = 2048
WEDGES = 16
SHOT_DEV = 2
SHOTS = 16
Z = 8
N_SHOT = 8


def set_ends(values, key, low, top_value):
    place = [jax.random.randint(jax.random.fold_in(key, axis), (), 0, length) for axis, length in enumerate(values.shape)]
    longest = values.shape.index(max(values.shape))
    neighbour = place[:longest] + [(place[longest] + 1) % values.shape[longest]] + place[longest + 1:]
    return values.at[tuple(place)].set(low).at[tuple(neighbour)].set(top_value)


def level_of(stream_key, extent, split, smallest, top_value):
    gain = 1.0
    for position, parts in split:
        draws = jax.random.uniform(jax.random.fold_in(jax.random.fold_in(stream_key, 6), position), (parts,), jnp.float32, smallest / len(split), top_value / len(split))
        gain = gain * jnp.repeat(jnp.exp(draws), extent[position] // parts).reshape((-1,) + (1,) * (len(extent) - 1 - position))
    return gain


def gaussian(stream_key, extent, width, limit, cuts=(), kind=jnp.bfloat16):
    entries = jax.random.normal(stream_key, extent, jnp.float32) * width
    if len(cuts) > 0:
        entries = level_of(stream_key, extent, cuts, -0.22, 0.18) * entries
    return jnp.clip(entries, min=-limit, max=limit).astype(kind)


def setup_inputs(seed: int = 0) -> dict:
    splits = jax.random.split(jax.random.key(seed), 4)
    return {
        "partials": gaussian(splits[0], (SHOTS, Z, NX, NY), 0.25, 2.5, ((0, 8), (2, 32))),
        "wedges": set_ends(jax.random.randint(splits[1], (NY, NX), 0, WEDGES), jax.random.fold_in(splits[1], 1), 0, WEDGES - 1).astype(jnp.int32),
        "levels": jnp.clip(jnp.exp(jax.random.uniform(splits[2], (WEDGES,), jnp.float32, math.log(0.25), math.log(1.5))), 0.25, 1.5),
    }


def split_length(length):
    first = max((d for d in range(1, math.isqrt(length) + 1) if length % d == 0))
    return (first, length // first)

def small_tables(length):
    indices = jnp.arange(length, dtype=jnp.int32)
    products = indices[:, None] * indices[None, :] % length
    angles = products.astype(jnp.float32) * (2.0 * math.pi / length)
    return (jnp.cos(angles).astype(jnp.bfloat16), jnp.sin(angles).astype(jnp.bfloat16))

def twiddles(first, second):
    length = first * second
    rows_idx = jnp.arange(first, dtype=jnp.int32)
    cols_idx = jnp.arange(second, dtype=jnp.int32)
    products = rows_idx[:, None] * cols_idx[None, :] % length
    angles = products.astype(jnp.float32) * (2.0 * math.pi / length)
    return (jnp.cos(angles), jnp.sin(angles))

def contract_one(data, table):
    return jnp.einsum('...ab,ak->...kb', data.astype(jnp.float32), table.astype(jnp.float32))

def contract_two(data, table):
    return jnp.einsum('...kb,bq->...kq', data.astype(jnp.float32), table.astype(jnp.float32))

def section_one(real, imag, sign, length, first_row):
    first, second = split_length(length)
    cosine, sine = small_tables(first)
    source = real if real is not None else imag
    rows = source.shape[-1] // second
    cosine = cosine[first_row:first_row + rows]
    sine = sine[first_row:first_row + rows]
    shape = source.shape[:-1] + (rows, second)
    acc_real = jnp.zeros(source.shape[:-1] + (first, second), jnp.float32)
    acc_imag = jnp.zeros(source.shape[:-1] + (first, second), jnp.float32)
    if real is not None:
        folded = real.reshape(shape)
        acc_real = acc_real + contract_one(folded, cosine)
        acc_imag = acc_imag + sign * contract_one(folded, sine)
    if imag is not None:
        folded = imag.reshape(shape)
        acc_real = acc_real - sign * contract_one(folded, sine)
        acc_imag = acc_imag + contract_one(folded, cosine)
    return (acc_real, acc_imag)

def section_two(acc_real, acc_imag, sign):
    first = acc_real.shape[-2]
    second = acc_real.shape[-1]
    turn_cos, turn_sin = twiddles(first, second)
    mid_real = (acc_real * turn_cos - sign * acc_imag * turn_sin).astype(jnp.bfloat16)
    mid_imag = (acc_imag * turn_cos + sign * acc_real * turn_sin).astype(jnp.bfloat16)
    cosine, sine = small_tables(second)
    out_real = contract_two(mid_real, cosine) - sign * contract_two(mid_imag, sine)
    out_imag = contract_two(mid_imag, cosine) + sign * contract_two(mid_real, sine)
    shape = acc_real.shape[:-2] + (first * second,)
    out_real = jnp.swapaxes(out_real, -1, -2).reshape(shape)
    out_imag = jnp.swapaxes(out_imag, -1, -2).reshape(shape)
    return (out_real, out_imag)

def transform(real, imag, sign, length):
    acc_real, acc_imag = section_one(real, imag, sign, length, 0)
    return section_two(acc_real, acc_imag, sign)

def reference(partials, wedges, levels):
    scale_cols = 1.0 / math.sqrt(NY)
    scale_rows = 1.0 / math.sqrt(NX)
    levels_cell = levels[wedges]

    def one_slice(slice_index):
        slab_data = lax.dynamic_index_in_dim(partials, slice_index, 1, keepdims=False)
        groups = lax.optimization_barrier(jnp.sum(slab_data.astype(jnp.float32).reshape(N_SHOT, SHOT_DEV, NX, NY), axis=1))
        groups = lax.optimization_barrier(groups.astype(jnp.bfloat16)).astype(jnp.float32)
        stacked = lax.optimization_barrier(jnp.sum(groups, axis=0)).astype(jnp.bfloat16)
        real_a, imag_a = transform(stacked, None, -1.0, NY)
        real_one = (real_a * scale_cols).astype(jnp.bfloat16)
        imag_one = (imag_a * scale_cols).astype(jnp.bfloat16)
        real_b, imag_b = transform(real_one.T, imag_one.T, -1.0, NX)
        real_two = real_b * scale_rows
        imag_two = imag_b * scale_rows
        magnitude = jnp.sqrt(real_two * real_two + imag_two * imag_two)
        factor = jnp.maximum(magnitude - levels_cell, 0.0) / jnp.maximum(magnitude, levels_cell)
        kept_real = (real_two * factor).astype(jnp.bfloat16)
        kept_imag = (imag_two * factor).astype(jnp.bfloat16)
        real_c, imag_c = transform(kept_real, kept_imag, 1.0, NX)
        back_real = (real_c * scale_rows).astype(jnp.bfloat16)
        back_imag = (imag_c * scale_rows).astype(jnp.bfloat16)
        real_d, imag_d = transform(back_real.T, back_imag.T, 1.0, NY)
        return real_d * scale_cols
    return lax.map(one_slice, jnp.arange(Z, dtype=jnp.int32))
```

```python
import functools
import math

import jax
import jax.numpy as jnp
import ml_dtypes
import numpy as np
from jax import lax
from jax.experimental import pallas as pl
from jax.experimental.pallas import tpu as pltpu
from jax.sharding import PartitionSpec as P

MESH = pl.DeviceIdType.MESH
F32 = jnp.float32
BF16 = jnp.bfloat16
N = 2048
LAT = 32
ROWS = N // LAT
CHUNKS = 4
CROWS = ROWS // CHUNKS
HALF = math.sqrt(0.5)
NT = (((1,), (1,)), ((), ()))


def owned():
    ky = np.zeros((LAT, 32), np.int64)
    for d in range(LAT):
        for i in range(8):
            for s in (1, 2, 3):
                ky[d, 8 * s + i] = 64 * d + 8 * i + s
        for i in range(4):
            ky[d, i] = 64 * d + 8 * i + 4
        for i in range(4, 7):
            ky[d, i] = 64 * d + 8 * (i - 3)
        ky[d, 7] = 64 * d + (32 if d < 16 else 0)
    return ky


def forward_tables():
    ky = owned()
    y2 = np.arange(256)
    scale = 1.0 / math.sqrt(N)
    parts = []
    for s in range(4):
        rows = ky[:, 8 * s : 8 * s + 8].reshape(-1)
        angle = 2.0 * np.pi * ((rows[:, None] * y2[None, :]) % N) / N
        re, im = np.cos(angle), -np.sin(angle)
        if s == 0:
            packed = 16 * 8 + 7
            re[packed] = 1.0
            im[packed] = np.where(y2 % 2, -1.0, 1.0)
            four = (rows % 8 == 4)[:, None]
            zero = np.zeros_like(re)
            parts += [
                np.where(four, zero, re),
                np.where(four, re, zero),
                np.where(four, zero, im),
                np.where(four, im, zero),
            ]
        else:
            parts += [re, im]
    return (np.concatenate(parts, axis=1) * scale).astype(ml_dtypes.bfloat16)


def inverse_tables():
    ky = owned()
    y2 = np.arange(256)
    scale = 1.0 / math.sqrt(N)
    parts = []
    for s in range(4):
        rows = ky[:, 8 * s : 8 * s + 8].reshape(-1)
        angle = 2.0 * np.pi * ((rows[:, None] * y2[None, :]) % N) / N
        cos, sin = 2.0 * np.cos(angle), 2.0 * np.sin(angle)
        if s == 0:
            packed = 16 * 8 + 7
            cos[packed] = 1.0
            sin[packed] = -np.where(y2 % 2, -1.0, 1.0)
            four = (rows % 8 == 4)[:, None]
            zero = np.zeros_like(cos)
            top = np.concatenate([np.where(four, zero, cos), np.where(four, cos, zero)], axis=1)
            low = np.concatenate([np.where(four, zero, -sin), np.where(four, -sin, zero)], axis=1)
        else:
            top = np.concatenate([cos, sin], axis=1)
            low = np.concatenate([-sin, cos], axis=1)
        parts += [top, low]
    return (np.concatenate(parts, axis=0) * scale).astype(ml_dtypes.bfloat16)


def lateral_tables():
    index = np.arange(128)
    angle = 2.0 * np.pi * ((index[:, None] * index[None, :]) % 128) / 128
    cos, sin = np.cos(angle), np.sin(angle)
    forward = np.block([[cos, -sin], [sin, cos]])
    inverse = np.block([[cos, sin], [-sin, cos]])
    return np.concatenate([forward, inverse], axis=0).astype(ml_dtypes.bfloat16)


def turn_tables():
    angle = 2.0 * np.pi * (np.arange(16)[:, None] * np.arange(128)[None, :]) / N
    scale = 1.0 / math.sqrt(N)
    cos, sin = np.cos(angle) * scale, np.sin(angle) * scale
    return np.stack([cos, -sin, 0.5 * cos, 0.5 * sin]).astype(np.float32)


def pick_tables():
    own = np.zeros((48, 64))
    mirror = np.zeros((48, 64))
    for i in range(8):
        for s in (1, 2, 3):
            own[8 * s + i, 8 * i + s] = 1
            mirror[8 * s + i, 8 * (7 - i) + 8 - s] = 1
    for i in range(4):
        own[i, 8 * i + 4] = 1
        mirror[i, 8 * (7 - i) + 4] = 1
    for i in range(4, 7):
        own[i, 8 * (i - 3)] = 1
        mirror[i, 8 * (11 - i)] = 1
    own[7, 32] = mirror[7, 32] = 1
    own[39, 0] = mirror[39, 0] = 1
    return np.concatenate([own, mirror], axis=0).astype(ml_dtypes.bfloat16)


def lane_tables():
    lanes = np.arange(128)
    place = (lanes % 16) * 8 + lanes // 16
    own = np.zeros((128, 128))
    own[lanes, place] = 1
    mirror = np.zeros((256, 128))
    mirror[128 - lanes, place] = 1
    return np.concatenate([own, mirror], axis=0).astype(ml_dtypes.bfloat16)


def turn(pair, step, length, sign):
    re, im = pair
    step = step % length
    if step == 0:
        return pair
    if 4 * step == length:
        return (-im, re) if sign > 0 else (im, -re)
    if 8 * step == length:
        return ((re - sign * im) * HALF, (im + sign * re) * HALF)
    if 8 * step == 3 * length:
        return ((-re - sign * im) * HALF, (-im + sign * re) * HALF)
    cos = math.cos(2.0 * math.pi * step / length)
    sin = sign * math.sin(2.0 * math.pi * step / length)
    return (re * cos - im * sin, im * cos + re * sin)


def short_transform(values, sign):
    count = len(values)
    if count == 1:
        return values
    even = short_transform(values[0::2], sign)
    odd = short_transform(values[1::2], sign)
    low, high = [], []
    for k in range(count // 2):
        re, im = turn(odd[k], k, count, sign)
        low.append((even[k][0] + re, even[k][1] + im))
        high.append((even[k][0] - re, even[k][1] - im))
    return low + high


def real_eight(u):
    a = [u[k] + u[k + 4] for k in range(4)]
    b = [u[k] - u[k + 4] for k in range(4)]
    even, odd = a[0] + a[2], a[1] + a[3]
    minus, plus = (b[1] - b[3]) * HALF, (b[1] + b[3]) * HALF
    return (
        even + odd,
        even - odd,
        (b[0] + minus, -(b[2] + plus)),
        (a[0] - a[2], a[3] - a[1]),
        (b[0] - minus, b[2] - plus),
    )


def real_eight_back(zero, four, one, two, three):
    plus, minus = zero + four, zero - four
    (r1, i1), (r2, i2), (r3, i3) = one, two, three
    p0, p1 = plus + r2, plus - r2
    m0, m1 = minus - i2, minus + i2
    e0, e1 = r1 + r3, i3 - i1
    o0 = (r1 - i1 - r3 - i3) * HALF
    o1 = (r3 - i3 - r1 - i1) * HALF
    return [p0 + e0, m0 + o0, p1 + e1, m1 + o1, p0 - e0, m0 - o0, p1 - e1, m1 - o1]


def spread(tiles, lane):
    for bit in (8, 4, 2, 1):
        high = (lane // 8) % (2 * bit) >= bit
        new = list(tiles)
        for t in range(16):
            if t & bit:
                continue
            first, second = tiles[t], tiles[t | bit]
            new[t] = jnp.where(high, pltpu.roll(second, 8 * bit, 1), first)
            new[t | bit] = jnp.where(high, second, pltpu.roll(first, 128 - 8 * bit, 1))
        tiles = new
    return tiles


def kernel(
    part_hbm, wedge_hbm, levels, ft_hbm, it_hbm, xt_hbm, tw_hbm, pick_hbm, lane_hbm,
    out,
    part, wedge, ft, it, xt, tw, pick, lanet,
    relay, side, final, cross,
    folded0, folded1, send, held, xr, xi, level1, level2, own_ids, mir_ids, spec_ids, mir_in, spec_in, back, got, mid,
    load_sem, table_sem, relay_s, relay_r, side_s, side_r, final_s, final_r, cross_s, cross_r,
    first_s, first_r, second_s, second_r, wedge_s, wedge_r,
):
    shot = lax.axis_index("shot")
    lat = lax.axis_index("lat")
    n_shot = lax.axis_size("shot")
    y, xh = shot // 2, shot % 2
    up, down = (shot + 2) % n_shot, (shot + n_shot - 2) % n_shot
    y_up, y_down, y_far = (y + 1) % 4, (y + 3) % 4, (y + 2) % 4
    flip = lat + 2 - 4 * ((lat // 2) % 2)
    other = shot + 1 - 2 * xh

    def rows(c):
        return pl.ds(c * CROWS, CROWS)

    loads = [
        pltpu.make_async_copy(
            part_hbm.at[:, :, rows(c), :], part.at[:, :, rows(c), :], load_sem.at[c]
        )
        for c in range(CHUNKS)
    ]
    loads[0].start()
    tables = [
        pltpu.make_async_copy(src, dst, table_sem.at[k])
        for k, (src, dst) in enumerate(
            [(wedge_hbm, wedge), (pick_hbm, pick), (lane_hbm, lanet), (ft_hbm, ft),
             (xt_hbm, xt), (tw_hbm, tw), (it_hbm, it)]
        )
    ]
    for c in range(1, CHUNKS):
        loads[c].start()
    for copy in tables:
        copy.start()

    barrier = pltpu.get_barrier_semaphore()

    def greet(s, l):
        pl.semaphore_signal(barrier, inc=1, device_id=(s, l), device_id_type=MESH)

    @pl.loop(1, LAT)
    def _(k):
        greet(shot, (lat + k) % LAT)

    greet(up, lat)
    greet(down, lat)
    greet(other, flip)
    pl.semaphore_wait(barrier, LAT - 1 + 3)

    def copy_to(src, dst, s_sem, r_sem, s, l):
        return pltpu.make_async_remote_copy(
            src_ref=src, dst_ref=dst, send_sem=s_sem, recv_sem=r_sem, device_id=(s, l), device_id_type=MESH
        )

    def slab(q, c):
        return part.at[0, q, rows(c), :]

    def relay_copy(c, k):
        q = 2 * y_far + k
        return copy_to(
            slab(q, c), relay.at[c, k], relay_s.at[c, k], relay_r.at[c, k], up if k == 0 else down, lat
        )

    def side_copy(c, k):
        q = 2 * y_up + 1 if k == 0 else 2 * y_down
        return copy_to(
            slab(q, c), side.at[c, k], side_s.at[c, k], side_r.at[c, k], up if k == 0 else down, lat
        )

    def final_copy(c, k):
        q = 2 * y_up if k == 0 else 2 * y_down + 1
        return copy_to(
            slab(q, c), final.at[c, k], final_s.at[c, k], final_r.at[c, k], up if k == 0 else down, lat
        )

    def cross_copy(c, h):
        return copy_to(
            slab(2 * y + h, c), cross.at[c, xh], cross_s.at[c, h], cross_r.at[c, xh], 2 * y + h, flip
        )

    def pair(q, c):
        return part[0, q, rows(c), :].astype(F32) + part[1, q, rows(c), :].astype(F32)

    def begin(c):
        loads[c].wait()
        for k in range(2):
            q = 2 * y_far + k
            part[0, q, rows(c), :] = pair(q, c).astype(BF16)
            relay_copy(c, k).start()
        for k in range(2):
            q = 2 * y_up + 1 if k == 0 else 2 * y_down
            part[0, q, rows(c), :] = pair(q, c).astype(BF16)
            side_copy(c, k).start()

    def forward(c):
        for k in range(2):
            q = 2 * y_up if k == 0 else 2 * y_down + 1
            relay_copy(c, k).wait_recv()
            part[0, q, rows(c), :] = (pair(q, c) + relay[c, k].astype(F32)).astype(BF16)
            final_copy(c, k).start()

    def across(c):
        for k in range(2):
            side_copy(c, k).wait_recv()
            final_copy(c, k).wait_recv()
        for h in range(2):
            q = 2 * y + h
            total = pair(q, c) + final[c, h].astype(F32) + side[c, 1 - h].astype(F32)
            part[0, q, rows(c), :] = total.astype(BF16)
            cross_copy(c, h).start()

    def fold(c):
        for h in range(2):
            pltpu.make_async_copy(cross.at[c, h], cross.at[c, h], cross_r.at[c, h]).wait()
        top, low = pl.ds(c * CROWS, CROWS), pl.ds(ROWS + c * CROWS, CROWS)
        u = []
        for k in range(8):
            cols = pl.ds(256 * k, 256)
            u.append(cross[c, 0, :, cols].astype(F32) + cross[c, 1, :, cols].astype(F32))
        zero, four, one, two, three = real_eight(u)
        zero, four = zero.astype(BF16), four.astype(BF16)
        blank = jnp.zeros((CROWS, 512), BF16)
        folded0[top, 0:256] = zero
        folded0[top, 256:512] = four
        folded0[top, 512:1024] = blank
        folded0[low, 0:512] = blank
        folded0[low, 512:768] = zero
        folded0[low, 768:1024] = four
        for s, (re, im) in enumerate((one, two, three)):
            re, im, neg = re.astype(BF16), im.astype(BF16), (-im).astype(BF16)
            folded1[s, top, 0:256] = re
            folded1[s, top, 256:512] = neg
            folded1[s, low, 0:256] = im
            folded1[s, low, 256:512] = re

    lane = lax.broadcasted_iota(jnp.int32, (1, 128), 1)
    seventh = lax.broadcasted_iota(jnp.int32, (8, 128), 0) == 7

    partner = LAT - 1 - lat
    corner = jnp.where(lat == 0, 16, LAT - lat)

    def mirror_copy():
        return copy_to(
            mir_ids.at[:, pl.ds(0, 32), :], mir_in, wedge_s.at[0], wedge_r.at[0], shot, partner
        )

    def corner_copy(k):
        src = (own_ids if k == 0 else mir_ids).at[:, pl.ds(32, 16), :]
        return copy_to(src, spec_in.at[k], wedge_s.at[1 + k], wedge_r.at[1 + k], shot, corner)

    def wedges_out():
        for k in range(3):
            tables[k].wait()
        ids = wedge[...].astype(F32).astype(BF16)
        chosen = jnp.dot(pick[...], ids, preferred_element_type=F32).astype(BF16)
        own, mir = chosen[:48], chosen[48:]
        tall = jnp.concatenate([own[:, 128 * t : 128 * t + 128] for t in range(16)], axis=0)
        moved = jnp.dot(tall, lanet[0:128, :], preferred_element_type=F32)
        for t, tile in enumerate(spread([moved[48 * t : 48 * t + 48] for t in range(16)], lane)):
            own_ids[t] = tile.astype(BF16)
        tall = jnp.concatenate(
            [
                jnp.concatenate(
                    [mir[:, 128 * (15 - t) : 128 * (16 - t)],
                     mir[:, 128 * ((16 - t) % 16) : 128 * ((16 - t) % 16) + 128]],
                    axis=1,
                )
                for t in range(16)
            ],
            axis=0,
        )
        moved = jnp.dot(tall, lanet[128:384, :], preferred_element_type=F32)
        for t, tile in enumerate(spread([moved[48 * t : 48 * t + 48] for t in range(16)], lane)):
            mir_ids[t] = tile.astype(BF16)
        mirror_copy().start()

        @pl.when(lat < 16)
        def _():
            for k in range(2):
                corner_copy(k).start()

    def look_up(ids):
        found = jnp.full(ids.shape, levels[0], F32)
        for w in range(1, 16):
            found = jnp.where(ids == float(w), levels[w], found)
        return found

    def wedges_in():
        mirror_copy().wait_recv()

        @pl.when(lat >= 16)
        def _():
            for k in range(2):
                corner_copy(k).wait_recv()

        @pl.loop(0, 16)
        def _(kk):
            own = own_ids[kk].astype(F32)
            mir = mir_ids[kk].astype(F32)
            got_mir = mir_in[kk].astype(F32)
            spec_own = spec_in[0, kk].astype(F32)
            spec_mir = spec_in[1, kk].astype(F32)
            level1[kk, 0:8, :] = look_up(jnp.where(seventh & (lat >= 16), own[32:40], own[0:8]))
            level1[kk, 8:32, :] = look_up(own[8:32])
            level1[kk, 32:40, :] = look_up(spec_own[0:8])
            row = jnp.where(lat == 16, mir[32:40], spec_mir[0:8])
            level2[kk, 0:8, :] = look_up(jnp.where(seventh & (lat >= 16), row, got_mir[0:8]))
            level2[kk, 8:32, :] = look_up(got_mir[8:32])
            level2[kk, 32:40, :] = look_up(spec_mir[0:8])

    begin(0)
    begin(1)
    forward(0)
    wedges_out()
    begin(2)
    forward(1)
    across(0)
    begin(3)
    forward(2)
    across(1)
    fold(0)
    forward(3)
    across(2)
    fold(1)
    wedges_in()
    across(3)
    fold(2)
    for k in range(3, 7):
        tables[k].wait()
    fold(3)

    pieces = [
        lax.dot_general(ft[:, 0:1024], folded0[...], NT, preferred_element_type=F32).reshape(LAT, 8, 128)
    ]
    for s in range(3):
        pieces.append(
            lax.dot_general(
                ft[:, 1024 + 512 * s : 1536 + 512 * s], folded1[s], NT, preferred_element_type=F32
            ).reshape(LAT, 8, 128)
        )
    for k in range(2):
        both = jnp.concatenate([pieces[2 * k], pieces[2 * k + 1]], axis=1)
        send[:, 16 * k : 16 * k + 16, :] = both.astype(BF16)

    def first_copy(dest):
        return copy_to(send.at[dest], held.at[flip], first_s, first_r, shot, dest)

    @pl.loop(1, LAT)
    def _(k):
        first_copy((lat + k) % LAT).start()

    held[flip] = send[lat]
    all_but_one = held.at[pl.ds(0, LAT - 1)]
    pltpu.make_async_copy(all_but_one, all_but_one, first_r).wait()

    low = lane < 64
    packed = seventh & (lat == 16)
    nothing = jnp.zeros((8, 128), F32)
    for p in range(16):
        u0, u1 = held[2 * p].astype(F32), held[2 * p + 1].astype(F32)
        re = jnp.where(low, u0, pltpu.roll(u1, 64, 1))
        im = jnp.where(low, pltpu.roll(u0, 64, 1), u1)
        xr[p, 0:32, :] = re
        xi[p, 0:8, :] = jnp.where(packed, 0.0, im[0:8])
        xi[p, 8:32, :] = im[8:32]
        xr[p, 32:40, :] = im[0:8]
        xi[p, 32:40, :] = nothing

    def lateral(sign):
        base = 0 if sign < 0 else 2

        @pl.loop(0, 5)
        def _(g):
            at = pl.ds(pl.multiple_of(8 * g, 8), 8)
            values = []
            for p in range(16):
                value = (xr[p, at, :], xi[p, at, :])
                if sign > 0:
                    cos, sin = tw[base, p : p + 1, :], tw[base + 1, p : p + 1, :]
                    value = (value[0] * cos - value[1] * sin, value[1] * cos + value[0] * sin)
                values.append(value)
            for p, value in enumerate(short_transform(values, sign)):
                if sign < 0:
                    cos, sin = tw[base, p : p + 1, :], tw[base + 1, p : p + 1, :]
                    value = (value[0] * cos - value[1] * sin, value[1] * cos + value[0] * sin)
                xr[p, at, :] = value[0]
                xi[p, at, :] = value[1]

    lateral(-1)
    for b in range(4):
        some = pl.ds(4 * b, 4)
        both = jnp.concatenate([xr[some].reshape(160, 128), xi[some].reshape(160, 128)], axis=1)
        spectrum = jnp.dot(both.astype(BF16), xt[0:256, :], preferred_element_type=F32)
        re, im = spectrum[:, :128], spectrum[:, 128:]
        inverse = lax.rsqrt(jnp.maximum(re * re + im * im, 1e-30))
        factor = jnp.maximum(1.0 - level1[some].reshape(160, 128) * inverse, 0.0)
        factor += jnp.maximum(1.0 - level2[some].reshape(160, 128) * inverse, 0.0)
        both = jnp.concatenate([re * factor, im * factor], axis=1)
        inner = jnp.dot(both.astype(BF16), xt[256:512, :], preferred_element_type=F32)
        xr[some] = inner[:, :128].reshape(4, 40, 128)
        xi[some] = inner[:, 128:].reshape(4, 40, 128)
    lateral(1)

    for p in range(16):
        re, im = xr[p, 0:32, :], xi[p, 0:32, :]
        im = jnp.concatenate([jnp.where(packed, xr[p, 32:40, :], im[0:8]), im[8:32]], axis=0)
        back[2 * p] = jnp.where(low, re, pltpu.roll(im, 64, 1)).astype(BF16)
        back[2 * p + 1] = jnp.where(low, pltpu.roll(re, 64, 1), im).astype(BF16)

    def second_copy(dest):
        return copy_to(back.at[dest], got.at[lat], second_s, second_r, shot, dest)

    @pl.loop(1, LAT)
    def _(k):
        second_copy((lat + k) % LAT).start()

    got[lat] = back[lat]
    all_but_one = got.at[pl.ds(0, LAT - 1)]
    pltpu.make_async_copy(all_but_one, all_but_one, second_r).wait()

    for s in range(4):
        tall = got[:, 16 * (s // 2) : 16 * (s // 2) + 16, :].astype(F32)
        flat = tall[:, 8 * (s % 2) : 8 * (s % 2) + 8, :].reshape(256, 128).T.astype(BF16)
        wide = jnp.concatenate([flat[:64], flat[64:]], axis=1)
        mid[s] = jnp.dot(wide, it[512 * s : 512 * s + 512, :], preferred_element_type=F32)

    @pl.loop(0, 8)
    def _(g):
        at = pl.ds(pl.multiple_of(8 * g, 8), 8)
        parts = [(mid[s, at, 0:256], mid[s, at, 256:512]) for s in range(4)]
        values = real_eight_back(parts[0][0], parts[0][1], parts[1], parts[2], parts[3])
        for k in range(8):
            out[0, at, 256 * k : 256 * k + 256] = values[k]

    for c in range(CHUNKS):
        for k in range(2):
            relay_copy(c, k).wait_send()
            side_copy(c, k).wait_send()
            final_copy(c, k).wait_send()
            cross_copy(c, k).wait_send()
    sent = send.at[pl.ds(0, LAT - 1)]
    pltpu.make_async_copy(sent, sent, first_s).wait()
    sent = back.at[pl.ds(0, LAT - 1)]
    pltpu.make_async_copy(sent, sent, second_s).wait()
    mirror_copy().wait_send()

    @pl.when(lat < 16)
    def _():
        for k in range(2):
            corner_copy(k).wait_send()


def on_device(partials, wedges, levels):
    tables = [
        jnp.asarray(t)
        for t in (
            forward_tables(), inverse_tables(), lateral_tables(), turn_tables(), pick_tables(), lane_tables()
        )
    ]
    anywhere = pl.BlockSpec(memory_space=pl.ANY)
    vmem, dma = pltpu.VMEM, pltpu.SemaphoreType.DMA
    two = dma((CHUNKS, 2))
    return pl.pallas_call(
        kernel,
        out_shape=jax.ShapeDtypeStruct((1, ROWS, N), F32),
        in_specs=[anywhere, anywhere, pl.BlockSpec(memory_space=pltpu.SMEM)] + [anywhere] * 6,
        out_specs=pl.BlockSpec(memory_space=pltpu.VMEM),
        scratch_shapes=[
            vmem(partials.shape, BF16),
            vmem(wedges.shape, jnp.int32),
            *[vmem(t.shape, t.dtype) for t in tables],
            vmem((CHUNKS, 2, CROWS, N), BF16),
            vmem((CHUNKS, 2, CROWS, N), BF16),
            vmem((CHUNKS, 2, CROWS, N), BF16),
            vmem((CHUNKS, 2, CROWS, N), BF16),
            vmem((128, 1024), BF16),
            vmem((3, 128, 512), BF16),
            vmem((LAT, 32, 128), BF16),
            vmem((LAT, 32, 128), BF16),
            vmem((16, 40, 128), F32),
            vmem((16, 40, 128), F32),
            vmem((16, 40, 128), F32),
            vmem((16, 40, 128), F32),
            vmem((16, 48, 128), BF16),
            vmem((16, 48, 128), BF16),
            vmem((16, 16, 128), BF16),
            vmem((16, 32, 128), BF16),
            vmem((2, 16, 16, 128), BF16),
            vmem((LAT, 32, 128), BF16),
            vmem((LAT, 32, 128), BF16),
            vmem((4, ROWS, 512), F32),
            dma((CHUNKS,)),
            dma((7,)),
            two, two, two, two, two, two, two, two,
            dma, dma, dma, dma,
            dma((3,)),
            dma((3,)),
        ],
        compiler_params=pltpu.CompilerParams(
            collective_id=0, has_side_effects=True, vmem_limit_bytes=40 * 1024 * 1024
        ),
        name="stack_threshold",
    )(partials, wedges, levels, *tables)


def solution(mesh):
    in_specs = (P("shot", None, "lat", None), P("lat", None), P())
    return jax.shard_map(
        on_device, mesh=mesh, in_specs=in_specs, out_specs=P("shot", "lat", None), check_vma=False
    )
```

```python
import functools
import math

import jax
import jax.numpy as jnp
import ml_dtypes
import numpy as np
from jax import lax
from jax.experimental import pallas as pl
from jax.experimental.pallas import tpu as pltpu
from jax.sharding import PartitionSpec as P

MESH = pl.DeviceIdType.MESH
F32 = jnp.float32
BF16 = jnp.bfloat16
N = 2048
LAT = 32
ROWS = N // LAT
CHUNKS = 4
CROWS = ROWS // CHUNKS
HALF = math.sqrt(0.5)
NT = (((1,), (1,)), ((), ()))


def owned():
    ky = np.zeros((LAT, 32), np.int64)
    for d in range(LAT):
        for i in range(8):
            for s in (1, 2, 3):
                ky[d, 8 * s + i] = 64 * d + 8 * i + s
        for i in range(4):
            ky[d, i] = 64 * d + 8 * i + 4
        for i in range(4, 7):
            ky[d, i] = 64 * d + 8 * (i - 3)
        ky[d, 7] = 64 * d + (32 if d < 16 else 0)
    return ky


def forward_tables():
    ky = owned()
    y2 = np.arange(256)
    scale = 1.0 / math.sqrt(N)
    parts = []
    for s in range(4):
        rows = ky[:, 8 * s : 8 * s + 8].reshape(-1)
        angle = 2.0 * np.pi * ((rows[:, None] * y2[None, :]) % N) / N
        re, im = np.cos(angle), -np.sin(angle)
        if s == 0:
            packed = 16 * 8 + 7
            re[packed] = np.where(y2 % 2, -1.0, 1.0)
            im[packed] = 1.0
            four = (rows % 8 == 4)[:, None]
            zero = np.zeros_like(re)
            parts += [
                np.where(four, zero, re),
                np.where(four, re, zero),
                np.where(four, zero, im),
                np.where(four, im, zero),
            ]
        else:
            parts += [re, im]
    return (np.concatenate(parts, axis=1) * scale).astype(ml_dtypes.bfloat16)


def inverse_tables():
    ky = owned()
    y2 = np.arange(256)
    scale = 1.0 / math.sqrt(N)
    parts = []
    for s in range(4):
        rows = ky[:, 8 * s : 8 * s + 8].reshape(-1)
        angle = 2.0 * np.pi * ((rows[:, None] * y2[None, :]) % N) / N
        cos, sin = 2.0 * np.cos(angle), 2.0 * np.sin(angle)
        if s == 0:
            packed = 16 * 8 + 7
            cos[packed] = np.where(y2 % 2, -1.0, 1.0)
            sin[packed] = -1.0
            four = (rows % 8 == 4)[:, None]
            zero = np.zeros_like(cos)
            top = np.concatenate([np.where(four, zero, cos), np.where(four, cos, zero)], axis=1)
            low = np.concatenate([np.where(four, zero, -sin), np.where(four, -sin, zero)], axis=1)
        else:
            top = np.concatenate([cos, sin], axis=1)
            low = np.concatenate([-sin, cos], axis=1)
        parts += [top, low]
    return (np.concatenate(parts, axis=0) * scale).astype(ml_dtypes.bfloat16)


def lateral_tables():
    index = np.arange(128)
    angle = 2.0 * np.pi * ((index[:, None] * index[None, :]) % 128) / 128
    cos, sin = np.cos(angle), np.sin(angle)
    forward = np.block([[cos, -sin], [sin, cos]])
    inverse = np.block([[cos, sin], [-sin, cos]])
    return np.concatenate([forward, inverse], axis=0).astype(ml_dtypes.bfloat16)


def turn_tables():
    angle = 2.0 * np.pi * (np.arange(16)[:, None] * np.arange(128)[None, :]) / N
    scale = 1.0 / math.sqrt(N)
    cos, sin = np.cos(angle) * scale, np.sin(angle) * scale
    return np.stack([cos, -sin, 0.5 * cos, 0.5 * sin]).astype(np.float32)


def pick_tables():
    own = np.zeros((48, 64))
    mirror = np.zeros((48, 64))
    for i in range(8):
        for s in (1, 2, 3):
            own[8 * s + i, 8 * i + s] = 1
            mirror[8 * s + i, 8 * (7 - i) + 8 - s] = 1
    for i in range(4):
        own[i, 8 * i + 4] = 1
        mirror[i, 8 * (7 - i) + 4] = 1
    for i in range(4, 7):
        own[i, 8 * (i - 3)] = 1
        mirror[i, 8 * (11 - i)] = 1
    own[7, 32] = mirror[7, 32] = 1
    own[39, 0] = mirror[39, 0] = 1
    return np.concatenate([own, mirror], axis=0).astype(ml_dtypes.bfloat16)


def lane_tables():
    lanes = np.arange(128)
    place = (lanes % 16) * 8 + lanes // 16
    own = np.zeros((128, 128))
    own[lanes, place] = 1
    mirror = np.zeros((256, 128))
    mirror[128 - lanes, place] = 1
    return np.concatenate([own, mirror], axis=0).astype(ml_dtypes.bfloat16)


def turn(pair, step, length, sign):
    re, im = pair
    step = step % length
    if step == 0:
        return pair
    if 4 * step == length:
        return (-im, re) if sign > 0 else (im, -re)
    if 8 * step == length:
        return ((re - sign * im) * HALF, (im + sign * re) * HALF)
    if 8 * step == 3 * length:
        return ((-re - sign * im) * HALF, (-im + sign * re) * HALF)
    cos = math.cos(2.0 * math.pi * step / length)
    sin = sign * math.sin(2.0 * math.pi * step / length)
    return (re * cos - im * sin, im * cos + re * sin)


def short_transform(values, sign):
    count = len(values)
    if count == 1:
        return values
    even = short_transform(values[0::2], sign)
    odd = short_transform(values[1::2], sign)
    low, high = [], []
    for k in range(count // 2):
        re, im = turn(odd[k], k, count, sign)
        low.append((even[k][0] + re, even[k][1] + im))
        high.append((even[k][0] - re, even[k][1] - im))
    return low + high


def real_eight(u):
    a = [u[k] + u[k + 4] for k in range(4)]
    b = [u[k] - u[k + 4] for k in range(4)]
    even, odd = a[0] + a[2], a[1] + a[3]
    minus, plus = (b[1] - b[3]) * HALF, (b[1] + b[3]) * HALF
    return (
        even + odd,
        even - odd,
        (b[0] + minus, -(b[2] + plus)),
        (a[0] - a[2], a[3] - a[1]),
        (b[0] - minus, b[2] - plus),
    )


def real_eight_back(zero, four, one, two, three):
    plus, minus = zero + four, zero - four
    (r1, i1), (r2, i2), (r3, i3) = one, two, three
    p0, p1 = plus + r2, plus - r2
    m0, m1 = minus - i2, minus + i2
    e0, e1 = r1 + r3, i3 - i1
    o0 = (r1 - i1 - r3 - i3) * HALF
    o1 = (r3 - i3 - r1 - i1) * HALF
    return [p0 + e0, m0 + o0, p1 + e1, m1 + o1, p0 - e0, m0 - o0, p1 - e1, m1 - o1]


def spread(tiles, lane):
    for bit in (8, 4, 2, 1):
        high = (lane // 8) % (2 * bit) >= bit
        new = list(tiles)
        for t in range(16):
            if t & bit:
                continue
            first, second = tiles[t], tiles[t | bit]
            new[t] = jnp.where(high, pltpu.roll(second, 8 * bit, 1), first)
            new[t | bit] = jnp.where(high, second, pltpu.roll(first, 128 - 8 * bit, 1))
        tiles = new
    return tiles


def kernel(
    part_hbm, wedge_hbm, levels, ft_hbm, it_hbm, xt_hbm, tw_hbm, pick_hbm, lane_hbm,
    out,
    part, wedge, ft, it, xt, tw, pick, lanet,
    relay, side, final, cross,
    folded0, folded1, send, held, xr, xi, level1, level2, own_ids, mir_ids, mir_in, spec_in, back, got, mid,
    load_sem, table_sem, relay_s, relay_r, side_s, side_r, final_s, final_r, cross_s, cross_r,
    first_s, first_r, second_s, second_r, wedge_s, wedge_r,
):
    shot = lax.axis_index("shot")
    lat = lax.axis_index("lat")
    n_shot = lax.axis_size("shot")
    y, xh = shot // 2, shot % 2
    up, down = (shot + 2) % n_shot, (shot + n_shot - 2) % n_shot
    y_up, y_down, y_far = (y + 1) % 4, (y + 3) % 4, (y + 2) % 4
    flip = lat + 2 - 4 * ((lat // 2) % 2)
    other = shot + 1 - 2 * xh

    def rows(c):
        return pl.ds(c * CROWS, CROWS)

    loads = [
        pltpu.make_async_copy(
            part_hbm.at[:, :, rows(c), :], part.at[:, :, rows(c), :], load_sem.at[c]
        )
        for c in range(CHUNKS)
    ]
    loads[0].start()
    tables = [
        pltpu.make_async_copy(src, dst, table_sem.at[k])
        for k, (src, dst) in enumerate(
            [(wedge_hbm, wedge), (pick_hbm, pick), (lane_hbm, lanet), (ft_hbm, ft),
             (xt_hbm, xt), (tw_hbm, tw), (it_hbm, it)]
        )
    ]
    for c in range(1, CHUNKS):
        loads[c].start()
    for copy in tables:
        copy.start()

    barrier = pltpu.get_barrier_semaphore()

    def greet(s, l):
        pl.semaphore_signal(barrier, inc=1, device_id=(s, l), device_id_type=MESH)

    @pl.loop(1, LAT)
    def _(k):
        greet(shot, (lat + k) % LAT)

    greet(up, lat)
    greet(down, lat)
    greet(other, flip)
    pl.semaphore_wait(barrier, LAT - 1 + 3)

    def copy_to(src, dst, s_sem, r_sem, s, l):
        return pltpu.make_async_remote_copy(
            src_ref=src, dst_ref=dst, send_sem=s_sem, recv_sem=r_sem, device_id=(s, l), device_id_type=MESH
        )

    def slab(q, c):
        return part.at[0, q, rows(c), :]

    def relay_copy(c, k):
        q = 2 * y_far + k
        return copy_to(
            slab(q, c), relay.at[c, k], relay_s.at[c, k], relay_r.at[c, k], up if k == 0 else down, lat
        )

    def side_copy(c, k):
        q = 2 * y_up + 1 if k == 0 else 2 * y_down
        return copy_to(
            slab(q, c), side.at[c, k], side_s.at[c, k], side_r.at[c, k], up if k == 0 else down, lat
        )

    def final_copy(c, k):
        q = 2 * y_up if k == 0 else 2 * y_down + 1
        return copy_to(
            slab(q, c), final.at[c, k], final_s.at[c, k], final_r.at[c, k], up if k == 0 else down, lat
        )

    def cross_copy(c, h):
        return copy_to(
            slab(2 * y + h, c), cross.at[c, xh], cross_s.at[c, h], cross_r.at[c, xh], 2 * y + h, flip
        )

    def pair(q, c):
        return part[0, q, rows(c), :].astype(F32) + part[1, q, rows(c), :].astype(F32)

    def begin(c):
        loads[c].wait()
        for k in range(2):
            q = 2 * y_far + k
            part[0, q, rows(c), :] = pair(q, c).astype(BF16)
            relay_copy(c, k).start()
        for k in range(2):
            q = 2 * y_up + 1 if k == 0 else 2 * y_down
            part[0, q, rows(c), :] = pair(q, c).astype(BF16)
            side_copy(c, k).start()

    def forward(c):
        for k in range(2):
            q = 2 * y_up if k == 0 else 2 * y_down + 1
            relay_copy(c, k).wait_recv()
            part[0, q, rows(c), :] = (pair(q, c) + relay[c, k].astype(F32)).astype(BF16)
            final_copy(c, k).start()

    def across(c):
        for k in range(2):
            side_copy(c, k).wait_recv()
            final_copy(c, k).wait_recv()
        for h in range(2):
            q = 2 * y + h
            total = pair(q, c) + final[c, h].astype(F32) + side[c, 1 - h].astype(F32)
            part[0, q, rows(c), :] = total.astype(BF16)
            cross_copy(c, h).start()

    def fold(c):
        for h in range(2):
            pltpu.make_async_copy(cross.at[c, h], cross.at[c, h], cross_r.at[c, h]).wait()
        top, low = pl.ds(c * CROWS, CROWS), pl.ds(ROWS + c * CROWS, CROWS)
        u = []
        for k in range(8):
            cols = pl.ds(256 * k, 256)
            u.append(cross[c, 0, :, cols].astype(F32) + cross[c, 1, :, cols].astype(F32))
        zero, four, one, two, three = real_eight(u)
        zero, four = zero.astype(BF16), four.astype(BF16)
        blank = jnp.zeros((CROWS, 512), BF16)
        folded0[top, 0:256] = zero
        folded0[top, 256:512] = four
        folded0[top, 512:1024] = blank
        folded0[low, 0:512] = blank
        folded0[low, 512:768] = zero
        folded0[low, 768:1024] = four
        for s, (re, im) in enumerate((one, two, three)):
            re, im, neg = re.astype(BF16), im.astype(BF16), (-im).astype(BF16)
            folded1[s, top, 0:256] = re
            folded1[s, top, 256:512] = neg
            folded1[s, low, 0:256] = im
            folded1[s, low, 256:512] = re

    lane = lax.broadcasted_iota(jnp.int32, (1, 128), 1)
    seventh = lax.broadcasted_iota(jnp.int32, (8, 128), 0) == 7

    partner = LAT - 1 - lat
    corner = jnp.where(lat == 0, 16, LAT - lat)

    def mirror_copy():
        return copy_to(
            mir_ids.at[:, pl.ds(0, 32), :], mir_in, wedge_s.at[0], wedge_r.at[0], shot, partner
        )

    def corner_copy(k):
        src = (own_ids if k == 0 else mir_ids).at[:, pl.ds(32, 16), :]
        return copy_to(src, spec_in.at[k], wedge_s.at[1 + k], wedge_r.at[1 + k], shot, corner)

    def wedges_out():
        for k in range(3):
            tables[k].wait()
        ids = wedge[...].astype(F32).astype(BF16)
        chosen = jnp.dot(pick[...], ids, preferred_element_type=F32).astype(BF16)
        own, mir = chosen[:48], chosen[48:]
        tall = jnp.concatenate([own[:, 128 * t : 128 * t + 128] for t in range(16)], axis=0)
        moved = jnp.dot(tall, lanet[0:128, :], preferred_element_type=F32)
        for t, tile in enumerate(spread([moved[48 * t : 48 * t + 48] for t in range(16)], lane)):
            own_ids[t] = tile.astype(BF16)
        tall = jnp.concatenate(
            [
                jnp.concatenate(
                    [mir[:, 128 * (15 - t) : 128 * (16 - t)],
                     mir[:, 128 * ((16 - t) % 16) : 128 * ((16 - t) % 16) + 128]],
                    axis=1,
                )
                for t in range(16)
            ],
            axis=0,
        )
        moved = jnp.dot(tall, lanet[128:384, :], preferred_element_type=F32)
        for t, tile in enumerate(spread([moved[48 * t : 48 * t + 48] for t in range(16)], lane)):
            mir_ids[t] = tile.astype(BF16)
        mirror_copy().start()

        @pl.when(lat < 16)
        def _():
            for k in range(2):
                corner_copy(k).start()

    def look_up(ids):
        found = jnp.full(ids.shape, levels[0], F32)
        for w in range(1, 16):
            found = jnp.where(ids == float(w), levels[w], found)
        return found

    def wedges_in():
        mirror_copy().wait_recv()

        @pl.when(lat >= 16)
        def _():
            for k in range(2):
                corner_copy(k).wait_recv()

        @pl.loop(0, 16)
        def _(kk):
            own = own_ids[kk].astype(F32)
            mir = mir_ids[kk].astype(F32)
            got_mir = mir_in[kk].astype(F32)
            spec_own = spec_in[0, kk].astype(F32)
            spec_mir = spec_in[1, kk].astype(F32)
            level1[kk, 0:8, :] = look_up(jnp.where(seventh & (lat >= 16), own[32:40], own[0:8]))
            level1[kk, 8:32, :] = look_up(own[8:32])
            level1[kk, 32:40, :] = look_up(spec_own[0:8])
            row = jnp.where(lat == 16, mir[32:40], spec_mir[0:8])
            level2[kk, 0:8, :] = look_up(jnp.where(seventh & (lat >= 16), row, got_mir[0:8]))
            level2[kk, 8:32, :] = look_up(got_mir[8:32])
            level2[kk, 32:40, :] = look_up(spec_mir[0:8])

    begin(0)
    begin(1)
    forward(0)
    wedges_out()
    begin(2)
    forward(1)
    across(0)
    begin(3)
    forward(2)
    across(1)
    fold(0)
    forward(3)
    across(2)
    fold(1)
    wedges_in()
    across(3)
    fold(2)
    for k in range(3, 7):
        tables[k].wait()
    fold(3)

    pieces = [
        lax.dot_general(ft[:, 0:1024], folded0[...], NT, preferred_element_type=F32).reshape(LAT, 8, 128)
    ]
    for s in range(3):
        pieces.append(
            lax.dot_general(
                ft[:, 1024 + 512 * s : 1536 + 512 * s], folded1[s], NT, preferred_element_type=F32
            ).reshape(LAT, 8, 128)
        )
    for k in range(2):
        both = jnp.concatenate([pieces[2 * k], pieces[2 * k + 1]], axis=1)
        send[:, 16 * k : 16 * k + 16, :] = both.astype(BF16)

    def first_copy(dest):
        return copy_to(send.at[dest], held.at[flip], first_s, first_r, shot, dest)

    @pl.loop(1, LAT)
    def _(k):
        first_copy((lat + k) % LAT).start()

    held[flip] = send[lat]
    all_but_one = held.at[pl.ds(0, LAT - 1)]
    pltpu.make_async_copy(all_but_one, all_but_one, first_r).wait()

    low = lane < 64
    packed = seventh & (lat == 16)
    nothing = jnp.zeros((8, 128), F32)
    for p in range(16):
        u0, u1 = held[2 * p].astype(F32), held[2 * p + 1].astype(F32)
        re = jnp.where(low, u0, pltpu.roll(u1, 64, 1))
        im = jnp.where(low, pltpu.roll(u0, 64, 1), u1)
        xr[p, 0:32, :] = re
        xi[p, 0:8, :] = jnp.where(packed, 0.0, im[0:8])
        xi[p, 8:32, :] = im[8:32]
        xr[p, 32:40, :] = im[0:8]
        xi[p, 32:40, :] = nothing

    def lateral(sign):
        base = 0 if sign < 0 else 2

        @pl.loop(0, 5)
        def _(g):
            at = pl.ds(pl.multiple_of(8 * g, 8), 8)
            values = []
            for p in range(16):
                value = (xr[p, at, :], xi[p, at, :])
                if sign > 0:
                    cos, sin = tw[base, p : p + 1, :], tw[base + 1, p : p + 1, :]
                    value = (value[0] * cos - value[1] * sin, value[1] * cos + value[0] * sin)
                values.append(value)
            for p, value in enumerate(short_transform(values, sign)):
                if sign < 0:
                    cos, sin = tw[base, p : p + 1, :], tw[base + 1, p : p + 1, :]
                    value = (value[0] * cos - value[1] * sin, value[1] * cos + value[0] * sin)
                xr[p, at, :] = value[0]
                xi[p, at, :] = value[1]

    lateral(-1)
    for b in range(4):
        some = pl.ds(4 * b, 4)
        both = jnp.concatenate([xr[some].reshape(160, 128), xi[some].reshape(160, 128)], axis=1)
        spectrum = jnp.dot(both.astype(BF16), xt[0:256, :], preferred_element_type=F32)
        re, im = spectrum[:, :128], spectrum[:, 128:]
        inverse = lax.rsqrt(jnp.maximum(re * re + im * im, 1e-30))
        factor = jnp.maximum(1.0 - level1[some].reshape(160, 128) * inverse, 0.0)
        factor += jnp.maximum(1.0 - level2[some].reshape(160, 128) * inverse, 0.0)
        both = jnp.concatenate([re * factor, im * factor], axis=1)
        inner = jnp.dot(both.astype(BF16), xt[256:512, :], preferred_element_type=F32)
        xr[some] = inner[:, :128].reshape(4, 40, 128)
        xi[some] = inner[:, 128:].reshape(4, 40, 128)
    lateral(1)

    for p in range(16):
        re, im = xr[p, 0:32, :], xi[p, 0:32, :]
        im = jnp.concatenate([jnp.where(packed, xr[p, 32:40, :], im[0:8]), im[8:32]], axis=0)
        back[2 * p] = jnp.where(low, re, pltpu.roll(im, 64, 1)).astype(BF16)
        back[2 * p + 1] = jnp.where(low, pltpu.roll(re, 64, 1), im).astype(BF16)

    def second_copy(dest):
        return copy_to(back.at[dest], got.at[lat], second_s, second_r, shot, dest)

    @pl.loop(1, LAT)
    def _(k):
        second_copy((lat + k) % LAT).start()

    got[lat] = back[lat]
    all_but_one = got.at[pl.ds(0, LAT - 1)]
    pltpu.make_async_copy(all_but_one, all_but_one, second_r).wait()

    for s in range(4):
        tall = got[:, 16 * (s // 2) : 16 * (s // 2) + 16, :].astype(F32)
        flat = tall[:, 8 * (s % 2) : 8 * (s % 2) + 8, :].reshape(256, 128).T.astype(BF16)
        wide = jnp.concatenate([flat[:64], flat[64:]], axis=1)
        mid[s] = jnp.dot(wide, it[512 * s : 512 * s + 512, :], preferred_element_type=F32)

    @pl.loop(0, 8)
    def _(g):
        at = pl.ds(pl.multiple_of(8 * g, 8), 8)
        parts = [(mid[s, at, 0:256], mid[s, at, 256:512]) for s in range(4)]
        values = real_eight_back(parts[0][0], parts[0][1], parts[1], parts[2], parts[3])
        for k in range(8):
            out[0, at, 256 * k : 256 * k + 256] = values[k]

    for c in range(CHUNKS):
        for k in range(2):
            relay_copy(c, k).wait_send()
            side_copy(c, k).wait_send()
            final_copy(c, k).wait_send()
            cross_copy(c, k).wait_send()
    sent = send.at[pl.ds(0, LAT - 1)]
    pltpu.make_async_copy(sent, sent, first_s).wait()
    sent = back.at[pl.ds(0, LAT - 1)]
    pltpu.make_async_copy(sent, sent, second_s).wait()
    mirror_copy().wait_send()

    @pl.when(lat < 16)
    def _():
        for k in range(2):
            corner_copy(k).wait_send()


def on_device(partials, wedges, levels):
    tables = [
        jnp.asarray(t)
        for t in (
            forward_tables(), inverse_tables(), lateral_tables(), turn_tables(), pick_tables(), lane_tables()
        )
    ]
    anywhere = pl.BlockSpec(memory_space=pltpu.HBM)
    vmem, dma = pltpu.VMEM, pltpu.SemaphoreType.DMA
    two = dma((CHUNKS, 2))
    return pl.pallas_call(
        kernel,
        out_shape=jax.ShapeDtypeStruct((1, ROWS, N), F32),
        in_specs=[anywhere, anywhere, pl.BlockSpec(memory_space=pltpu.SMEM)] + [anywhere] * 6,
        out_specs=pl.BlockSpec(memory_space=pltpu.VMEM),
        scratch_shapes=[
            vmem(partials.shape, BF16),
            vmem(wedges.shape, jnp.int32),
            *[vmem(t.shape, t.dtype) for t in tables],
            vmem((CHUNKS, 2, CROWS, N), BF16),
            vmem((CHUNKS, 2, CROWS, N), BF16),
            vmem((CHUNKS, 2, CROWS, N), BF16),
            vmem((CHUNKS, 2, CROWS, N), BF16),
            vmem((128, 1024), BF16),
            vmem((3, 128, 512), BF16),
            vmem((LAT, 32, 128), BF16),
            vmem((LAT, 32, 128), BF16),
            vmem((16, 40, 128), F32),
            vmem((16, 40, 128), F32),
            vmem((16, 40, 128), F32),
            vmem((16, 40, 128), F32),
            vmem((16, 48, 128), BF16),
            vmem((16, 48, 128), BF16),
            vmem((16, 32, 128), BF16),
            vmem((2, 16, 16, 128), BF16),
            vmem((LAT, 32, 128), BF16),
            vmem((LAT, 32, 128), BF16),
            vmem((4, ROWS, 512), F32),
            dma((CHUNKS,)),
            dma((7,)),
            two, two, two, two, two, two, two, two,
            dma, dma, dma, dma,
            dma((3,)),
            dma((3,)),
        ],
        compiler_params=pltpu.CompilerParams(
            collective_id=0, has_side_effects=True, vmem_limit_bytes=60 * 1024 * 1024
        ),
        name="stack_threshold",
    )(partials, wedges, levels, *tables)


def solution(mesh):
    in_specs = (P("shot", None, "lat", None), P("lat", None), P())
    return jax.shard_map(
        on_device, mesh=mesh, in_specs=in_specs, out_specs=P("shot", "lat", None), check_vma=False
    )
```

```python
import functools
import math

import jax
import jax.numpy as jnp
import ml_dtypes
import numpy as np
from jax import lax
from jax.experimental import pallas as pl
from jax.experimental.pallas import tpu as pltpu
from jax.sharding import PartitionSpec as P

MESH = pl.DeviceIdType.MESH
F32 = jnp.float32
BF16 = jnp.bfloat16
N = 2048
LAT = 32
ROWS = N // LAT
CHUNKS = 4
CROWS = ROWS // CHUNKS
HALF = math.sqrt(0.5)
NT = (((1,), (1,)), ((), ()))


def owned():
    ky = np.zeros((LAT, 32), np.int64)
    for d in range(LAT):
        for i in range(8):
            for s in (1, 2, 3):
                ky[d, 8 * s + i] = 64 * d + 8 * i + s
        for i in range(4):
            ky[d, i] = 64 * d + 8 * i + 4
        for i in range(4, 7):
            ky[d, i] = 64 * d + 8 * (i - 3)
        ky[d, 7] = 64 * d + (32 if d < 16 else 0)
    return ky


def forward_tables():
    ky = owned()
    y2 = np.arange(256)
    scale = 1.0 / math.sqrt(N)
    parts = []
    for s in range(4):
        rows = ky[:, 8 * s : 8 * s + 8].reshape(-1)
        angle = 2.0 * np.pi * ((rows[:, None] * y2[None, :]) % N) / N
        re, im = np.cos(angle), -np.sin(angle)
        if s == 0:
            packed = 16 * 8 + 7
            re[packed] = np.where(y2 % 2, -1.0, 1.0)
            im[packed] = 1.0
            four = (rows % 8 == 4)[:, None]
            zero = np.zeros_like(re)
            parts += [
                np.where(four, zero, re),
                np.where(four, re, zero),
                np.where(four, zero, im),
                np.where(four, im, zero),
            ]
        else:
            parts += [re, im]
    return (np.concatenate(parts, axis=1) * scale).astype(ml_dtypes.bfloat16)


def inverse_tables():
    ky = owned()
    y2 = np.arange(256)
    scale = 1.0 / math.sqrt(N)
    parts = []
    for s in range(4):
        rows = ky[:, 8 * s : 8 * s + 8].reshape(-1)
        angle = 2.0 * np.pi * ((rows[:, None] * y2[None, :]) % N) / N
        cos, sin = 2.0 * np.cos(angle), 2.0 * np.sin(angle)
        if s == 0:
            packed = 16 * 8 + 7
            cos[packed] = np.where(y2 % 2, -1.0, 1.0)
            sin[packed] = -1.0
            four = (rows % 8 == 4)[:, None]
            zero = np.zeros_like(cos)
            top = np.concatenate([np.where(four, zero, cos), np.where(four, cos, zero)], axis=1)
            low = np.concatenate([np.where(four, zero, -sin), np.where(four, -sin, zero)], axis=1)
        else:
            top = np.concatenate([cos, sin], axis=1)
            low = np.concatenate([-sin, cos], axis=1)
        parts += [top, low]
    return (np.concatenate(parts, axis=0) * scale).astype(ml_dtypes.bfloat16)


def lateral_tables():
    index = np.arange(128)
    angle = 2.0 * np.pi * ((index[:, None] * index[None, :]) % 128) / 128
    cos, sin = np.cos(angle), np.sin(angle)
    forward = np.block([[cos, -sin], [sin, cos]])
    inverse = np.block([[cos, sin], [-sin, cos]])
    return np.concatenate([forward, inverse], axis=0).astype(ml_dtypes.bfloat16)


def turn_tables():
    angle = 2.0 * np.pi * (np.arange(16)[:, None] * np.arange(128)[None, :]) / N
    scale = 1.0 / math.sqrt(N)
    cos, sin = np.cos(angle) * scale, np.sin(angle) * scale
    return np.stack([cos, -sin, 0.5 * cos, 0.5 * sin]).astype(np.float32)


def pick_tables():
    own = np.zeros((48, 64))
    mirror = np.zeros((48, 64))
    for i in range(8):
        for s in (1, 2, 3):
            own[8 * s + i, 8 * i + s] = 1
            mirror[8 * s + i, 8 * (7 - i) + 8 - s] = 1
    for i in range(4):
        own[i, 8 * i + 4] = 1
        mirror[i, 8 * (7 - i) + 4] = 1
    for i in range(4, 7):
        own[i, 8 * (i - 3)] = 1
        mirror[i, 8 * (11 - i)] = 1
    own[7, 32] = mirror[7, 32] = 1
    own[39, 0] = mirror[39, 0] = 1
    return np.concatenate([own, mirror], axis=0).astype(ml_dtypes.bfloat16)


def lane_tables():
    lanes = np.arange(128)
    place = (lanes % 16) * 8 + lanes // 16
    own = np.zeros((128, 128))
    own[lanes, place] = 1
    mirror = np.zeros((256, 128))
    mirror[128 - lanes, place] = 1
    return np.concatenate([own, mirror], axis=0).astype(ml_dtypes.bfloat16)


def turn(pair, step, length, sign):
    re, im = pair
    step = step % length
    if step == 0:
        return pair
    if 4 * step == length:
        return (-im, re) if sign > 0 else (im, -re)
    if 8 * step == length:
        return ((re - sign * im) * HALF, (im + sign * re) * HALF)
    if 8 * step == 3 * length:
        return ((-re - sign * im) * HALF, (-im + sign * re) * HALF)
    cos = math.cos(2.0 * math.pi * step / length)
    sin = sign * math.sin(2.0 * math.pi * step / length)
    return (re * cos - im * sin, im * cos + re * sin)


def short_transform(values, sign):
    count = len(values)
    if count == 1:
        return values
    even = short_transform(values[0::2], sign)
    odd = short_transform(values[1::2], sign)
    low, high = [], []
    for k in range(count // 2):
        re, im = turn(odd[k], k, count, sign)
        low.append((even[k][0] + re, even[k][1] + im))
        high.append((even[k][0] - re, even[k][1] - im))
    return low + high


def real_eight(u):
    a = [u[k] + u[k + 4] for k in range(4)]
    b = [u[k] - u[k + 4] for k in range(4)]
    even, odd = a[0] + a[2], a[1] + a[3]
    minus, plus = (b[1] - b[3]) * HALF, (b[1] + b[3]) * HALF
    return (
        even + odd,
        even - odd,
        (b[0] + minus, -(b[2] + plus)),
        (a[0] - a[2], a[3] - a[1]),
        (b[0] - minus, b[2] - plus),
    )


def real_eight_back(zero, four, one, two, three):
    plus, minus = zero + four, zero - four
    (r1, i1), (r2, i2), (r3, i3) = one, two, three
    p0, p1 = plus + r2, plus - r2
    m0, m1 = minus - i2, minus + i2
    e0, e1 = r1 + r3, i3 - i1
    o0 = (r1 - i1 - r3 - i3) * HALF
    o1 = (r3 - i3 - r1 - i1) * HALF
    return [p0 + e0, m0 + o0, p1 + e1, m1 + o1, p0 - e0, m0 - o0, p1 - e1, m1 - o1]


def spread(tiles, lane):
    for bit in (8, 4, 2, 1):
        high = (lane // 8) % (2 * bit) >= bit
        new = list(tiles)
        for t in range(16):
            if t & bit:
                continue
            first, second = tiles[t], tiles[t | bit]
            new[t] = jnp.where(high, pltpu.roll(second, 8 * bit, 1), first)
            new[t | bit] = jnp.where(high, second, pltpu.roll(first, 128 - 8 * bit, 1))
        tiles = new
    return tiles


def kernel(
    part_hbm, wedge_hbm, levels, ft_hbm, it_hbm, xt_hbm, tw_hbm, pick_hbm, lane_hbm,
    out,
    part, wedge, ft, it, xt, tw, pick, lanet,
    relay, side, final, cross,
    folded0, folded1, send, held, xr, xi, level1, level2, own_ids, mir_ids, mir_in, spec_in, back, got, mid,
    load_sem, table_sem, relay_s, relay_r, side_s, side_r, final_s, final_r, cross_s, cross_r,
    first_s, first_r, second_s, second_r, wedge_s, wedge_r, met,
):
    shot = lax.axis_index("shot")
    lat = lax.axis_index("lat")
    n_shot = lax.axis_size("shot")
    y, xh = shot // 2, shot % 2
    up, down = (shot + 2) % n_shot, (shot + n_shot - 2) % n_shot
    y_up, y_down, y_far = (y + 1) % 4, (y + 3) % 4, (y + 2) % 4
    flip = lat + 2 - 4 * ((lat // 2) % 2)
    other = shot + 1 - 2 * xh

    def rows(c):
        return pl.ds(c * CROWS, CROWS)

    loads = [
        pltpu.make_async_copy(
            part_hbm.at[:, :, rows(c), :], part.at[:, :, rows(c), :], load_sem.at[c]
        )
        for c in range(CHUNKS)
    ]
    loads[0].start()
    tables = [
        pltpu.make_async_copy(src, dst, table_sem.at[k])
        for k, (src, dst) in enumerate(
            [(wedge_hbm, wedge), (pick_hbm, pick), (lane_hbm, lanet), (ft_hbm, ft),
             (xt_hbm, xt), (tw_hbm, tw), (it_hbm, it)]
        )
    ]
    for c in range(1, CHUNKS):
        loads[c].start()
    for copy in tables:
        copy.start()

    barrier = pltpu.get_barrier_semaphore()

    def greet(s, l):
        pl.semaphore_signal(barrier, inc=1, device_id=(s, l), device_id_type=MESH)

    def neighbour(bit):
        return lat + bit - 2 * bit * ((lat // bit) % 2)

    bits = (1, 2, 4, 8, 16)
    for bit in bits:
        greet(shot, neighbour(bit))
    greet(up, lat)
    greet(down, lat)
    greet(other, flip)

    def meet(k):
        if k > 0:
            pl.semaphore_wait(met.at[k - 1], 1)
        if k < len(bits):
            pl.semaphore_signal(
                met.at[k], inc=1, device_id=(shot, neighbour(bits[k])), device_id_type=MESH
            )

    def copy_to(src, dst, s_sem, r_sem, s, l):
        return pltpu.make_async_remote_copy(
            src_ref=src, dst_ref=dst, send_sem=s_sem, recv_sem=r_sem, device_id=(s, l), device_id_type=MESH
        )

    def slab(q, c):
        return part.at[0, q, rows(c), :]

    def relay_copy(c, k):
        q = 2 * y_far + k
        return copy_to(
            slab(q, c), relay.at[c, k], relay_s.at[c, k], relay_r.at[c, k], up if k == 0 else down, lat
        )

    def side_copy(c, k):
        q = 2 * y_up + 1 if k == 0 else 2 * y_down
        return copy_to(
            slab(q, c), side.at[c, k], side_s.at[c, k], side_r.at[c, k], up if k == 0 else down, lat
        )

    def final_copy(c, k):
        q = 2 * y_up if k == 0 else 2 * y_down + 1
        return copy_to(
            slab(q, c), final.at[c, k], final_s.at[c, k], final_r.at[c, k], up if k == 0 else down, lat
        )

    def cross_copy(c, h):
        return copy_to(
            slab(2 * y + h, c), cross.at[c, xh], cross_s.at[c, h], cross_r.at[c, xh], 2 * y + h, flip
        )

    def pair(q, c):
        return part[0, q, rows(c), :].astype(F32) + part[1, q, rows(c), :].astype(F32)

    def prepare(c):
        loads[c].wait()
        for q in (2 * y_far, 2 * y_far + 1, 2 * y_up + 1, 2 * y_down):
            part[0, q, rows(c), :] = pair(q, c).astype(BF16)

    def launch(c):
        for k in range(2):
            relay_copy(c, k).start()
        for k in range(2):
            side_copy(c, k).start()

    def begin(c):
        prepare(c)
        launch(c)

    def forward(c):
        for k in range(2):
            q = 2 * y_up if k == 0 else 2 * y_down + 1
            relay_copy(c, k).wait_recv()
            part[0, q, rows(c), :] = (pair(q, c) + relay[c, k].astype(F32)).astype(BF16)
            final_copy(c, k).start()

    def across(c):
        for k in range(2):
            side_copy(c, k).wait_recv()
            final_copy(c, k).wait_recv()
        for h in range(2):
            q = 2 * y + h
            total = pair(q, c) + final[c, h].astype(F32) + side[c, 1 - h].astype(F32)
            part[0, q, rows(c), :] = total.astype(BF16)
            cross_copy(c, h).start()

    def fold(c):
        for h in range(2):
            pltpu.make_async_copy(cross.at[c, h], cross.at[c, h], cross_r.at[c, h]).wait()
        top, low = pl.ds(c * CROWS, CROWS), pl.ds(ROWS + c * CROWS, CROWS)
        u = []
        for k in range(8):
            cols = pl.ds(256 * k, 256)
            u.append(cross[c, 0, :, cols].astype(F32) + cross[c, 1, :, cols].astype(F32))
        zero, four, one, two, three = real_eight(u)
        zero, four = zero.astype(BF16), four.astype(BF16)
        blank = jnp.zeros((CROWS, 512), BF16)
        folded0[top, 0:256] = zero
        folded0[top, 256:512] = four
        folded0[top, 512:1024] = blank
        folded0[low, 0:512] = blank
        folded0[low, 512:768] = zero
        folded0[low, 768:1024] = four
        for s, (re, im) in enumerate((one, two, three)):
            re, im, neg = re.astype(BF16), im.astype(BF16), (-im).astype(BF16)
            folded1[s, top, 0:256] = re
            folded1[s, top, 256:512] = neg
            folded1[s, low, 0:256] = im
            folded1[s, low, 256:512] = re

    def first_copy(dest):
        return copy_to(send.at[dest], held.at[flip], first_s, first_r, shot, dest)

    def second_copy(dest):
        return copy_to(back.at[dest], got.at[lat], second_s, second_r, shot, dest)

    lane = lax.broadcasted_iota(jnp.int32, (1, 128), 1)
    low = lane < 64
    packed = (lax.broadcasted_iota(jnp.int32, (8, 128), 0) == 7) & (lat == 16)
    seventh = lax.broadcasted_iota(jnp.int32, (8, 128), 0) == 7

    partner = LAT - 1 - lat
    corner = jnp.where(lat == 0, 16, LAT - lat)

    def mirror_copy():
        return copy_to(
            mir_ids.at[:, pl.ds(0, 32), :], mir_in, wedge_s.at[0], wedge_r.at[0], shot, partner
        )

    def corner_copy(k):
        src = (own_ids if k == 0 else mir_ids).at[:, pl.ds(32, 16), :]
        return copy_to(src, spec_in.at[k], wedge_s.at[1 + k], wedge_r.at[1 + k], shot, corner)

    def wedges_out():
        for k in range(3):
            tables[k].wait()
        ids = wedge[...].astype(F32).astype(BF16)
        chosen = jnp.dot(pick[...], ids, preferred_element_type=F32).astype(BF16)
        own, mir = chosen[:48], chosen[48:]
        tall = jnp.concatenate([own[:, 128 * t : 128 * t + 128] for t in range(16)], axis=0)
        moved = jnp.dot(tall, lanet[0:128, :], preferred_element_type=F32)
        for t, tile in enumerate(spread([moved[48 * t : 48 * t + 48] for t in range(16)], lane)):
            own_ids[t] = tile.astype(BF16)
        tall = jnp.concatenate(
            [
                jnp.concatenate(
                    [mir[:, 128 * (15 - t) : 128 * (16 - t)],
                     mir[:, 128 * ((16 - t) % 16) : 128 * ((16 - t) % 16) + 128]],
                    axis=1,
                )
                for t in range(16)
            ],
            axis=0,
        )
        moved = jnp.dot(tall, lanet[128:384, :], preferred_element_type=F32)
        for t, tile in enumerate(spread([moved[48 * t : 48 * t + 48] for t in range(16)], lane)):
            mir_ids[t] = tile.astype(BF16)

    def wedges_go():
        mirror_copy().start()

        @pl.when(lat < 16)
        def _():
            for k in range(2):
                corner_copy(k).start()

    def look_up(ids):
        found = jnp.full(ids.shape, levels[0], F32)
        for w in range(1, 16):
            found = jnp.where(ids == float(w), levels[w], found)
        return found

    def wedges_in():
        mirror_copy().wait_recv()

        @pl.when(lat >= 16)
        def _():
            for k in range(2):
                corner_copy(k).wait_recv()

        @pl.loop(0, 16)
        def _(kk):
            own = own_ids[kk].astype(F32)
            mir = mir_ids[kk].astype(F32)
            got_mir = mir_in[kk].astype(F32)
            spec_own = spec_in[0, kk].astype(F32)
            spec_mir = spec_in[1, kk].astype(F32)
            level1[kk, 0:8, :] = look_up(jnp.where(seventh & (lat >= 16), own[32:40], own[0:8]))
            level1[kk, 8:32, :] = look_up(own[8:32])
            level1[kk, 32:40, :] = look_up(spec_own[0:8])
            row = jnp.where(lat == 16, mir[32:40], spec_mir[0:8])
            level2[kk, 0:8, :] = look_up(jnp.where(seventh & (lat >= 16), row, got_mir[0:8]))
            level2[kk, 8:32, :] = look_up(got_mir[8:32])
            level2[kk, 32:40, :] = look_up(spec_mir[0:8])

    def stack():
        prepare(0)
        pl.semaphore_wait(barrier, len(bits) + 3)
        launch(0)
        meet(0)
        begin(1)
        meet(1)
        forward(0)
        meet(2)
        wedges_out()
        meet(3)
        begin(2)
        forward(1)
        meet(4)
        across(0)
        begin(3)
        meet(5)
        wedges_go()
        forward(2)
        across(1)
        fold(0)
        forward(3)
        across(2)
        fold(1)
        wedges_in()
        across(3)
        fold(2)
        for k in range(3, 7):
            tables[k].wait()
        fold(3)

    def columns():
        pieces = [
            lax.dot_general(ft[:, 0:1024], folded0[...], NT, preferred_element_type=F32).reshape(LAT, 8, 128)
        ]
        for s in range(3):
            pieces.append(
                lax.dot_general(
                    ft[:, 1024 + 512 * s : 1536 + 512 * s], folded1[s], NT, preferred_element_type=F32
                ).reshape(LAT, 8, 128)
            )
        for k in range(2):
            both = jnp.concatenate([pieces[2 * k], pieces[2 * k + 1]], axis=1)
            send[:, 16 * k : 16 * k + 16, :] = both.astype(BF16)

        @pl.loop(1, LAT)
        def _(k):
            first_copy((lat + k) % LAT).start()

        held[flip] = send[lat]
        all_but_one = held.at[pl.ds(0, LAT - 1)]
        pltpu.make_async_copy(all_but_one, all_but_one, first_r).wait()

    def unpack():
        nothing = jnp.zeros((8, 128), F32)
        for p in range(16):
            u0, u1 = held[2 * p].astype(F32), held[2 * p + 1].astype(F32)
            re = jnp.where(low, u0, pltpu.roll(u1, 64, 1))
            im = jnp.where(low, pltpu.roll(u0, 64, 1), u1)
            xr[p, 0:32, :] = re
            xi[p, 0:8, :] = jnp.where(packed, 0.0, im[0:8])
            xi[p, 8:32, :] = im[8:32]
            xr[p, 32:40, :] = im[0:8]
            xi[p, 32:40, :] = nothing

    def lateral(sign):
        base = 0 if sign < 0 else 2

        @pl.loop(0, 5)
        def _(g):
            at = pl.ds(pl.multiple_of(8 * g, 8), 8)
            values = []
            for p in range(16):
                value = (xr[p, at, :], xi[p, at, :])
                if sign > 0:
                    cos, sin = tw[base, p : p + 1, :], tw[base + 1, p : p + 1, :]
                    value = (value[0] * cos - value[1] * sin, value[1] * cos + value[0] * sin)
                values.append(value)
            for p, value in enumerate(short_transform(values, sign)):
                if sign < 0:
                    cos, sin = tw[base, p : p + 1, :], tw[base + 1, p : p + 1, :]
                    value = (value[0] * cos - value[1] * sin, value[1] * cos + value[0] * sin)
                xr[p, at, :] = value[0]
                xi[p, at, :] = value[1]

    def middle():
        lateral(-1)
        for b in range(4):
            some = pl.ds(4 * b, 4)
            both = jnp.concatenate([xr[some].reshape(160, 128), xi[some].reshape(160, 128)], axis=1)
            spectrum = jnp.dot(both.astype(BF16), xt[0:256, :], preferred_element_type=F32)
            re, im = spectrum[:, :128], spectrum[:, 128:]
            inverse = lax.rsqrt(jnp.maximum(re * re + im * im, 1e-30))
            factor = jnp.maximum(1.0 - level1[some].reshape(160, 128) * inverse, 0.0)
            factor += jnp.maximum(1.0 - level2[some].reshape(160, 128) * inverse, 0.0)
            both = jnp.concatenate([re * factor, im * factor], axis=1)
            inner = jnp.dot(both.astype(BF16), xt[256:512, :], preferred_element_type=F32)
            xr[some] = inner[:, :128].reshape(4, 40, 128)
            xi[some] = inner[:, 128:].reshape(4, 40, 128)
        lateral(1)

    def turn_back():
        for p in range(16):
            re, im = xr[p, 0:32, :], xi[p, 0:32, :]
            im = jnp.concatenate([jnp.where(packed, xr[p, 32:40, :], im[0:8]), im[8:32]], axis=0)
            back[2 * p] = jnp.where(low, re, pltpu.roll(im, 64, 1)).astype(BF16)
            back[2 * p + 1] = jnp.where(low, pltpu.roll(re, 64, 1), im).astype(BF16)

        @pl.loop(1, LAT)
        def _(k):
            second_copy((lat + k) % LAT).start()

        got[lat] = back[lat]
        all_but_one = got.at[pl.ds(0, LAT - 1)]
        pltpu.make_async_copy(all_but_one, all_but_one, second_r).wait()

    def columns_back():
        for s in range(4):
            tall = got[:, 16 * (s // 2) : 16 * (s // 2) + 16, :].astype(F32)
            flat = tall[:, 8 * (s % 2) : 8 * (s % 2) + 8, :].reshape(256, 128).T.astype(BF16)
            wide = jnp.concatenate([flat[:64], flat[64:]], axis=1)
            mid[s] = jnp.dot(wide, it[512 * s : 512 * s + 512, :], preferred_element_type=F32)

        @pl.loop(0, 8)
        def _(g):
            at = pl.ds(pl.multiple_of(8 * g, 8), 8)
            parts = [(mid[s, at, 0:256], mid[s, at, 256:512]) for s in range(4)]
            values = real_eight_back(parts[0][0], parts[0][1], parts[1], parts[2], parts[3])
            for k in range(8):
                out[0, at, 256 * k : 256 * k + 256] = values[k]

    def drain():
        for c in range(CHUNKS):
            for k in range(2):
                relay_copy(c, k).wait_send()
                side_copy(c, k).wait_send()
                final_copy(c, k).wait_send()
                cross_copy(c, k).wait_send()
        sent = send.at[pl.ds(0, LAT - 1)]
        pltpu.make_async_copy(sent, sent, first_s).wait()
        sent = back.at[pl.ds(0, LAT - 1)]
        pltpu.make_async_copy(sent, sent, second_s).wait()
        mirror_copy().wait_send()

        @pl.when(lat < 16)
        def _():
            for k in range(2):
                corner_copy(k).wait_send()


    stack()
    columns()
    unpack()
    middle()
    turn_back()
    columns_back()
    drain()


def on_device(partials, wedges, levels):
    tables = [
        jnp.asarray(t)
        for t in (
            forward_tables(), inverse_tables(), lateral_tables(), turn_tables(), pick_tables(), lane_tables()
        )
    ]
    anywhere = pl.BlockSpec(memory_space=pltpu.HBM)
    vmem, dma = pltpu.VMEM, pltpu.SemaphoreType.DMA
    two = dma((CHUNKS, 2))
    return pl.pallas_call(
        kernel,
        out_shape=jax.ShapeDtypeStruct((1, ROWS, N), F32),
        in_specs=[anywhere, anywhere, pl.BlockSpec(memory_space=pltpu.SMEM)] + [anywhere] * 6,
        out_specs=pl.BlockSpec(memory_space=pltpu.VMEM),
        scratch_shapes=[
            vmem(partials.shape, BF16),
            vmem(wedges.shape, jnp.int32),
            *[vmem(t.shape, t.dtype) for t in tables],
            vmem((CHUNKS, 2, CROWS, N), BF16),
            vmem((CHUNKS, 2, CROWS, N), BF16),
            vmem((CHUNKS, 2, CROWS, N), BF16),
            vmem((CHUNKS, 2, CROWS, N), BF16),
            vmem((128, 1024), BF16),
            vmem((3, 128, 512), BF16),
            vmem((LAT, 32, 128), BF16),
            vmem((LAT, 32, 128), BF16),
            vmem((16, 40, 128), F32),
            vmem((16, 40, 128), F32),
            vmem((16, 40, 128), F32),
            vmem((16, 40, 128), F32),
            vmem((16, 48, 128), BF16),
            vmem((16, 48, 128), BF16),
            vmem((16, 32, 128), BF16),
            vmem((2, 16, 16, 128), BF16),
            vmem((LAT, 32, 128), BF16),
            vmem((LAT, 32, 128), BF16),
            vmem((4, ROWS, 512), F32),
            dma((CHUNKS,)),
            dma((7,)),
            two, two, two, two, two, two, two, two,
            dma, dma, dma, dma,
            dma((3,)),
            dma((3,)),
            pltpu.SemaphoreType.REGULAR((5,)),
        ],
        compiler_params=pltpu.CompilerParams(
            collective_id=0, has_side_effects=True, vmem_limit_bytes=32 * 1024 * 1024
        ),
        name="stack_threshold",
    )(partials, wedges, levels, *tables)


def solution(mesh):
    in_specs = (P("shot", None, "lat", None), P("lat", None), P())
    return jax.shard_map(
        on_device, mesh=mesh, in_specs=in_specs, out_specs=P("shot", "lat", None), check_vma=False
    )
```

```python
import functools
import math

import jax
import jax.numpy as jnp
import ml_dtypes
import numpy as np
from jax import lax
from jax.experimental import pallas as pl
from jax.experimental.pallas import tpu as pltpu
from jax.sharding import PartitionSpec as P

MESH = pl.DeviceIdType.MESH
F32 = jnp.float32
BF16 = jnp.bfloat16
N = 2048
LAT = 32
ROWS = N // LAT
CHUNKS = 4
CROWS = ROWS // CHUNKS
HALF = math.sqrt(0.5)
NT = (((1,), (1,)), ((), ()))


def owned():
    ky = np.zeros((LAT, 32), np.int64)
    for d in range(LAT):
        for i in range(8):
            for s in (1, 2, 3):
                ky[d, 8 * s + i] = 64 * d + 8 * i + s
        for i in range(4):
            ky[d, i] = 64 * d + 8 * i + 4
        for i in range(4, 7):
            ky[d, i] = 64 * d + 8 * (i - 3)
        ky[d, 7] = 64 * d + (32 if d < 16 else 0)
    return ky


def forward_tables():
    ky = owned()
    y2 = np.arange(256)
    scale = 1.0 / math.sqrt(N)
    parts = []
    for s in range(4):
        rows = ky[:, 8 * s : 8 * s + 8].reshape(-1)
        angle = 2.0 * np.pi * ((rows[:, None] * y2[None, :]) % N) / N
        re, im = np.cos(angle), -np.sin(angle)
        if s == 0:
            packed = 16 * 8 + 7
            re[packed] = np.where(y2 % 2, -1.0, 1.0)
            im[packed] = 1.0
            four = (rows % 8 == 4)[:, None]
            zero = np.zeros_like(re)
            parts += [
                np.where(four, zero, re),
                np.where(four, re, zero),
                np.where(four, zero, im),
                np.where(four, im, zero),
            ]
        else:
            parts += [re, im]
    return (np.concatenate(parts, axis=1) * scale).astype(ml_dtypes.bfloat16)


def inverse_tables():
    ky = owned()
    y2 = np.arange(256)
    scale = 1.0 / math.sqrt(N)
    parts = []
    for s in range(4):
        rows = ky[:, 8 * s : 8 * s + 8].reshape(-1)
        angle = 2.0 * np.pi * ((rows[:, None] * y2[None, :]) % N) / N
        cos, sin = 2.0 * np.cos(angle), 2.0 * np.sin(angle)
        if s == 0:
            packed = 16 * 8 + 7
            cos[packed] = np.where(y2 % 2, -1.0, 1.0)
            sin[packed] = -1.0
            four = (rows % 8 == 4)[:, None]
            zero = np.zeros_like(cos)
            top = np.concatenate([np.where(four, zero, cos), np.where(four, cos, zero)], axis=1)
            low = np.concatenate([np.where(four, zero, -sin), np.where(four, -sin, zero)], axis=1)
        else:
            top = np.concatenate([cos, sin], axis=1)
            low = np.concatenate([-sin, cos], axis=1)
        parts += [top, low]
    return (np.concatenate(parts, axis=0) * scale).astype(ml_dtypes.bfloat16)


def lateral_tables():
    index = np.arange(128)
    angle = 2.0 * np.pi * ((index[:, None] * index[None, :]) % 128) / 128
    cos, sin = np.cos(angle), np.sin(angle)
    forward = np.block([[cos, -sin], [sin, cos]])
    inverse = np.block([[cos, sin], [-sin, cos]])
    return np.concatenate([forward, inverse], axis=0).astype(ml_dtypes.bfloat16)


def turn_tables():
    angle = 2.0 * np.pi * (np.arange(16)[:, None] * np.arange(128)[None, :]) / N
    scale = 1.0 / math.sqrt(N)
    cos, sin = np.cos(angle) * scale, np.sin(angle) * scale
    return np.stack([cos, -sin, 0.5 * cos, 0.5 * sin]).astype(np.float32)


def pick_tables():
    own = np.zeros((48, 64))
    mirror = np.zeros((48, 64))
    for i in range(8):
        for s in (1, 2, 3):
            own[8 * s + i, 8 * i + s] = 1
            mirror[8 * s + i, 8 * (7 - i) + 8 - s] = 1
    for i in range(4):
        own[i, 8 * i + 4] = 1
        mirror[i, 8 * (7 - i) + 4] = 1
    for i in range(4, 7):
        own[i, 8 * (i - 3)] = 1
        mirror[i, 8 * (11 - i)] = 1
    own[7, 32] = mirror[7, 32] = 1
    own[39, 0] = mirror[39, 0] = 1
    return np.concatenate([own, mirror], axis=0).astype(ml_dtypes.bfloat16)


def lane_tables():
    lanes = np.arange(128)
    place = (lanes % 16) * 8 + lanes // 16
    own = np.zeros((128, 128))
    own[lanes, place] = 1
    mirror = np.zeros((256, 128))
    mirror[128 - lanes, place] = 1
    return np.concatenate([own, mirror], axis=0).astype(ml_dtypes.bfloat16)


def turn(pair, step, length, sign):
    re, im = pair
    step = step % length
    if step == 0:
        return pair
    if 4 * step == length:
        return (-im, re) if sign > 0 else (im, -re)
    if 8 * step == length:
        return ((re - sign * im) * HALF, (im + sign * re) * HALF)
    if 8 * step == 3 * length:
        return ((-re - sign * im) * HALF, (-im + sign * re) * HALF)
    cos = math.cos(2.0 * math.pi * step / length)
    sin = sign * math.sin(2.0 * math.pi * step / length)
    return (re * cos - im * sin, im * cos + re * sin)


def short_transform(values, sign):
    count = len(values)
    if count == 1:
        return values
    even = short_transform(values[0::2], sign)
    odd = short_transform(values[1::2], sign)
    low, high = [], []
    for k in range(count // 2):
        re, im = turn(odd[k], k, count, sign)
        low.append((even[k][0] + re, even[k][1] + im))
        high.append((even[k][0] - re, even[k][1] - im))
    return low + high


def real_eight(u):
    a = [u[k] + u[k + 4] for k in range(4)]
    b = [u[k] - u[k + 4] for k in range(4)]
    even, odd = a[0] + a[2], a[1] + a[3]
    minus, plus = (b[1] - b[3]) * HALF, (b[1] + b[3]) * HALF
    return (
        even + odd,
        even - odd,
        (b[0] + minus, -(b[2] + plus)),
        (a[0] - a[2], a[3] - a[1]),
        (b[0] - minus, b[2] - plus),
    )


def real_eight_back(zero, four, one, two, three):
    plus, minus = zero + four, zero - four
    (r1, i1), (r2, i2), (r3, i3) = one, two, three
    p0, p1 = plus + r2, plus - r2
    m0, m1 = minus - i2, minus + i2
    e0, e1 = r1 + r3, i3 - i1
    o0 = (r1 - i1 - r3 - i3) * HALF
    o1 = (r3 - i3 - r1 - i1) * HALF
    return (p0, m0, p1, m1), (e0, o0, e1, o1)


def spread(tiles, lane):
    for bit in (8, 4, 2, 1):
        high = (lane // 8) % (2 * bit) >= bit
        new = list(tiles)
        for t in range(16):
            if t & bit:
                continue
            first, second = tiles[t], tiles[t | bit]
            new[t] = jnp.where(high, pltpu.roll(second, 8 * bit, 1), first)
            new[t | bit] = jnp.where(high, second, pltpu.roll(first, 128 - 8 * bit, 1))
        tiles = new
    return tiles


def kernel(
    part_hbm, wedge_hbm, levels, ft_hbm, it_hbm, xt_hbm, tw_hbm, pick_hbm, lane_hbm,
    out_even, out_odd,
    part, wedge, ft, it, xt, tw, pick, lanet,
    relay, side, final, cross, wide, total, relay2, side2, final2,
    folded0, folded1, send, held, xr, xi, level1, level2, own_ids, mir_ids, mir_in, spec_in, back, got, mid,
    load_sem, table_sem, relay_s, relay_r, side_s, side_r, final_s, final_r, cross_s, cross_r,
    first_s, first_r, second_s, second_r, wedge_s, wedge_r,
    wide_s, wide_r, relay2_s, relay2_r, side2_s, side2_r, final2_s, final2_r, met,
):
    shot = lax.axis_index("shot")
    lat = lax.axis_index("lat")
    n_shot = lax.axis_size("shot")
    y, xh = shot // 2, shot % 2
    up, down = (shot + 2) % n_shot, (shot + n_shot - 2) % n_shot
    y_up, y_down, y_far = (y + 1) % 4, (y + 3) % 4, (y + 2) % 4
    flip = lat + 2 - 4 * ((lat // 2) % 2)
    other = shot + 1 - 2 * xh

    def rows(c):
        return pl.ds(c * CROWS, CROWS)

    loads = [
        pltpu.make_async_copy(
            part_hbm.at[:, :, rows(c), :], part.at[:, :, rows(c), :], load_sem.at[c]
        )
        for c in range(CHUNKS)
    ]
    loads[0].start()
    tables = [
        pltpu.make_async_copy(src, dst, table_sem.at[k])
        for k, (src, dst) in enumerate(
            [(wedge_hbm, wedge), (pick_hbm, pick), (lane_hbm, lanet), (ft_hbm, ft),
             (xt_hbm, xt), (tw_hbm, tw), (it_hbm, it)]
        )
    ]
    for c in range(1, CHUNKS):
        loads[c].start()
    for copy in tables:
        copy.start()

    barrier = pltpu.get_barrier_semaphore()

    def greet(s, l):
        pl.semaphore_signal(barrier, inc=1, device_id=(s, l), device_id_type=MESH)

    def neighbour(bit):
        return lat + bit - 2 * bit * ((lat // bit) % 2)

    bits = (1, 2, 4, 8, 16)
    for bit in bits:
        greet(shot, neighbour(bit))
    greet(up, lat)
    greet(down, lat)
    greet(other, flip)

    def meet(k):
        if k > 0:
            pl.semaphore_wait(met.at[k - 1], 1)
        if k < len(bits):
            pl.semaphore_signal(
                met.at[k], inc=1, device_id=(shot, neighbour(bits[k])), device_id_type=MESH
            )

    def copy_to(src, dst, s_sem, r_sem, s, l):
        return pltpu.make_async_remote_copy(
            src_ref=src, dst_ref=dst, send_sem=s_sem, recv_sem=r_sem, device_id=(s, l), device_id_type=MESH
        )

    def slab(q, c):
        return part.at[0, q, rows(c), :]

    def relay_copy(c, k):
        q = 2 * y_far + k
        return copy_to(
            slab(q, c), relay.at[c, k], relay_s.at[c, k], relay_r.at[c, k], up if k == 0 else down, lat
        )

    def side_copy(c, k):
        q = 2 * y_up + 1 if k == 0 else 2 * y_down
        return copy_to(
            slab(q, c), side.at[c, k], side_s.at[c, k], side_r.at[c, k], up if k == 0 else down, lat
        )

    def final_copy(c, k):
        q = 2 * y_up if k == 0 else 2 * y_down + 1
        return copy_to(
            slab(q, c), final.at[c, k], final_s.at[c, k], final_r.at[c, k], up if k == 0 else down, lat
        )

    def cross_copy(c, h):
        return copy_to(
            slab(2 * y + h, c), cross.at[c, xh], cross_s.at[c, h], cross_r.at[c, xh], 2 * y + h, flip
        )

    def pair(q, c):
        return part[0, q, rows(c), :].astype(F32) + part[1, q, rows(c), :].astype(F32)

    def prepare(c):
        loads[c].wait()
        for q in (2 * y_far, 2 * y_far + 1, 2 * y_up + 1, 2 * y_down):
            part[0, q, rows(c), :] = pair(q, c).astype(BF16)

    def launch(c):
        for k in range(2):
            relay_copy(c, k).start()
        for k in range(2):
            side_copy(c, k).start()

    def begin(c):
        prepare(c)
        launch(c)

    def forward(c):
        for k in range(2):
            q = 2 * y_up if k == 0 else 2 * y_down + 1
            relay_copy(c, k).wait_recv()
            part[0, q, rows(c), :] = (pair(q, c) + relay[c, k].astype(F32)).astype(BF16)
            final_copy(c, k).start()

    def across(c):
        for k in range(2):
            side_copy(c, k).wait_recv()
            final_copy(c, k).wait_recv()
        for h in range(2):
            q = 2 * y + h
            total = pair(q, c) + final[c, h].astype(F32) + side[c, 1 - h].astype(F32)
            part[0, q, rows(c), :] = total.astype(BF16)
            cross_copy(c, h).start()

    def fold(c):
        for h in range(2):
            pltpu.make_async_copy(cross.at[c, h], cross.at[c, h], cross_r.at[c, h]).wait()
        u = []
        for k in range(8):
            cols = pl.ds(256 * k, 256)
            u.append(cross[c, 0, :, cols].astype(F32) + cross[c, 1, :, cols].astype(F32))
        keep(c, u)

    def keep(c, u):
        top, low = pl.ds(c * CROWS, CROWS), pl.ds(ROWS + c * CROWS, CROWS)
        zero, four, one, two, three = real_eight(u)
        zero, four = zero.astype(BF16), four.astype(BF16)
        blank = jnp.zeros((CROWS, 512), BF16)
        folded0[top, 0:256] = zero
        folded0[top, 256:512] = four
        folded0[top, 512:1024] = blank
        folded0[low, 0:512] = blank
        folded0[low, 512:768] = zero
        folded0[low, 768:1024] = four
        for s, (re, im) in enumerate((one, two, three)):
            re, im, neg = re.astype(BF16), im.astype(BF16), (-im).astype(BF16)
            folded1[s, top, 0:256] = re
            folded1[s, top, 256:512] = neg
            folded1[s, low, 0:256] = im
            folded1[s, low, 256:512] = re

    halves = (pl.ds(0, N // 2), pl.ds(N // 2, N // 2))
    y_order = (y_far, y_up, y_down, y)

    def wide_copy(c, j, h):
        return copy_to(
            slab(2 * y_order[j] + h, c), wide.at[c, xh, j], wide_s.at[c, j, h], wide_r.at[c, j, xh],
            2 * y + h, flip,
        )

    def wide_prepare(c):
        loads[c].wait()
        for q in range(8):
            part[0, q, rows(c), :] = pair(q, c).astype(BF16)

    def wide_launch(c):
        for j in range(4):
            for h in range(2):
                wide_copy(c, j, h).start()

    def wide_sum(c, j):
        for h in range(2):
            pltpu.make_async_copy(wide.at[c, h, j], wide.at[c, h, j], wide_r.at[c, j, h]).wait()
        return wide[c, 0, j].astype(F32) + wide[c, 1, j].astype(F32)

    def half_copy(c, k, j, half, target, s_sem, r_sem):
        return copy_to(
            total.at[c, j, :, halves[half]], target.at[c, k], s_sem.at[c, k], r_sem.at[c, k],
            up if k == 0 else down, lat,
        )

    def relay2_copy(c, k):
        return half_copy(c, k, 0, k, relay2, relay2_s, relay2_r)

    def side2_copy(c, k):
        return half_copy(c, k, 1 + k, 1 - k, side2, side2_s, side2_r)

    def final2_copy(c, k):
        return half_copy(c, k, 1 + k, k, final2, final2_s, final2_r)

    def wide_relay(c):
        total[c, 0] = wide_sum(c, 0).astype(BF16)
        for k in range(2):
            relay2_copy(c, k).start()

    def wide_side(c):
        for k in range(2):
            total[c, 1 + k] = wide_sum(c, 1 + k).astype(BF16)
            side2_copy(c, k).start()

    def wide_final(c):
        for k in range(2):
            relay2_copy(c, k).wait_recv()
            both = wide[c, 0, 1 + k, :, halves[k]].astype(F32) + wide[c, 1, 1 + k, :, halves[k]].astype(F32)
            total[c, 1 + k, :, halves[k]] = (both + relay2[c, k].astype(F32)).astype(BF16)
            final2_copy(c, k).start()

    def wide_fold(c):
        mine = wide_sum(c, 3)
        for k in range(2):
            side2_copy(c, k).wait_recv()
            final2_copy(c, k).wait_recv()
        u = []
        for k in range(8):
            half, cols = k // 4, pl.ds(256 * (k % 4), 256)
            u.append(
                mine[:, 256 * k : 256 * k + 256]
                + final2[c, half, :, cols].astype(F32)
                + side2[c, 1 - half, :, cols].astype(F32)
            )
        keep(c, u)

    def first_copy(dest):
        return copy_to(send.at[dest], held.at[flip], first_s, first_r, shot, dest)

    def second_copy(dest):
        return copy_to(back.at[dest], got.at[lat], second_s, second_r, shot, dest)

    lane = lax.broadcasted_iota(jnp.int32, (1, 128), 1)
    low = lane < 64
    packed = (lax.broadcasted_iota(jnp.int32, (8, 128), 0) == 7) & (lat == 16)
    seventh = lax.broadcasted_iota(jnp.int32, (8, 128), 0) == 7

    partner = LAT - 1 - lat
    corner = jnp.where(lat == 0, 16, LAT - lat)

    def mirror_copy():
        return copy_to(
            mir_ids.at[:, pl.ds(0, 32), :], mir_in, wedge_s.at[0], wedge_r.at[0], shot, partner
        )

    def corner_copy(k):
        src = (own_ids if k == 0 else mir_ids).at[:, pl.ds(32, 16), :]
        return copy_to(src, spec_in.at[k], wedge_s.at[1 + k], wedge_r.at[1 + k], shot, corner)

    def wedges_out():
        for k in range(3):
            tables[k].wait()
        ids = wedge[...].astype(F32).astype(BF16)
        chosen = jnp.dot(pick[...], ids, preferred_element_type=F32).astype(BF16)
        own, mir = chosen[:48], chosen[48:]
        tall = jnp.concatenate([own[:, 128 * t : 128 * t + 128] for t in range(16)], axis=0)
        moved = jnp.dot(tall, lanet[0:128, :], preferred_element_type=F32)
        for t, tile in enumerate(spread([moved[48 * t : 48 * t + 48] for t in range(16)], lane)):
            own_ids[t] = tile.astype(BF16)
        tall = jnp.concatenate(
            [
                jnp.concatenate(
                    [mir[:, 128 * (15 - t) : 128 * (16 - t)],
                     mir[:, 128 * ((16 - t) % 16) : 128 * ((16 - t) % 16) + 128]],
                    axis=1,
                )
                for t in range(16)
            ],
            axis=0,
        )
        moved = jnp.dot(tall, lanet[128:384, :], preferred_element_type=F32)
        for t, tile in enumerate(spread([moved[48 * t : 48 * t + 48] for t in range(16)], lane)):
            mir_ids[t] = tile.astype(BF16)

    def wedges_go():
        mirror_copy().start()

        @pl.when(lat < 16)
        def _():
            for k in range(2):
                corner_copy(k).start()

    def look_up(ids):
        found = jnp.full(ids.shape, levels[0], F32)
        for w in range(1, 16):
            found = jnp.where(ids == float(w), levels[w], found)
        return found

    def wedges_in():
        mirror_copy().wait_recv()

        @pl.when(lat >= 16)
        def _():
            for k in range(2):
                corner_copy(k).wait_recv()

        @pl.loop(0, 16)
        def _(kk):
            own = own_ids[kk].astype(F32)
            mir = mir_ids[kk].astype(F32)
            got_mir = mir_in[kk].astype(F32)
            spec_own = spec_in[0, kk].astype(F32)
            spec_mir = spec_in[1, kk].astype(F32)
            level1[kk, 0:8, :] = look_up(jnp.where(seventh & (lat >= 16), own[32:40], own[0:8]))
            level1[kk, 8:32, :] = look_up(own[8:32])
            level1[kk, 32:40, :] = look_up(spec_own[0:8])
            row = jnp.where(lat == 16, mir[32:40], spec_mir[0:8])
            level2[kk, 0:8, :] = look_up(jnp.where(seventh & (lat >= 16), row, got_mir[0:8]))
            level2[kk, 8:32, :] = look_up(got_mir[8:32])
            level2[kk, 32:40, :] = look_up(spec_mir[0:8])

    def stack():
        wide_prepare(0)
        pl.semaphore_wait(barrier, len(bits) + 3)
        wide_launch(0)
        begin(2)
        meet(0)
        wide_prepare(1)
        wide_launch(1)
        meet(1)
        forward(2)
        wide_relay(0)
        begin(3)
        wide_side(0)
        meet(2)
        across(2)
        forward(3)
        meet(3)
        wide_final(0)
        wedges_out()
        meet(4)
        wide_relay(1)
        across(3)
        wide_fold(0)
        meet(5)
        wedges_go()
        wide_side(1)
        wide_final(1)
        fold(2)
        wedges_in()
        for k in range(3, 7):
            tables[k].wait()
        wide_fold(1)
        fold(3)

    def columns():
        pieces = [
            lax.dot_general(ft[:, 0:1024], folded0[...], NT, preferred_element_type=F32).reshape(LAT, 8, 128)
        ]
        for s in range(3):
            pieces.append(
                lax.dot_general(
                    ft[:, 1024 + 512 * s : 1536 + 512 * s], folded1[s], NT, preferred_element_type=F32
                ).reshape(LAT, 8, 128)
            )
        for k in range(2):
            both = jnp.concatenate([pieces[2 * k], pieces[2 * k + 1]], axis=1)
            send[:, 16 * k : 16 * k + 16, :] = both.astype(BF16)

        @pl.loop(1, LAT)
        def _(k):
            first_copy((lat + k) % LAT).start()

        held[flip] = send[lat]
        all_but_one = held.at[pl.ds(0, LAT - 1)]
        pltpu.make_async_copy(all_but_one, all_but_one, first_r).wait()

    def unpack():
        nothing = jnp.zeros((8, 128), F32)
        for p in range(16):
            u0, u1 = held[2 * p].astype(F32), held[2 * p + 1].astype(F32)
            re = jnp.where(low, u0, pltpu.roll(u1, 64, 1))
            im = jnp.where(low, pltpu.roll(u0, 64, 1), u1)
            xr[p, 0:32, :] = re
            xi[p, 0:8, :] = jnp.where(packed, 0.0, im[0:8])
            xi[p, 8:32, :] = im[8:32]
            xr[p, 32:40, :] = im[0:8]
            xi[p, 32:40, :] = nothing

    def lateral(sign):
        base = 0 if sign < 0 else 2

        @pl.loop(0, 5)
        def _(g):
            at = pl.ds(pl.multiple_of(8 * g, 8), 8)
            values = []
            for p in range(16):
                value = (xr[p, at, :], xi[p, at, :])
                if sign > 0:
                    cos, sin = tw[base, p : p + 1, :], tw[base + 1, p : p + 1, :]
                    value = (value[0] * cos - value[1] * sin, value[1] * cos + value[0] * sin)
                values.append(value)
            for p, value in enumerate(short_transform(values, sign)):
                if sign < 0:
                    cos, sin = tw[base, p : p + 1, :], tw[base + 1, p : p + 1, :]
                    value = (value[0] * cos - value[1] * sin, value[1] * cos + value[0] * sin)
                xr[p, at, :] = value[0]
                xi[p, at, :] = value[1]

    def middle():
        lateral(-1)
        for b in range(4):
            some = pl.ds(4 * b, 4)
            both = jnp.concatenate([xr[some].reshape(160, 128), xi[some].reshape(160, 128)], axis=1)
            spectrum = jnp.dot(both.astype(BF16), xt[0:256, :], preferred_element_type=F32)
            re, im = spectrum[:, :128], spectrum[:, 128:]
            inverse = lax.rsqrt(jnp.maximum(re * re + im * im, 1e-30))
            factor = jnp.maximum(1.0 - level1[some].reshape(160, 128) * inverse, 0.0)
            factor += jnp.maximum(1.0 - level2[some].reshape(160, 128) * inverse, 0.0)
            both = jnp.concatenate([re * factor, im * factor], axis=1)
            inner = jnp.dot(both.astype(BF16), xt[256:512, :], preferred_element_type=F32)
            xr[some] = inner[:, :128].reshape(4, 40, 128)
            xi[some] = inner[:, 128:].reshape(4, 40, 128)
        lateral(1)

    def turn_back():
        for p in range(16):
            re, im = xr[p, 0:32, :], xi[p, 0:32, :]
            im = jnp.concatenate([jnp.where(packed, xr[p, 32:40, :], im[0:8]), im[8:32]], axis=0)
            back[2 * p] = jnp.where(low, re, pltpu.roll(im, 64, 1)).astype(BF16)
            back[2 * p + 1] = jnp.where(low, pltpu.roll(re, 64, 1), im).astype(BF16)

        @pl.loop(1, LAT)
        def _(k):
            second_copy((lat + k) % LAT).start()

        got[lat] = back[lat]
        all_but_one = got.at[pl.ds(0, LAT - 1)]
        pltpu.make_async_copy(all_but_one, all_but_one, second_r).wait()

    def columns_back():
        for s in range(4):
            tall = got[:, 16 * (s // 2) : 16 * (s // 2) + 16, :].astype(F32)
            flat = tall[:, 8 * (s % 2) : 8 * (s % 2) + 8, :].reshape(256, 128).T.astype(BF16)
            wide = jnp.concatenate([flat[:64], flat[64:]], axis=1)
            mid[s] = jnp.dot(wide, it[512 * s : 512 * s + 512, :], preferred_element_type=F32)

        @pl.loop(0, 8)
        def _(g):
            at = pl.ds(pl.multiple_of(8 * g, 8), 8)
            parts = [(mid[s, at, 0:256], mid[s, at, 256:512]) for s in range(4)]
            even, odd = real_eight_back(parts[0][0], parts[0][1], parts[1], parts[2], parts[3])
            for k in range(4):
                out_even[0, at, 256 * k : 256 * k + 256] = even[k]
                out_odd[0, at, 256 * k : 256 * k + 256] = odd[k]

    def drain():
        for c in range(2, CHUNKS):
            for k in range(2):
                relay_copy(c, k).wait_send()
                side_copy(c, k).wait_send()
                final_copy(c, k).wait_send()
                cross_copy(c, k).wait_send()
        for c in range(2):
            for k in range(2):
                relay2_copy(c, k).wait_send()
                side2_copy(c, k).wait_send()
                final2_copy(c, k).wait_send()
                for j in range(4):
                    wide_copy(c, j, k).wait_send()
        sent = send.at[pl.ds(0, LAT - 1)]
        pltpu.make_async_copy(sent, sent, first_s).wait()
        sent = back.at[pl.ds(0, LAT - 1)]
        pltpu.make_async_copy(sent, sent, second_s).wait()
        mirror_copy().wait_send()

        @pl.when(lat < 16)
        def _():
            for k in range(2):
                corner_copy(k).wait_send()


    stack()
    columns()
    unpack()
    middle()
    turn_back()
    columns_back()
    drain()


def on_device(partials, wedges, levels):
    tables = [
        jnp.asarray(t)
        for t in (
            forward_tables(), inverse_tables(), lateral_tables(), turn_tables(), pick_tables(), lane_tables()
        )
    ]
    anywhere = pl.BlockSpec(memory_space=pltpu.HBM)
    vmem, dma = pltpu.VMEM, pltpu.SemaphoreType.DMA
    two = dma((CHUNKS, 2))
    even, odd = pl.pallas_call(
        kernel,
        out_shape=[jax.ShapeDtypeStruct((1, ROWS, N // 2), F32)] * 2,
        in_specs=[anywhere, anywhere, pl.BlockSpec(memory_space=pltpu.SMEM)] + [anywhere] * 6,
        out_specs=[pl.BlockSpec(memory_space=pltpu.VMEM)] * 2,
        scratch_shapes=[
            vmem(partials.shape, BF16),
            vmem(wedges.shape, jnp.int32),
            *[vmem(t.shape, t.dtype) for t in tables],
            vmem((CHUNKS, 2, CROWS, N), BF16),
            vmem((CHUNKS, 2, CROWS, N), BF16),
            vmem((CHUNKS, 2, CROWS, N), BF16),
            vmem((CHUNKS, 2, CROWS, N), BF16),
            vmem((2, 2, 4, CROWS, N), BF16),
            vmem((2, 4, CROWS, N), BF16),
            vmem((2, 2, CROWS, N // 2), BF16),
            vmem((2, 2, CROWS, N // 2), BF16),
            vmem((2, 2, CROWS, N // 2), BF16),
            vmem((128, 1024), BF16),
            vmem((3, 128, 512), BF16),
            vmem((LAT, 32, 128), BF16),
            vmem((LAT, 32, 128), BF16),
            vmem((16, 40, 128), F32),
            vmem((16, 40, 128), F32),
            vmem((16, 40, 128), F32),
            vmem((16, 40, 128), F32),
            vmem((16, 48, 128), BF16),
            vmem((16, 48, 128), BF16),
            vmem((16, 32, 128), BF16),
            vmem((2, 16, 16, 128), BF16),
            vmem((LAT, 32, 128), BF16),
            vmem((LAT, 32, 128), BF16),
            vmem((4, ROWS, 512), F32),
            dma((CHUNKS,)),
            dma((7,)),
            two, two, two, two, two, two, two, two,
            dma, dma, dma, dma,
            dma((3,)),
            dma((3,)),
            dma((2, 4, 2)), dma((2, 4, 2)),
            dma((2, 2)), dma((2, 2)), dma((2, 2)), dma((2, 2)), dma((2, 2)), dma((2, 2)),
            pltpu.SemaphoreType.REGULAR((5,)),
        ],
        compiler_params=pltpu.CompilerParams(
            collective_id=0, has_side_effects=True, vmem_limit_bytes=60 * 1024 * 1024
        ),
        name="stack_threshold",
    )(partials, wedges, levels, *tables)
    return jnp.concatenate([even + odd, even - odd], axis=-1)


def solution(mesh):
    in_specs = (P("shot", None, "lat", None), P("lat", None), P())
    return jax.shard_map(
        on_device, mesh=mesh, in_specs=in_specs, out_specs=P("shot", "lat", None), check_vma=False
    )
```

```python
import functools
import math

import jax
import jax.numpy as jnp
import ml_dtypes
import numpy as np
from jax import lax
from jax.experimental import pallas as pl
from jax.experimental.pallas import tpu as pltpu
from jax.sharding import PartitionSpec as P

MESH = pl.DeviceIdType.MESH
F32 = jnp.float32
BF16 = jnp.bfloat16
N = 2048
LAT = 32
ROWS = N // LAT
CHUNKS = 4
CROWS = ROWS // CHUNKS
HALF = math.sqrt(0.5)
NT = (((1,), (1,)), ((), ()))


def owned():
    ky = np.zeros((LAT, 32), np.int64)
    for d in range(LAT):
        for i in range(8):
            for s in (1, 2, 3):
                ky[d, 8 * s + i] = 64 * d + 8 * i + s
        for i in range(4):
            ky[d, i] = 64 * d + 8 * i + 4
        for i in range(4, 7):
            ky[d, i] = 64 * d + 8 * (i - 3)
        ky[d, 7] = 64 * d + (32 if d < 16 else 0)
    return ky


def forward_tables():
    ky = owned()
    y2 = np.arange(256)
    scale = 1.0 / math.sqrt(N)
    parts = []
    for s in range(4):
        rows = ky[:, 8 * s : 8 * s + 8].reshape(-1)
        angle = 2.0 * np.pi * ((rows[:, None] * y2[None, :]) % N) / N
        re, im = np.cos(angle), -np.sin(angle)
        if s == 0:
            packed = 16 * 8 + 7
            re[packed] = np.where(y2 % 2, -1.0, 1.0)
            im[packed] = 1.0
            four = (rows % 8 == 4)[:, None]
            zero = np.zeros_like(re)
            parts += [
                np.where(four, zero, re),
                np.where(four, re, zero),
                np.where(four, zero, im),
                np.where(four, im, zero),
            ]
        else:
            parts += [re, im]
    return (np.concatenate(parts, axis=1) * scale).astype(ml_dtypes.bfloat16)


def inverse_tables():
    ky = owned()
    y2 = np.arange(256)
    scale = 2.0 / math.sqrt(N)
    parts = []
    for s in range(4):
        rows = ky[:, 8 * s : 8 * s + 8].reshape(-1)
        angle = 2.0 * np.pi * ((rows[:, None] * y2[None, :]) % N) / N
        cos, sin = 2.0 * np.cos(angle), 2.0 * np.sin(angle)
        if s == 0:
            packed = 16 * 8 + 7
            cos[packed] = np.where(y2 % 2, -1.0, 1.0)
            sin[packed] = -1.0
            four = (rows % 8 == 4)[:, None]
            zero = np.zeros_like(cos)
            top = np.concatenate([np.where(four, zero, cos), np.where(four, cos, zero)], axis=1)
            low = np.concatenate([np.where(four, zero, -sin), np.where(four, -sin, zero)], axis=1)
        else:
            top = np.concatenate([cos, sin], axis=1)
            low = np.concatenate([-sin, cos], axis=1)
        parts += [top, low]
    return (np.concatenate(parts, axis=0) * scale).astype(ml_dtypes.bfloat16)


def lateral_tables():
    index = np.arange(128)
    angle = 2.0 * np.pi * ((index[:, None] * index[None, :]) % 128) / 128
    cos, sin = np.cos(angle), np.sin(angle)
    forward = np.block([[cos, -sin], [sin, cos]])
    inverse = np.block([[cos, sin], [-sin, cos]])
    return np.concatenate([forward, inverse], axis=0).astype(ml_dtypes.bfloat16)


def turn_tables():
    angle = 2.0 * np.pi * (np.arange(16)[:, None] * np.arange(128)[None, :]) / N
    scale = 1.0 / math.sqrt(N)
    cos, sin = np.cos(angle) * scale, np.sin(angle) * scale
    return np.stack([cos, -sin, 0.5 * cos, 0.5 * sin]).astype(np.float32)


def pick_tables():
    own = np.zeros((48, 64))
    mirror = np.zeros((48, 64))
    for i in range(8):
        for s in (1, 2, 3):
            own[8 * s + i, 8 * i + s] = 1
            mirror[8 * s + i, 8 * (7 - i) + 8 - s] = 1
    for i in range(4):
        own[i, 8 * i + 4] = 1
        mirror[i, 8 * (7 - i) + 4] = 1
    for i in range(4, 7):
        own[i, 8 * (i - 3)] = 1
        mirror[i, 8 * (11 - i)] = 1
    own[7, 32] = mirror[7, 32] = 1
    own[39, 0] = mirror[39, 0] = 1
    return np.concatenate([own, mirror], axis=0).astype(ml_dtypes.bfloat16)


def lane_tables():
    lanes = np.arange(128)
    place = (lanes % 16) * 8 + lanes // 16
    own = np.zeros((128, 128))
    own[lanes, place] = 1
    mirror = np.zeros((256, 128))
    mirror[128 - lanes, place] = 1
    return np.concatenate([own, mirror], axis=0).astype(ml_dtypes.bfloat16)


def turn(pair, step, length, sign):
    re, im = pair
    step = step % length
    if step == 0:
        return pair
    if 4 * step == length:
        return (-im, re) if sign > 0 else (im, -re)
    if 8 * step == length:
        return ((re - sign * im) * HALF, (im + sign * re) * HALF)
    if 8 * step == 3 * length:
        return ((-re - sign * im) * HALF, (-im + sign * re) * HALF)
    cos = math.cos(2.0 * math.pi * step / length)
    sin = sign * math.sin(2.0 * math.pi * step / length)
    return (re * cos - im * sin, im * cos + re * sin)


def short_transform(values, sign):
    count = len(values)
    if count == 1:
        return values
    even = short_transform(values[0::2], sign)
    odd = short_transform(values[1::2], sign)
    low, high = [], []
    for k in range(count // 2):
        re, im = turn(odd[k], k, count, sign)
        low.append((even[k][0] + re, even[k][1] + im))
        high.append((even[k][0] - re, even[k][1] - im))
    return low + high


def real_eight(u):
    a = [u[k] + u[k + 4] for k in range(4)]
    b = [u[k] - u[k + 4] for k in range(4)]
    even, odd = a[0] + a[2], a[1] + a[3]
    minus, plus = (b[1] - b[3]) * HALF, (b[1] + b[3]) * HALF
    return (
        even + odd,
        even - odd,
        (b[0] + minus, -(b[2] + plus)),
        (a[0] - a[2], a[3] - a[1]),
        (b[0] - minus, b[2] - plus),
    )


def real_eight_back(zero, four, one, two, three):
    plus, minus = zero + four, zero - four
    (r1, i1), (r2, i2), (r3, i3) = one, two, three
    p0, p1 = plus + r2, plus - r2
    m0, m1 = minus - i2, minus + i2
    e0, e1 = r1 + r3, i3 - i1
    o0 = (r1 - i1 - r3 - i3) * HALF
    o1 = (r3 - i3 - r1 - i1) * HALF
    return (p0, m0, p1, m1), (e0, o0, e1, o1)


def spread(tiles, lane):
    for bit in (8, 4, 2, 1):
        high = (lane // 8) % (2 * bit) >= bit
        new = list(tiles)
        for t in range(16):
            if t & bit:
                continue
            first, second = tiles[t], tiles[t | bit]
            new[t] = jnp.where(high, pltpu.roll(second, 8 * bit, 1), first)
            new[t | bit] = jnp.where(high, second, pltpu.roll(first, 128 - 8 * bit, 1))
        tiles = new
    return tiles


def kernel(
    part_hbm, wedge_hbm, levels, ft_hbm, it_hbm, xt_hbm, tw_hbm, pick_hbm, lane_hbm,
    out,
    part, wedge, ft, it, xt, tw, pick, lanet,
    relay, side, final, cross, wide, total, relay2, side2, final2,
    folded0, folded1, send, held, xr, xi, level1, level2, own_ids, mir_ids, mir_in, spec_in, back, got, mid,
    load_sem, table_sem, relay_s, relay_r, side_s, side_r, final_s, final_r, cross_s, cross_r,
    first_s, first_r, second_s, second_r, wedge_s, wedge_r,
    wide_s, wide_r, relay2_s, relay2_r, side2_s, side2_r, final2_s, final2_r,
):
    shot = lax.axis_index("shot")
    lat = lax.axis_index("lat")
    n_shot = lax.axis_size("shot")
    y, xh = shot // 2, shot % 2
    up, down = (shot + 2) % n_shot, (shot + n_shot - 2) % n_shot
    y_up, y_down, y_far = (y + 1) % 4, (y + 3) % 4, (y + 2) % 4
    flip = lat + 2 - 4 * ((lat // 2) % 2)
    other = shot + 1 - 2 * xh

    def rows(c):
        return pl.ds(c * CROWS, CROWS)

    loads = [
        pltpu.make_async_copy(
            part_hbm.at[:, :, rows(c), :], part.at[:, :, rows(c), :], load_sem.at[c]
        )
        for c in range(CHUNKS)
    ]
    loads[0].start()
    tables = [
        pltpu.make_async_copy(src, dst, table_sem.at[k])
        for k, (src, dst) in enumerate(
            [(wedge_hbm, wedge), (pick_hbm, pick), (lane_hbm, lanet), (ft_hbm, ft),
             (xt_hbm, xt), (tw_hbm, tw), (it_hbm, it)]
        )
    ]
    for c in (2, 1, 3):
        loads[c].start()
    for copy in tables:
        copy.start()

    barrier = pltpu.get_barrier_semaphore()

    def greet(s, l):
        pl.semaphore_signal(barrier, inc=1, device_id=(s, l), device_id_type=MESH)

    @pl.loop(1, LAT)
    def _(k):
        greet(shot, (lat + k) % LAT)

    greet(up, lat)
    greet(down, lat)
    greet(other, flip)

    def copy_to(src, dst, s_sem, r_sem, s, l):
        return pltpu.make_async_remote_copy(
            src_ref=src, dst_ref=dst, send_sem=s_sem, recv_sem=r_sem, device_id=(s, l), device_id_type=MESH
        )

    def slab(q, c):
        return part.at[0, q, rows(c), :]

    def relay_copy(c, k):
        q = 2 * y_far + k
        return copy_to(
            slab(q, c), relay.at[c, k], relay_s.at[c, k], relay_r.at[c, k], up if k == 0 else down, lat
        )

    def side_copy(c, k):
        q = 2 * y_up + 1 if k == 0 else 2 * y_down
        return copy_to(
            slab(q, c), side.at[c, k], side_s.at[c, k], side_r.at[c, k], up if k == 0 else down, lat
        )

    def final_copy(c, k):
        q = 2 * y_up if k == 0 else 2 * y_down + 1
        return copy_to(
            slab(q, c), final.at[c, k], final_s.at[c, k], final_r.at[c, k], up if k == 0 else down, lat
        )

    def cross_copy(c, h):
        return copy_to(
            slab(2 * y + h, c), cross.at[c, xh], cross_s.at[c, h], cross_r.at[c, xh], 2 * y + h, flip
        )

    def pair(q, c):
        return part[0, q, rows(c), :].astype(F32) + part[1, q, rows(c), :].astype(F32)

    def prepare(c):
        loads[c].wait()
        for q in (2 * y_far, 2 * y_far + 1, 2 * y_up + 1, 2 * y_down):
            part[0, q, rows(c), :] = pair(q, c).astype(BF16)

    def launch(c):
        for k in range(2):
            relay_copy(c, k).start()
        for k in range(2):
            side_copy(c, k).start()

    def begin(c):
        prepare(c)
        launch(c)

    def forward(c):
        for k in range(2):
            q = 2 * y_up if k == 0 else 2 * y_down + 1
            relay_copy(c, k).wait_recv()
            part[0, q, rows(c), :] = (pair(q, c) + relay[c, k].astype(F32)).astype(BF16)
            final_copy(c, k).start()

    def across(c):
        for k in range(2):
            side_copy(c, k).wait_recv()
            final_copy(c, k).wait_recv()
        for h in range(2):
            q = 2 * y + h
            total = pair(q, c) + final[c, h].astype(F32) + side[c, 1 - h].astype(F32)
            part[0, q, rows(c), :] = total.astype(BF16)
            cross_copy(c, h).start()

    def fold(c):
        for h in range(2):
            pltpu.make_async_copy(cross.at[c, h], cross.at[c, h], cross_r.at[c, h]).wait()
        u = []
        for k in range(8):
            cols = pl.ds(256 * k, 256)
            u.append(cross[c, 0, :, cols].astype(F32) + cross[c, 1, :, cols].astype(F32))
        keep(c, u)

    def keep(c, u):
        top, low = pl.ds(c * CROWS, CROWS), pl.ds(ROWS + c * CROWS, CROWS)
        zero, four, one, two, three = real_eight(u)
        zero, four = zero.astype(BF16), four.astype(BF16)
        blank = jnp.zeros((CROWS, 512), BF16)
        folded0[top, 0:256] = zero
        folded0[top, 256:512] = four
        folded0[top, 512:1024] = blank
        folded0[low, 0:512] = blank
        folded0[low, 512:768] = zero
        folded0[low, 768:1024] = four
        for s, (re, im) in enumerate((one, two, three)):
            re, im, neg = re.astype(BF16), im.astype(BF16), (-im).astype(BF16)
            folded1[s, top, 0:256] = re
            folded1[s, top, 256:512] = neg
            folded1[s, low, 0:256] = im
            folded1[s, low, 256:512] = re

    halves = (pl.ds(0, N // 2), pl.ds(N // 2, N // 2))
    y_order = (y_far, y_up, y_down, y)

    def wide_copy(c, j, h):
        return copy_to(
            slab(2 * y_order[j] + h, c), wide.at[c, xh, j], wide_s.at[c, j, h], wide_r.at[c, j, xh],
            2 * y + h, flip,
        )

    def wide_prepare(c):
        loads[c].wait()
        for q in range(8):
            part[0, q, rows(c), :] = pair(q, c).astype(BF16)

    def wide_launch(c):
        for j in range(4):
            for h in range(2):
                wide_copy(c, j, h).start()

    def wide_sum(c, j):
        for h in range(2):
            pltpu.make_async_copy(wide.at[c, h, j], wide.at[c, h, j], wide_r.at[c, j, h]).wait()
        return wide[c, 0, j].astype(F32) + wide[c, 1, j].astype(F32)

    def half_copy(c, k, j, half, target, s_sem, r_sem):
        return copy_to(
            total.at[c, j, :, halves[half]], target.at[c, k], s_sem.at[c, k], r_sem.at[c, k],
            up if k == 0 else down, lat,
        )

    def relay2_copy(c, k):
        return half_copy(c, k, 0, k, relay2, relay2_s, relay2_r)

    def side2_copy(c, k):
        return half_copy(c, k, 1 + k, 1 - k, side2, side2_s, side2_r)

    def final2_copy(c, k):
        return half_copy(c, k, 1 + k, k, final2, final2_s, final2_r)

    def wide_relay(c):
        total[c, 0] = wide_sum(c, 0).astype(BF16)
        for k in range(2):
            relay2_copy(c, k).start()

    def wide_side(c):
        for k in range(2):
            total[c, 1 + k] = wide_sum(c, 1 + k).astype(BF16)
            side2_copy(c, k).start()

    def wide_final(c):
        for k in range(2):
            relay2_copy(c, k).wait_recv()
            both = wide[c, 0, 1 + k, :, halves[k]].astype(F32) + wide[c, 1, 1 + k, :, halves[k]].astype(F32)
            total[c, 1 + k, :, halves[k]] = (both + relay2[c, k].astype(F32)).astype(BF16)
            final2_copy(c, k).start()

    def wide_fold(c):
        mine = wide_sum(c, 3)
        for k in range(2):
            side2_copy(c, k).wait_recv()
            final2_copy(c, k).wait_recv()
        u = []
        for k in range(8):
            half, cols = k // 4, pl.ds(256 * (k % 4), 256)
            u.append(
                mine[:, 256 * k : 256 * k + 256]
                + final2[c, half, :, cols].astype(F32)
                + side2[c, 1 - half, :, cols].astype(F32)
            )
        keep(c, u)

    def first_copy(dest):
        return copy_to(send.at[dest], held.at[flip], first_s, first_r, shot, dest)

    def second_copy(dest):
        return copy_to(back.at[dest], got.at[lat], second_s, second_r, shot, dest)

    lane = lax.broadcasted_iota(jnp.int32, (1, 128), 1)
    low = lane < 64
    packed = (lax.broadcasted_iota(jnp.int32, (8, 128), 0) == 7) & (lat == 16)
    seventh = lax.broadcasted_iota(jnp.int32, (8, 128), 0) == 7

    partner = LAT - 1 - lat
    corner = jnp.where(lat == 0, 16, LAT - lat)

    def mirror_copy():
        return copy_to(
            mir_ids.at[:, pl.ds(0, 32), :], mir_in, wedge_s.at[0], wedge_r.at[0], shot, partner
        )

    def corner_copy(k):
        src = (own_ids if k == 0 else mir_ids).at[:, pl.ds(32, 16), :]
        return copy_to(src, spec_in.at[k], wedge_s.at[1 + k], wedge_r.at[1 + k], shot, corner)

    def wedges_out():
        for k in range(3):
            tables[k].wait()
        ids = wedge[...].astype(F32).astype(BF16)
        chosen = jnp.dot(pick[...], ids, preferred_element_type=F32).astype(BF16)
        own, mir = chosen[:48], chosen[48:]
        tall = jnp.concatenate([own[:, 128 * t : 128 * t + 128] for t in range(16)], axis=0)
        moved = jnp.dot(tall, lanet[0:128, :], preferred_element_type=F32)
        for t, tile in enumerate(spread([moved[48 * t : 48 * t + 48] for t in range(16)], lane)):
            own_ids[t] = tile.astype(BF16)
        tall = jnp.concatenate(
            [
                jnp.concatenate(
                    [mir[:, 128 * (15 - t) : 128 * (16 - t)],
                     mir[:, 128 * ((16 - t) % 16) : 128 * ((16 - t) % 16) + 128]],
                    axis=1,
                )
                for t in range(16)
            ],
            axis=0,
        )
        moved = jnp.dot(tall, lanet[128:384, :], preferred_element_type=F32)
        for t, tile in enumerate(spread([moved[48 * t : 48 * t + 48] for t in range(16)], lane)):
            mir_ids[t] = tile.astype(BF16)

    def wedges_go():
        mirror_copy().start()

        @pl.when(lat < 16)
        def _():
            for k in range(2):
                corner_copy(k).start()

    def look_up(ids):
        found = jnp.full(ids.shape, levels[0], F32)
        for w in range(1, 16):
            found = jnp.where(ids == float(w), levels[w], found)
        return found

    def wedges_in():
        mirror_copy().wait_recv()

        @pl.when(lat >= 16)
        def _():
            for k in range(2):
                corner_copy(k).wait_recv()

        @pl.loop(0, 16)
        def _(kk):
            own = own_ids[kk].astype(F32)
            mir = mir_ids[kk].astype(F32)
            got_mir = mir_in[kk].astype(F32)
            spec_own = spec_in[0, kk].astype(F32)
            spec_mir = spec_in[1, kk].astype(F32)
            level1[kk, 0:8, :] = look_up(jnp.where(seventh & (lat >= 16), own[32:40], own[0:8]))
            level1[kk, 8:32, :] = look_up(own[8:32])
            level1[kk, 32:40, :] = look_up(spec_own[0:8])
            row = jnp.where(lat == 16, mir[32:40], spec_mir[0:8])
            level2[kk, 0:8, :] = look_up(jnp.where(seventh & (lat >= 16), row, got_mir[0:8]))
            level2[kk, 8:32, :] = look_up(got_mir[8:32])
            level2[kk, 32:40, :] = look_up(spec_mir[0:8])

    def stack():
        wide_prepare(0)
        pl.semaphore_wait(barrier, LAT + 2)
        wide_launch(0)
        begin(2)
        wide_prepare(1)
        wide_launch(1)
        begin(3)
        wedges_out()
        wedges_go()
        forward(2)
        forward(3)
        wide_relay(0)
        wide_side(0)
        across(2)
        across(3)
        wide_final(0)
        wide_relay(1)
        wide_side(1)
        wide_final(1)
        wide_fold(0)
        wedges_in()
        for k in range(3, 7):
            tables[k].wait()
        wide_fold(1)
        fold(2)
        fold(3)

    def columns():
        pieces = [
            lax.dot_general(ft[:, 0:1024], folded0[...], NT, preferred_element_type=F32).reshape(LAT, 8, 128)
        ]
        for s in range(3):
            pieces.append(
                lax.dot_general(
                    ft[:, 1024 + 512 * s : 1536 + 512 * s], folded1[s], NT, preferred_element_type=F32
                ).reshape(LAT, 8, 128)
            )
        for k in range(2):
            both = jnp.concatenate([pieces[2 * k], pieces[2 * k + 1]], axis=1)
            send[:, 16 * k : 16 * k + 16, :] = both.astype(BF16)

        @pl.loop(1, LAT)
        def _(k):
            first_copy((lat + k) % LAT).start()

        held[flip] = send[lat]
        all_but_one = held.at[pl.ds(0, LAT - 1)]
        pltpu.make_async_copy(all_but_one, all_but_one, first_r).wait()

    def unpack():
        nothing = jnp.zeros((8, 128), F32)
        for p in range(16):
            u0, u1 = held[2 * p].astype(F32), held[2 * p + 1].astype(F32)
            re = jnp.where(low, u0, pltpu.roll(u1, 64, 1))
            im = jnp.where(low, pltpu.roll(u0, 64, 1), u1)
            xr[p, 0:32, :] = re
            xi[p, 0:8, :] = jnp.where(packed, 0.0, im[0:8])
            xi[p, 8:32, :] = im[8:32]
            xr[p, 32:40, :] = im[0:8]
            xi[p, 32:40, :] = nothing

    def lateral(sign):
        base = 0 if sign < 0 else 2

        @pl.loop(0, 5)
        def _(g):
            at = pl.ds(pl.multiple_of(8 * g, 8), 8)
            values = []
            for p in range(16):
                value = (xr[p, at, :], xi[p, at, :])
                if sign > 0:
                    cos, sin = tw[base, p : p + 1, :], tw[base + 1, p : p + 1, :]
                    value = (value[0] * cos - value[1] * sin, value[1] * cos + value[0] * sin)
                values.append(value)
            for p, value in enumerate(short_transform(values, sign)):
                if sign < 0:
                    cos, sin = tw[base, p : p + 1, :], tw[base + 1, p : p + 1, :]
                    value = (value[0] * cos - value[1] * sin, value[1] * cos + value[0] * sin)
                xr[p, at, :] = value[0]
                xi[p, at, :] = value[1]

    def middle():
        lateral(-1)
        for b in range(4):
            some = pl.ds(4 * b, 4)
            both = jnp.concatenate([xr[some].reshape(160, 128), xi[some].reshape(160, 128)], axis=1)
            spectrum = jnp.dot(both.astype(BF16), xt[0:256, :], preferred_element_type=F32)
            re, im = spectrum[:, :128], spectrum[:, 128:]
            inverse = lax.rsqrt(jnp.maximum(re * re + im * im, 1e-30))
            factor = jnp.maximum(1.0 - level1[some].reshape(160, 128) * inverse, 0.0)
            factor += jnp.maximum(1.0 - level2[some].reshape(160, 128) * inverse, 0.0)
            both = jnp.concatenate([re * factor, im * factor], axis=1)
            inner = jnp.dot(both.astype(BF16), xt[256:512, :], preferred_element_type=F32)
            xr[some] = inner[:, :128].reshape(4, 40, 128)
            xi[some] = inner[:, 128:].reshape(4, 40, 128)
        lateral(1)

    def turn_back():
        for p in range(16):
            re, im = xr[p, 0:32, :], xi[p, 0:32, :]
            im = jnp.concatenate([jnp.where(packed, xr[p, 32:40, :], im[0:8]), im[8:32]], axis=0)
            back[2 * p] = jnp.where(low, re, pltpu.roll(im, 64, 1)).astype(BF16)
            back[2 * p + 1] = jnp.where(low, pltpu.roll(re, 64, 1), im).astype(BF16)

        @pl.loop(1, LAT)
        def _(k):
            second_copy((lat + k) % LAT).start()

        got[lat] = back[lat]
        all_but_one = got.at[pl.ds(0, LAT - 1)]
        pltpu.make_async_copy(all_but_one, all_but_one, second_r).wait()

    def columns_back():
        for s in range(4):
            tall = got[:, 16 * (s // 2) : 16 * (s // 2) + 16, :].astype(F32)
            flat = tall[:, 8 * (s % 2) : 8 * (s % 2) + 8, :].reshape(256, 128).T.astype(BF16)
            wide = jnp.concatenate([flat[:64], flat[64:]], axis=1)
            mid[s] = jnp.dot(wide, it[512 * s : 512 * s + 512, :], preferred_element_type=F32)

        @pl.loop(0, 8)
        def _(g):
            at = pl.ds(pl.multiple_of(8 * g, 8), 8)
            parts = [(mid[s, at, 0:256], mid[s, at, 256:512]) for s in range(4)]
            even, odd = real_eight_back(parts[0][0], parts[0][1], parts[1], parts[2], parts[3])
            for k in range(4):
                out[0, at, 256 * k : 256 * k + 256] = even[k] + odd[k]
                out[0, at, 1024 + 256 * k : 1280 + 256 * k] = even[k] - odd[k]

    def drain():
        for c in range(2, CHUNKS):
            for k in range(2):
                relay_copy(c, k).wait_send()
                side_copy(c, k).wait_send()
                final_copy(c, k).wait_send()
                cross_copy(c, k).wait_send()
        for c in range(2):
            for k in range(2):
                relay2_copy(c, k).wait_send()
                side2_copy(c, k).wait_send()
                final2_copy(c, k).wait_send()
                for j in range(4):
                    wide_copy(c, j, k).wait_send()
        sent = send.at[pl.ds(0, LAT - 1)]
        pltpu.make_async_copy(sent, sent, first_s).wait()
        sent = back.at[pl.ds(0, LAT - 1)]
        pltpu.make_async_copy(sent, sent, second_s).wait()
        mirror_copy().wait_send()

        @pl.when(lat < 16)
        def _():
            for k in range(2):
                corner_copy(k).wait_send()


    stack()
    columns()
    unpack()
    middle()
    turn_back()
    columns_back()
    drain()


def on_device(partials, wedges, levels):
    tables = [
        jnp.asarray(t)
        for t in (
            forward_tables(), inverse_tables(), lateral_tables(), turn_tables(), pick_tables(), lane_tables()
        )
    ]
    anywhere = pl.BlockSpec(memory_space=pltpu.HBM)
    vmem, dma = pltpu.VMEM, pltpu.SemaphoreType.DMA
    two = dma((CHUNKS, 2))
    doubled = pl.pallas_call(
        kernel,
        out_shape=jax.ShapeDtypeStruct((1, ROWS, N), F32),
        in_specs=[anywhere, anywhere, pl.BlockSpec(memory_space=pltpu.SMEM)] + [anywhere] * 6,
        out_specs=pl.BlockSpec(memory_space=pltpu.VMEM),
        scratch_shapes=[
            vmem(partials.shape, BF16),
            vmem(wedges.shape, jnp.int32),
            *[vmem(t.shape, t.dtype) for t in tables],
            vmem((CHUNKS, 2, CROWS, N), BF16),
            vmem((CHUNKS, 2, CROWS, N), BF16),
            vmem((CHUNKS, 2, CROWS, N), BF16),
            vmem((CHUNKS, 2, CROWS, N), BF16),
            vmem((2, 2, 4, CROWS, N), BF16),
            vmem((2, 4, CROWS, N), BF16),
            vmem((2, 2, CROWS, N // 2), BF16),
            vmem((2, 2, CROWS, N // 2), BF16),
            vmem((2, 2, CROWS, N // 2), BF16),
            vmem((128, 1024), BF16),
            vmem((3, 128, 512), BF16),
            vmem((LAT, 32, 128), BF16),
            vmem((LAT, 32, 128), BF16),
            vmem((16, 40, 128), F32),
            vmem((16, 40, 128), F32),
            vmem((16, 40, 128), F32),
            vmem((16, 40, 128), F32),
            vmem((16, 48, 128), BF16),
            vmem((16, 48, 128), BF16),
            vmem((16, 32, 128), BF16),
            vmem((2, 16, 16, 128), BF16),
            vmem((LAT, 32, 128), BF16),
            vmem((LAT, 32, 128), BF16),
            vmem((4, ROWS, 512), F32),
            dma((CHUNKS,)),
            dma((7,)),
            two, two, two, two, two, two, two, two,
            dma, dma, dma, dma,
            dma((3,)),
            dma((3,)),
            dma((2, 4, 2)), dma((2, 4, 2)),
            dma((2, 2)), dma((2, 2)), dma((2, 2)), dma((2, 2)), dma((2, 2)), dma((2, 2)),
        ],
        compiler_params=pltpu.CompilerParams(
            collective_id=0, has_side_effects=True, vmem_limit_bytes=60 * 1024 * 1024
        ),
        name="stack_threshold",
    )(partials, wedges, levels, *tables)
    return doubled * 0.5


def solution(mesh):
    in_specs = (P("shot", None, "lat", None), P("lat", None), P())
    return jax.shard_map(
        on_device, mesh=mesh, in_specs=in_specs, out_specs=P("shot", "lat", None), check_vma=False
    )
```

```python
import functools
import math

import jax
import jax.numpy as jnp
import ml_dtypes
import numpy as np
from jax import lax
from jax.experimental import pallas as pl
from jax.experimental.pallas import tpu as pltpu
from jax.sharding import PartitionSpec as P

MESH = pl.DeviceIdType.MESH
F32 = jnp.float32
BF16 = jnp.bfloat16
N = 2048
LAT = 32
ROWS = N // LAT
CHUNKS = 4
CROWS = ROWS // CHUNKS
HALF = math.sqrt(0.5)
NT = (((1,), (1,)), ((), ()))


def owned():
    ky = np.zeros((LAT, 32), np.int64)
    for d in range(LAT):
        for i in range(8):
            for s in (1, 2, 3):
                ky[d, 8 * s + i] = 64 * d + 8 * i + s
        for i in range(4):
            ky[d, i] = 64 * d + 8 * i + 4
        for i in range(4, 7):
            ky[d, i] = 64 * d + 8 * (i - 3)
        ky[d, 7] = 64 * d + (32 if d < 16 else 0)
    return ky


def forward_tables():
    ky = owned()
    y2 = np.arange(256)
    scale = 1.0 / math.sqrt(N)
    parts = []
    for s in range(4):
        rows = ky[:, 8 * s : 8 * s + 8].reshape(-1)
        angle = 2.0 * np.pi * ((rows[:, None] * y2[None, :]) % N) / N
        re, im = np.cos(angle), -np.sin(angle)
        if s == 0:
            packed = 16 * 8 + 7
            re[packed] = np.where(y2 % 2, -1.0, 1.0)
            im[packed] = 1.0
            four = (rows % 8 == 4)[:, None]
            zero = np.zeros_like(re)
            parts += [
                np.where(four, zero, re),
                np.where(four, re, zero),
                np.where(four, zero, im),
                np.where(four, im, zero),
            ]
        else:
            parts += [re, im]
    return (np.concatenate(parts, axis=1) * scale).astype(ml_dtypes.bfloat16)


def inverse_tables():
    ky = owned()
    y2 = np.arange(256)
    scale = 2.0 / math.sqrt(N)
    parts = []
    for s in range(4):
        rows = ky[:, 8 * s : 8 * s + 8].reshape(-1)
        angle = 2.0 * np.pi * ((rows[:, None] * y2[None, :]) % N) / N
        cos, sin = 2.0 * np.cos(angle), 2.0 * np.sin(angle)
        if s == 0:
            packed = 16 * 8 + 7
            cos[packed] = np.where(y2 % 2, -1.0, 1.0)
            sin[packed] = -1.0
            four = (rows % 8 == 4)[:, None]
            zero = np.zeros_like(cos)
            top = np.concatenate([np.where(four, zero, cos), np.where(four, cos, zero)], axis=1)
            low = np.concatenate([np.where(four, zero, -sin), np.where(four, -sin, zero)], axis=1)
        else:
            top = np.concatenate([cos, sin], axis=1)
            low = np.concatenate([-sin, cos], axis=1)
        parts += [top, low]
    return (np.concatenate(parts, axis=0) * scale).astype(ml_dtypes.bfloat16)


def lateral_tables():
    index = np.arange(128)
    angle = 2.0 * np.pi * ((index[:, None] * index[None, :]) % 128) / 128
    cos, sin = np.cos(angle), np.sin(angle)
    forward = np.block([[cos, -sin], [sin, cos]])
    inverse = np.block([[cos, sin], [-sin, cos]])
    return np.concatenate([forward, inverse], axis=0).astype(ml_dtypes.bfloat16)


def turn_tables():
    angle = 2.0 * np.pi * (np.arange(16)[:, None] * np.arange(128)[None, :]) / N
    scale = 1.0 / math.sqrt(N)
    cos, sin = np.cos(angle) * scale, np.sin(angle) * scale
    return np.stack([cos, -sin, 0.5 * cos, 0.5 * sin]).astype(np.float32)


def pick_tables():
    own = np.zeros((48, 64))
    mirror = np.zeros((48, 64))
    for i in range(8):
        for s in (1, 2, 3):
            own[8 * s + i, 8 * i + s] = 1
            mirror[8 * s + i, 8 * (7 - i) + 8 - s] = 1
    for i in range(4):
        own[i, 8 * i + 4] = 1
        mirror[i, 8 * (7 - i) + 4] = 1
    for i in range(4, 7):
        own[i, 8 * (i - 3)] = 1
        mirror[i, 8 * (11 - i)] = 1
    own[7, 32] = mirror[7, 32] = 1
    own[39, 0] = mirror[39, 0] = 1
    return np.concatenate([own, mirror], axis=0).astype(ml_dtypes.bfloat16)


def lane_tables():
    lanes = np.arange(128)
    place = (lanes % 16) * 8 + lanes // 16
    own = np.zeros((128, 128))
    own[lanes, place] = 1
    mirror = np.zeros((256, 128))
    mirror[128 - lanes, place] = 1
    return np.concatenate([own, mirror], axis=0).astype(ml_dtypes.bfloat16)


def turn(pair, step, length, sign):
    re, im = pair
    step = step % length
    if step == 0:
        return pair
    if 4 * step == length:
        return (-im, re) if sign > 0 else (im, -re)
    if 8 * step == length:
        return ((re - sign * im) * HALF, (im + sign * re) * HALF)
    if 8 * step == 3 * length:
        return ((-re - sign * im) * HALF, (-im + sign * re) * HALF)
    cos = math.cos(2.0 * math.pi * step / length)
    sin = sign * math.sin(2.0 * math.pi * step / length)
    return (re * cos - im * sin, im * cos + re * sin)


def short_transform(values, sign):
    count = len(values)
    if count == 1:
        return values
    even = short_transform(values[0::2], sign)
    odd = short_transform(values[1::2], sign)
    low, high = [], []
    for k in range(count // 2):
        re, im = turn(odd[k], k, count, sign)
        low.append((even[k][0] + re, even[k][1] + im))
        high.append((even[k][0] - re, even[k][1] - im))
    return low + high


def real_eight(u):
    a = [u[k] + u[k + 4] for k in range(4)]
    b = [u[k] - u[k + 4] for k in range(4)]
    even, odd = a[0] + a[2], a[1] + a[3]
    minus, plus = (b[1] - b[3]) * HALF, (b[1] + b[3]) * HALF
    return (
        even + odd,
        even - odd,
        (b[0] + minus, -(b[2] + plus)),
        (a[0] - a[2], a[3] - a[1]),
        (b[0] - minus, b[2] - plus),
    )


def real_eight_back(zero, four, one, two, three):
    plus, minus = zero + four, zero - four
    (r1, i1), (r2, i2), (r3, i3) = one, two, three
    p0, p1 = plus + r2, plus - r2
    m0, m1 = minus - i2, minus + i2
    e0, e1 = r1 + r3, i3 - i1
    o0 = (r1 - i1 - r3 - i3) * HALF
    o1 = (r3 - i3 - r1 - i1) * HALF
    return (p0, m0, p1, m1), (e0, o0, e1, o1)


def spread(tiles, lane):
    for bit in (8, 4, 2, 1):
        high = (lane // 8) % (2 * bit) >= bit
        new = list(tiles)
        for t in range(16):
            if t & bit:
                continue
            first, second = tiles[t], tiles[t | bit]
            new[t] = jnp.where(high, pltpu.roll(second, 8 * bit, 1), first)
            new[t | bit] = jnp.where(high, second, pltpu.roll(first, 128 - 8 * bit, 1))
        tiles = new
    return tiles


def kernel(
    part_hbm, wedge_hbm, levels, ft_hbm, it_hbm, xt_hbm, tw_hbm, pick_hbm, lane_hbm,
    out,
    part, wedge, ft, it, xt, tw, pick, lanet,
    relay, side, final, cross, wide, total, relay2, side2, final2,
    folded0, folded1, send, held, xr, xi, level1, level2, own_ids, mir_ids, mir_in, spec_in, back, got, mid,
    load_sem, table_sem, relay_s, relay_r, side_s, side_r, final_s, final_r, cross_s, cross_r,
    first_s, first_r, second_s, second_r, wedge_s, wedge_r,
    wide_s, wide_r, relay2_s, relay2_r, side2_s, side2_r, final2_s, final2_r,
):
    shot = lax.axis_index("shot")
    lat = lax.axis_index("lat")
    n_shot = lax.axis_size("shot")
    y, xh = shot // 2, shot % 2
    up, down = (shot + 2) % n_shot, (shot + n_shot - 2) % n_shot
    y_up, y_down, y_far = (y + 1) % 4, (y + 3) % 4, (y + 2) % 4
    flip = lat + 2 - 4 * ((lat // 2) % 2)
    other = shot + 1 - 2 * xh

    def rows(c):
        return pl.ds(c * CROWS, CROWS)

    loads = [
        pltpu.make_async_copy(
            part_hbm.at[:, :, rows(c), :], part.at[:, :, rows(c), :], load_sem.at[c]
        )
        for c in range(CHUNKS)
    ]
    loads[0].start()
    tables = [
        pltpu.make_async_copy(src, dst, table_sem.at[k])
        for k, (src, dst) in enumerate(
            [(wedge_hbm, wedge), (pick_hbm, pick), (lane_hbm, lanet), (ft_hbm, ft),
             (xt_hbm, xt), (tw_hbm, tw), (it_hbm, it)]
        )
    ]
    for c in (2, 1, 3):
        loads[c].start()
    for copy in tables:
        copy.start()

    barrier = pltpu.get_barrier_semaphore()

    def greet(s, l):
        pl.semaphore_signal(barrier, inc=1, device_id=(s, l), device_id_type=MESH)

    greet(up, lat)
    greet(down, lat)
    greet(other, flip)
    greet(other, LAT - 1 - lat)

    @pl.loop(1, LAT)
    def _(k):
        greet(shot, (lat + k) % LAT)

    def copy_to(src, dst, s_sem, r_sem, s, l):
        return pltpu.make_async_remote_copy(
            src_ref=src, dst_ref=dst, send_sem=s_sem, recv_sem=r_sem, device_id=(s, l), device_id_type=MESH
        )

    def slab(q, c):
        return part.at[0, q, rows(c), :]

    def relay_copy(c, k):
        q = 2 * y_far + k
        return copy_to(
            slab(q, c), relay.at[c, k], relay_s.at[c, k], relay_r.at[c, k], up if k == 0 else down, lat
        )

    def side_copy(c, k):
        q = 2 * y_up + 1 if k == 0 else 2 * y_down
        return copy_to(
            slab(q, c), side.at[c, k], side_s.at[c, k], side_r.at[c, k], up if k == 0 else down, lat
        )

    def final_copy(c, k):
        q = 2 * y_up if k == 0 else 2 * y_down + 1
        return copy_to(
            slab(q, c), final.at[c, k], final_s.at[c, k], final_r.at[c, k], up if k == 0 else down, lat
        )

    def cross_copy(c, h):
        return copy_to(
            slab(2 * y + h, c), cross.at[c, xh], cross_s.at[c, h], cross_r.at[c, xh], 2 * y + h, flip
        )

    def pair(q, c):
        return part[0, q, rows(c), :].astype(F32) + part[1, q, rows(c), :].astype(F32)

    def prepare(c):
        loads[c].wait()
        for q in (2 * y_far, 2 * y_far + 1, 2 * y_up + 1, 2 * y_down):
            part[0, q, rows(c), :] = pair(q, c).astype(BF16)

    def launch(c):
        for k in range(2):
            relay_copy(c, k).start()
        for k in range(2):
            side_copy(c, k).start()

    def begin(c):
        prepare(c)
        launch(c)

    def forward(c):
        for k in range(2):
            q = 2 * y_up if k == 0 else 2 * y_down + 1
            relay_copy(c, k).wait_recv()
            part[0, q, rows(c), :] = (pair(q, c) + relay[c, k].astype(F32)).astype(BF16)
            final_copy(c, k).start()

    def across(c):
        for k in range(2):
            side_copy(c, k).wait_recv()
            final_copy(c, k).wait_recv()
        for h in range(2):
            q = 2 * y + h
            total = pair(q, c) + final[c, h].astype(F32) + side[c, 1 - h].astype(F32)
            part[0, q, rows(c), :] = total.astype(BF16)
            cross_copy(c, h).start()

    def fold(c):
        for h in range(2):
            pltpu.make_async_copy(cross.at[c, h], cross.at[c, h], cross_r.at[c, h]).wait()
        u = []
        for k in range(8):
            cols = pl.ds(256 * k, 256)
            u.append(cross[c, 0, :, cols].astype(F32) + cross[c, 1, :, cols].astype(F32))
        keep(c, u)

    def keep(c, u):
        top, low = pl.ds(c * CROWS, CROWS), pl.ds(ROWS + c * CROWS, CROWS)
        zero, four, one, two, three = real_eight(u)
        zero, four = zero.astype(BF16), four.astype(BF16)
        blank = jnp.zeros((CROWS, 512), BF16)
        folded0[top, 0:256] = zero
        folded0[top, 256:512] = four
        folded0[top, 512:1024] = blank
        folded0[low, 0:512] = blank
        folded0[low, 512:768] = zero
        folded0[low, 768:1024] = four
        for s, (re, im) in enumerate((one, two, three)):
            re, im, neg = re.astype(BF16), im.astype(BF16), (-im).astype(BF16)
            folded1[s, top, 0:256] = re
            folded1[s, top, 256:512] = neg
            folded1[s, low, 0:256] = im
            folded1[s, low, 256:512] = re

    halves = (pl.ds(0, N // 2), pl.ds(N // 2, N // 2))
    y_order = (y_far, y_up, y_down, y)

    def wide_copy(c, j, h):
        return copy_to(
            slab(2 * y_order[j] + h, c), wide.at[c, xh, j], wide_s.at[c, j, h], wide_r.at[c, j, xh],
            2 * y + h, flip,
        )

    def wide_prepare(c):
        loads[c].wait()
        for q in range(8):
            part[0, q, rows(c), :] = pair(q, c).astype(BF16)

    def wide_launch(c):
        for j in range(4):
            for h in range(2):
                wide_copy(c, j, h).start()

    def wide_sum(c, j):
        for h in range(2):
            pltpu.make_async_copy(wide.at[c, h, j], wide.at[c, h, j], wide_r.at[c, j, h]).wait()
        return wide[c, 0, j].astype(F32) + wide[c, 1, j].astype(F32)

    def half_copy(c, k, j, half, target, s_sem, r_sem):
        return copy_to(
            total.at[c, j, :, halves[half]], target.at[c, k], s_sem.at[c, k], r_sem.at[c, k],
            up if k == 0 else down, lat,
        )

    def relay2_copy(c, k):
        return half_copy(c, k, 0, k, relay2, relay2_s, relay2_r)

    def side2_copy(c, k):
        return half_copy(c, k, 1 + k, 1 - k, side2, side2_s, side2_r)

    def final2_copy(c, k):
        return half_copy(c, k, 1 + k, k, final2, final2_s, final2_r)

    def wide_relay(c):
        total[c, 0] = wide_sum(c, 0).astype(BF16)
        for k in range(2):
            relay2_copy(c, k).start()

    def wide_side(c):
        for k in range(2):
            total[c, 1 + k] = wide_sum(c, 1 + k).astype(BF16)
            side2_copy(c, k).start()

    def wide_final(c):
        for k in range(2):
            relay2_copy(c, k).wait_recv()
            both = wide[c, 0, 1 + k, :, halves[k]].astype(F32) + wide[c, 1, 1 + k, :, halves[k]].astype(F32)
            total[c, 1 + k, :, halves[k]] = (both + relay2[c, k].astype(F32)).astype(BF16)
            final2_copy(c, k).start()

    def wide_fold(c):
        mine = wide_sum(c, 3)
        for k in range(2):
            side2_copy(c, k).wait_recv()
            final2_copy(c, k).wait_recv()
        u = []
        for k in range(8):
            half, cols = k // 4, pl.ds(256 * (k % 4), 256)
            u.append(
                mine[:, 256 * k : 256 * k + 256]
                + final2[c, half, :, cols].astype(F32)
                + side2[c, 1 - half, :, cols].astype(F32)
            )
        keep(c, u)

    def first_copy(dest):
        return copy_to(send.at[dest], held.at[flip], first_s, first_r, shot, dest)

    def second_copy(dest):
        return copy_to(back.at[dest], got.at[lat], second_s, second_r, shot, dest)

    lane = lax.broadcasted_iota(jnp.int32, (1, 128), 1)
    low = lane < 64
    packed = (lax.broadcasted_iota(jnp.int32, (8, 128), 0) == 7) & (lat == 16)
    seventh = lax.broadcasted_iota(jnp.int32, (8, 128), 0) == 7

    partner = LAT - 1 - lat
    corner = jnp.where(lat == 0, 16, LAT - lat)

    def mirror_copy(k):
        some = pl.ds(8 * k, 8)
        return copy_to(
            mir_ids.at[some, pl.ds(0, 32), :], mir_in.at[some], wedge_s.at[2 + k], wedge_r.at[2 + k],
            shot if k == 0 else other, partner,
        )

    def corner_copy(k):
        src = (own_ids if k == 0 else mir_ids).at[:, pl.ds(32, 16), :]
        return copy_to(src, spec_in.at[k], wedge_s.at[k], wedge_r.at[k], shot, corner)

    def wedges_out():
        for k in range(3):
            tables[k].wait()
        ids = wedge[...].astype(F32).astype(BF16)
        chosen = jnp.dot(pick[...], ids, preferred_element_type=F32).astype(BF16)
        own, mir = chosen[:48], chosen[48:]
        tall = jnp.concatenate([own[:, 128 * t : 128 * t + 128] for t in range(16)], axis=0)
        moved = jnp.dot(tall, lanet[0:128, :], preferred_element_type=F32)
        for t, tile in enumerate(spread([moved[48 * t : 48 * t + 48] for t in range(16)], lane)):
            own_ids[t] = tile.astype(BF16)
        tall = jnp.concatenate(
            [
                jnp.concatenate(
                    [mir[:, 128 * (15 - t) : 128 * (16 - t)],
                     mir[:, 128 * ((16 - t) % 16) : 128 * ((16 - t) % 16) + 128]],
                    axis=1,
                )
                for t in range(16)
            ],
            axis=0,
        )
        moved = jnp.dot(tall, lanet[128:384, :], preferred_element_type=F32)
        for t, tile in enumerate(spread([moved[48 * t : 48 * t + 48] for t in range(16)], lane)):
            mir_ids[t] = tile.astype(BF16)

    def wedges_go():
        for k in range(2):
            mirror_copy(k).start()

        @pl.when(lat < 16)
        def _():
            for k in range(2):
                corner_copy(k).start()

    def look_up(ids):
        found = jnp.full(ids.shape, levels[0], F32)
        for w in range(1, 16):
            found = jnp.where(ids == float(w), levels[w], found)
        return found

    def wedges_in():
        for k in range(2):
            mirror_copy(k).wait_recv()

        @pl.when(lat >= 16)
        def _():
            for k in range(2):
                corner_copy(k).wait_recv()

        @pl.loop(0, 16)
        def _(kk):
            own = own_ids[kk].astype(F32)
            mir = mir_ids[kk].astype(F32)
            got_mir = mir_in[kk].astype(F32)
            spec_own = spec_in[0, kk].astype(F32)
            spec_mir = spec_in[1, kk].astype(F32)
            level1[kk, 0:8, :] = look_up(jnp.where(seventh & (lat >= 16), own[32:40], own[0:8]))
            level1[kk, 8:32, :] = look_up(own[8:32])
            level1[kk, 32:40, :] = look_up(spec_own[0:8])
            row = jnp.where(lat == 16, mir[32:40], spec_mir[0:8])
            level2[kk, 0:8, :] = look_up(jnp.where(seventh & (lat >= 16), row, got_mir[0:8]))
            level2[kk, 8:32, :] = look_up(got_mir[8:32])
            level2[kk, 32:40, :] = look_up(spec_mir[0:8])

    def stack():
        wide_prepare(0)
        pl.semaphore_wait(barrier, LAT + 3)
        wide_launch(0)
        begin(2)
        wide_prepare(1)
        wide_launch(1)
        begin(3)
        wedges_out()
        wedges_go()
        forward(2)
        forward(3)
        wide_relay(0)
        wide_side(0)
        across(2)
        across(3)
        wide_final(0)
        wide_relay(1)
        wide_side(1)
        wide_final(1)
        wide_fold(0)
        wedges_in()
        for k in range(3, 7):
            tables[k].wait()
        wide_fold(1)
        fold(2)
        fold(3)

    def columns():
        pieces = [
            lax.dot_general(ft[:, 0:1024], folded0[...], NT, preferred_element_type=F32).reshape(LAT, 8, 128)
        ]
        for s in range(3):
            pieces.append(
                lax.dot_general(
                    ft[:, 1024 + 512 * s : 1536 + 512 * s], folded1[s], NT, preferred_element_type=F32
                ).reshape(LAT, 8, 128)
            )
        for k in range(2):
            both = jnp.concatenate([pieces[2 * k], pieces[2 * k + 1]], axis=1)
            send[:, 16 * k : 16 * k + 16, :] = both.astype(BF16)

        @pl.loop(1, LAT)
        def _(k):
            first_copy((lat + k) % LAT).start()

        held[flip] = send[lat]
        all_but_one = held.at[pl.ds(0, LAT - 1)]
        pltpu.make_async_copy(all_but_one, all_but_one, first_r).wait()

    def unpack():
        nothing = jnp.zeros((8, 128), F32)
        for p in range(16):
            u0, u1 = held[2 * p].astype(F32), held[2 * p + 1].astype(F32)
            re = jnp.where(low, u0, pltpu.roll(u1, 64, 1))
            im = jnp.where(low, pltpu.roll(u0, 64, 1), u1)
            xr[p, 0:32, :] = re
            xi[p, 0:8, :] = jnp.where(packed, 0.0, im[0:8])
            xi[p, 8:32, :] = im[8:32]
            xr[p, 32:40, :] = im[0:8]
            xi[p, 32:40, :] = nothing

    def lateral(sign):
        base = 0 if sign < 0 else 2

        @pl.loop(0, 5)
        def _(g):
            at = pl.ds(pl.multiple_of(8 * g, 8), 8)
            values = []
            for p in range(16):
                value = (xr[p, at, :], xi[p, at, :])
                if sign > 0:
                    cos, sin = tw[base, p : p + 1, :], tw[base + 1, p : p + 1, :]
                    value = (value[0] * cos - value[1] * sin, value[1] * cos + value[0] * sin)
                values.append(value)
            for p, value in enumerate(short_transform(values, sign)):
                if sign < 0:
                    cos, sin = tw[base, p : p + 1, :], tw[base + 1, p : p + 1, :]
                    value = (value[0] * cos - value[1] * sin, value[1] * cos + value[0] * sin)
                xr[p, at, :] = value[0]
                xi[p, at, :] = value[1]

    def middle():
        lateral(-1)
        for b in range(4):
            some = pl.ds(4 * b, 4)
            both = jnp.concatenate([xr[some].reshape(160, 128), xi[some].reshape(160, 128)], axis=1)
            spectrum = jnp.dot(both.astype(BF16), xt[0:256, :], preferred_element_type=F32)
            re, im = spectrum[:, :128], spectrum[:, 128:]
            inverse = lax.rsqrt(jnp.maximum(re * re + im * im, 1e-30))
            factor = jnp.maximum(1.0 - level1[some].reshape(160, 128) * inverse, 0.0)
            factor += jnp.maximum(1.0 - level2[some].reshape(160, 128) * inverse, 0.0)
            both = jnp.concatenate([re * factor, im * factor], axis=1)
            inner = jnp.dot(both.astype(BF16), xt[256:512, :], preferred_element_type=F32)
            xr[some] = inner[:, :128].reshape(4, 40, 128)
            xi[some] = inner[:, 128:].reshape(4, 40, 128)
        lateral(1)

    def turn_back():
        for p in range(16):
            re, im = xr[p, 0:32, :], xi[p, 0:32, :]
            im = jnp.concatenate([jnp.where(packed, xr[p, 32:40, :], im[0:8]), im[8:32]], axis=0)
            back[2 * p] = jnp.where(low, re, pltpu.roll(im, 64, 1)).astype(BF16)
            back[2 * p + 1] = jnp.where(low, pltpu.roll(re, 64, 1), im).astype(BF16)

        @pl.loop(1, LAT)
        def _(k):
            second_copy((lat + k) % LAT).start()

        got[lat] = back[lat]
        all_but_one = got.at[pl.ds(0, LAT - 1)]
        pltpu.make_async_copy(all_but_one, all_but_one, second_r).wait()

    def columns_back():
        for s in range(4):
            tall = got[:, 16 * (s // 2) : 16 * (s // 2) + 16, :].astype(F32)
            flat = tall[:, 8 * (s % 2) : 8 * (s % 2) + 8, :].reshape(256, 128).T.astype(BF16)
            wide = jnp.concatenate([flat[:64], flat[64:]], axis=1)
            mid[s] = jnp.dot(wide, it[512 * s : 512 * s + 512, :], preferred_element_type=F32)

        @pl.loop(0, 8)
        def _(g):
            at = pl.ds(pl.multiple_of(8 * g, 8), 8)
            parts = [(mid[s, at, 0:256], mid[s, at, 256:512]) for s in range(4)]
            even, odd = real_eight_back(parts[0][0], parts[0][1], parts[1], parts[2], parts[3])
            for k in range(4):
                out[0, at, 256 * k : 256 * k + 256] = even[k] + odd[k]
                out[0, at, 1024 + 256 * k : 1280 + 256 * k] = even[k] - odd[k]

    def drain():
        for c in range(2, CHUNKS):
            for k in range(2):
                relay_copy(c, k).wait_send()
                side_copy(c, k).wait_send()
                final_copy(c, k).wait_send()
                cross_copy(c, k).wait_send()
        for c in range(2):
            for k in range(2):
                relay2_copy(c, k).wait_send()
                side2_copy(c, k).wait_send()
                final2_copy(c, k).wait_send()
                for j in range(4):
                    wide_copy(c, j, k).wait_send()
        sent = send.at[pl.ds(0, LAT - 1)]
        pltpu.make_async_copy(sent, sent, first_s).wait()
        sent = back.at[pl.ds(0, LAT - 1)]
        pltpu.make_async_copy(sent, sent, second_s).wait()
        for k in range(2):
            mirror_copy(k).wait_send()

        @pl.when(lat < 16)
        def _():
            for k in range(2):
                corner_copy(k).wait_send()


    stack()
    columns()
    unpack()
    middle()
    turn_back()
    columns_back()
    drain()


def on_device(partials, wedges, levels):
    tables = [
        jnp.asarray(t)
        for t in (
            forward_tables(), inverse_tables(), lateral_tables(), turn_tables(), pick_tables(), lane_tables()
        )
    ]
    anywhere = pl.BlockSpec(memory_space=pltpu.HBM)
    vmem, dma = pltpu.VMEM, pltpu.SemaphoreType.DMA
    two = dma((CHUNKS, 2))
    doubled = pl.pallas_call(
        kernel,
        out_shape=jax.ShapeDtypeStruct((1, ROWS, N), F32),
        in_specs=[anywhere, anywhere, pl.BlockSpec(memory_space=pltpu.SMEM)] + [anywhere] * 6,
        out_specs=pl.BlockSpec(memory_space=pltpu.VMEM),
        scratch_shapes=[
            vmem(partials.shape, BF16),
            vmem(wedges.shape, jnp.int32),
            *[vmem(t.shape, t.dtype) for t in tables],
            vmem((CHUNKS, 2, CROWS, N), BF16),
            vmem((CHUNKS, 2, CROWS, N), BF16),
            vmem((CHUNKS, 2, CROWS, N), BF16),
            vmem((CHUNKS, 2, CROWS, N), BF16),
            vmem((2, 2, 4, CROWS, N), BF16),
            vmem((2, 4, CROWS, N), BF16),
            vmem((2, 2, CROWS, N // 2), BF16),
            vmem((2, 2, CROWS, N // 2), BF16),
            vmem((2, 2, CROWS, N // 2), BF16),
            vmem((128, 1024), BF16),
            vmem((3, 128, 512), BF16),
            vmem((LAT, 32, 128), BF16),
            vmem((LAT, 32, 128), BF16),
            vmem((16, 40, 128), F32),
            vmem((16, 40, 128), F32),
            vmem((16, 40, 128), F32),
            vmem((16, 40, 128), F32),
            vmem((16, 48, 128), BF16),
            vmem((16, 48, 128), BF16),
            vmem((16, 32, 128), BF16),
            vmem((2, 16, 16, 128), BF16),
            vmem((LAT, 32, 128), BF16),
            vmem((LAT, 32, 128), BF16),
            vmem((4, ROWS, 512), F32),
            dma((CHUNKS,)),
            dma((7,)),
            two, two, two, two, two, two, two, two,
            dma, dma, dma, dma,
            dma((4,)),
            dma((4,)),
            dma((2, 4, 2)), dma((2, 4, 2)),
            dma((2, 2)), dma((2, 2)), dma((2, 2)), dma((2, 2)), dma((2, 2)), dma((2, 2)),
        ],
        compiler_params=pltpu.CompilerParams(
            collective_id=0, has_side_effects=True, vmem_limit_bytes=60 * 1024 * 1024
        ),
        name="stack_threshold",
    )(partials, wedges, levels, *tables)
    return doubled * 0.5


def solution(mesh):
    in_specs = (P("shot", None, "lat", None), P("lat", None), P())
    return jax.shard_map(
        on_device, mesh=mesh, in_specs=in_specs, out_specs=P("shot", "lat", None), check_vma=False
    )
```

```python
import functools
import math

import jax
import jax.numpy as jnp
import ml_dtypes
import numpy as np
from jax import lax
from jax.experimental import pallas as pl
from jax.experimental.pallas import tpu as pltpu
from jax.sharding import PartitionSpec as P

MESH = pl.DeviceIdType.MESH
F32 = jnp.float32
BF16 = jnp.bfloat16
N = 2048
LAT = 32
ROWS = N // LAT
CHUNKS = 4
CROWS = ROWS // CHUNKS
HALF = math.sqrt(0.5)
NT = (((1,), (1,)), ((), ()))


def owned():
    ky = np.zeros((LAT, 32), np.int64)
    for d in range(LAT):
        for i in range(8):
            for s in (1, 2, 3):
                ky[d, 8 * s + i] = 64 * d + 8 * i + s
        for i in range(4):
            ky[d, i] = 64 * d + 8 * i + 4
        for i in range(4, 7):
            ky[d, i] = 64 * d + 8 * (i - 3)
        ky[d, 7] = 64 * d + (32 if d < 16 else 0)
    return ky


def forward_tables():
    ky = owned()
    y2 = np.arange(256)
    scale = 1.0 / math.sqrt(N)
    parts = []
    for s in range(4):
        rows = ky[:, 8 * s : 8 * s + 8].reshape(-1)
        angle = 2.0 * np.pi * ((rows[:, None] * y2[None, :]) % N) / N
        re, im = np.cos(angle), -np.sin(angle)
        if s == 0:
            packed = 16 * 8 + 7
            re[packed] = np.where(y2 % 2, -1.0, 1.0)
            im[packed] = 1.0
            four = (rows % 8 == 4)[:, None]
            zero = np.zeros_like(re)
            parts += [
                np.where(four, zero, re),
                np.where(four, re, zero),
                np.where(four, zero, im),
                np.where(four, im, zero),
            ]
        else:
            parts += [re, im]
    return (np.concatenate(parts, axis=1) * scale).astype(ml_dtypes.bfloat16)


def inverse_tables():
    ky = owned()
    y2 = np.arange(256)
    scale = 2.0 / math.sqrt(N)
    parts = []
    for s in range(4):
        rows = ky[:, 8 * s : 8 * s + 8].reshape(-1)
        angle = 2.0 * np.pi * ((rows[:, None] * y2[None, :]) % N) / N
        cos, sin = 2.0 * np.cos(angle), 2.0 * np.sin(angle)
        if s == 0:
            packed = 16 * 8 + 7
            cos[packed] = np.where(y2 % 2, -1.0, 1.0)
            sin[packed] = -1.0
            four = (rows % 8 == 4)[:, None]
            zero = np.zeros_like(cos)
            top = np.concatenate([np.where(four, zero, cos), np.where(four, cos, zero)], axis=1)
            low = np.concatenate([np.where(four, zero, -sin), np.where(four, -sin, zero)], axis=1)
        else:
            top = np.concatenate([cos, sin], axis=1)
            low = np.concatenate([-sin, cos], axis=1)
        parts += [top, low]
    return (np.concatenate(parts, axis=0) * scale).astype(ml_dtypes.bfloat16)


def lateral_tables():
    index = np.arange(128)
    angle = 2.0 * np.pi * ((index[:, None] * index[None, :]) % 128) / 128
    cos, sin = np.cos(angle), np.sin(angle)
    forward = np.block([[cos, -sin], [sin, cos]])
    inverse = np.block([[cos, sin], [-sin, cos]])
    return np.concatenate([forward, inverse], axis=0).astype(ml_dtypes.bfloat16)


def turn_tables():
    angle = 2.0 * np.pi * (np.arange(16)[:, None] * np.arange(128)[None, :]) / N
    scale = 1.0 / math.sqrt(N)
    cos, sin = np.cos(angle) * scale, np.sin(angle) * scale
    return np.stack([cos, -sin, 0.5 * cos, 0.5 * sin]).astype(np.float32)


def pick_tables():
    own = np.zeros((48, 64))
    mirror = np.zeros((48, 64))
    for i in range(8):
        for s in (1, 2, 3):
            own[8 * s + i, 8 * i + s] = 1
            mirror[8 * s + i, 8 * (7 - i) + 8 - s] = 1
    for i in range(4):
        own[i, 8 * i + 4] = 1
        mirror[i, 8 * (7 - i) + 4] = 1
    for i in range(4, 7):
        own[i, 8 * (i - 3)] = 1
        mirror[i, 8 * (11 - i)] = 1
    own[7, 32] = mirror[7, 32] = 1
    own[39, 0] = mirror[39, 0] = 1
    return np.concatenate([own, mirror], axis=0).astype(ml_dtypes.bfloat16)


def lane_tables():
    lanes = np.arange(128)
    place = (lanes % 16) * 8 + lanes // 16
    own = np.zeros((128, 128))
    own[lanes, place] = 1
    mirror = np.zeros((256, 128))
    mirror[128 - lanes, place] = 1
    return np.concatenate([own, mirror], axis=0).astype(ml_dtypes.bfloat16)


def turn(pair, step, length, sign):
    re, im = pair
    step = step % length
    if step == 0:
        return pair
    if 4 * step == length:
        return (-im, re) if sign > 0 else (im, -re)
    if 8 * step == length:
        return ((re - sign * im) * HALF, (im + sign * re) * HALF)
    if 8 * step == 3 * length:
        return ((-re - sign * im) * HALF, (-im + sign * re) * HALF)
    cos = math.cos(2.0 * math.pi * step / length)
    sin = sign * math.sin(2.0 * math.pi * step / length)
    return (re * cos - im * sin, im * cos + re * sin)


def short_transform(values, sign):
    count = len(values)
    if count == 1:
        return values
    even = short_transform(values[0::2], sign)
    odd = short_transform(values[1::2], sign)
    low, high = [], []
    for k in range(count // 2):
        re, im = turn(odd[k], k, count, sign)
        low.append((even[k][0] + re, even[k][1] + im))
        high.append((even[k][0] - re, even[k][1] - im))
    return low + high


def real_eight(u):
    a = [u[k] + u[k + 4] for k in range(4)]
    b = [u[k] - u[k + 4] for k in range(4)]
    even, odd = a[0] + a[2], a[1] + a[3]
    minus, plus = (b[1] - b[3]) * HALF, (b[1] + b[3]) * HALF
    return (
        even + odd,
        even - odd,
        (b[0] + minus, -(b[2] + plus)),
        (a[0] - a[2], a[3] - a[1]),
        (b[0] - minus, b[2] - plus),
    )


def real_eight_back(zero, four, one, two, three):
    plus, minus = zero + four, zero - four
    (r1, i1), (r2, i2), (r3, i3) = one, two, three
    p0, p1 = plus + r2, plus - r2
    m0, m1 = minus - i2, minus + i2
    e0, e1 = r1 + r3, i3 - i1
    o0 = (r1 - i1 - r3 - i3) * HALF
    o1 = (r3 - i3 - r1 - i1) * HALF
    return (p0, m0, p1, m1), (e0, o0, e1, o1)


def spread(tiles, lane):
    for bit in (8, 4, 2, 1):
        high = (lane // 8) % (2 * bit) >= bit
        new = list(tiles)
        for t in range(16):
            if t & bit:
                continue
            first, second = tiles[t], tiles[t | bit]
            new[t] = jnp.where(high, pltpu.roll(second, 8 * bit, 1), first)
            new[t | bit] = jnp.where(high, second, pltpu.roll(first, 128 - 8 * bit, 1))
        tiles = new
    return tiles


def kernel(
    part_hbm, wedge_hbm, levels, ft_hbm, it_hbm, xt_hbm, tw_hbm, pick_hbm, lane_hbm,
    out,
    part, wedge, ft, it, xt, tw, pick, lanet,
    relay, side, final, cross, wide, total, relay2, side2, final2,
    folded0, folded1, send, held, xr, xi, level1, level2, own_ids, mir_ids, mir_in, spec_in, back, got, mid,
    load_sem, table_sem, relay_s, relay_r, side_s, side_r, final_s, final_r, cross_s, cross_r,
    first_s, first_r, second_s, second_r, wedge_s, wedge_r,
    wide_s, wide_r, relay2_s, relay2_r, side2_s, side2_r, final2_s, final2_r,
):
    shot = lax.axis_index("shot")
    lat = lax.axis_index("lat")
    n_shot = lax.axis_size("shot")
    y, xh = shot // 2, shot % 2
    up, down = (shot + 2) % n_shot, (shot + n_shot - 2) % n_shot
    y_up, y_down, y_far = (y + 1) % 4, (y + 3) % 4, (y + 2) % 4
    flip = lat + 2 - 4 * ((lat // 2) % 2)
    other = shot + 1 - 2 * xh

    def rows(c):
        return pl.ds(c * CROWS, CROWS)

    loads = [
        pltpu.make_async_copy(
            part_hbm.at[:, :, rows(c), :], part.at[:, :, rows(c), :], load_sem.at[c]
        )
        for c in range(CHUNKS)
    ]
    loads[0].start()
    tables = [
        pltpu.make_async_copy(src, dst, table_sem.at[k])
        for k, (src, dst) in enumerate(
            [(wedge_hbm, wedge), (pick_hbm, pick), (lane_hbm, lanet), (ft_hbm, ft),
             (xt_hbm, xt), (tw_hbm, tw), (it_hbm, it)]
        )
    ]
    for c in (2, 1, 3):
        loads[c].start()
    for copy in tables:
        copy.start()

    barrier = pltpu.get_barrier_semaphore()

    def greet(s, l):
        pl.semaphore_signal(barrier, inc=1, device_id=(s, l), device_id_type=MESH)

    greet(up, lat)
    greet(down, lat)
    greet(other, flip)
    greet(other, LAT - 1 - lat)

    @pl.loop(1, LAT)
    def _(k):
        greet(shot, (lat + k) % LAT)

    def copy_to(src, dst, s_sem, r_sem, s, l):
        return pltpu.make_async_remote_copy(
            src_ref=src, dst_ref=dst, send_sem=s_sem, recv_sem=r_sem, device_id=(s, l), device_id_type=MESH
        )

    def slab(q, c):
        return part.at[0, q, rows(c), :]

    def relay_copy(c, k):
        q = 2 * y_far + k
        return copy_to(
            slab(q, c), relay.at[c, k], relay_s.at[c, k], relay_r.at[c, k], up if k == 0 else down, lat
        )

    def side_copy(c, k):
        q = 2 * y_up + 1 if k == 0 else 2 * y_down
        return copy_to(
            slab(q, c), side.at[c, k], side_s.at[c, k], side_r.at[c, k], up if k == 0 else down, lat
        )

    def final_copy(c, k):
        q = 2 * y_up if k == 0 else 2 * y_down + 1
        return copy_to(
            slab(q, c), final.at[c, k], final_s.at[c, k], final_r.at[c, k], up if k == 0 else down, lat
        )

    def cross_copy(c, h):
        return copy_to(
            slab(2 * y + h, c), cross.at[c, xh], cross_s.at[c, h], cross_r.at[c, xh], 2 * y + h, flip
        )

    def pair(q, c):
        return part[0, q, rows(c), :].astype(F32) + part[1, q, rows(c), :].astype(F32)

    def prepare(c):
        loads[c].wait()
        for q in (2 * y_far, 2 * y_far + 1, 2 * y_up + 1, 2 * y_down):
            part[0, q, rows(c), :] = pair(q, c).astype(BF16)

    def launch(c):
        for k in range(2):
            relay_copy(c, k).start()
        for k in range(2):
            side_copy(c, k).start()

    def begin(c):
        prepare(c)
        launch(c)

    def forward(c):
        for k in range(2):
            q = 2 * y_up if k == 0 else 2 * y_down + 1
            relay_copy(c, k).wait_recv()
            part[0, q, rows(c), :] = (pair(q, c) + relay[c, k].astype(F32)).astype(BF16)
            final_copy(c, k).start()

    def across(c):
        for k in range(2):
            side_copy(c, k).wait_recv()
            final_copy(c, k).wait_recv()
        for h in range(2):
            q = 2 * y + h
            total = pair(q, c) + final[c, h].astype(F32) + side[c, 1 - h].astype(F32)
            part[0, q, rows(c), :] = total.astype(BF16)
            cross_copy(c, h).start()

    def fold(c):
        for h in range(2):
            pltpu.make_async_copy(cross.at[c, h], cross.at[c, h], cross_r.at[c, h]).wait()
        u = []
        for k in range(8):
            cols = pl.ds(256 * k, 256)
            u.append(cross[c, 0, :, cols].astype(F32) + cross[c, 1, :, cols].astype(F32))
        keep(c, u)

    def keep(c, u):
        top, low = pl.ds(c * CROWS, CROWS), pl.ds(ROWS + c * CROWS, CROWS)
        zero, four, one, two, three = real_eight(u)
        zero, four = zero.astype(BF16), four.astype(BF16)
        blank = jnp.zeros((CROWS, 512), BF16)
        folded0[top, 0:256] = zero
        folded0[top, 256:512] = four
        folded0[top, 512:1024] = blank
        folded0[low, 0:512] = blank
        folded0[low, 512:768] = zero
        folded0[low, 768:1024] = four
        for s, (re, im) in enumerate((one, two, three)):
            re, im, neg = re.astype(BF16), im.astype(BF16), (-im).astype(BF16)
            folded1[s, top, 0:256] = re
            folded1[s, top, 256:512] = neg
            folded1[s, low, 0:256] = im
            folded1[s, low, 256:512] = re

    halves = (pl.ds(0, N // 2), pl.ds(N // 2, N // 2))
    y_order = (y_far, y_up, y_down, y)

    def wide_copy(c, j, h):
        return copy_to(
            slab(2 * y_order[j] + h, c), wide.at[c, xh, j], wide_s.at[c, j, h], wide_r.at[c, j, xh],
            2 * y + h, flip,
        )

    def wide_prepare(c):
        loads[c].wait()
        for q in range(8):
            part[0, q, rows(c), :] = pair(q, c).astype(BF16)

    def wide_launch(c):
        for j in range(4):
            for h in range(2):
                wide_copy(c, j, h).start()

    def wide_sum(c, j):
        for h in range(2):
            pltpu.make_async_copy(wide.at[c, h, j], wide.at[c, h, j], wide_r.at[c, j, h]).wait()
        return wide[c, 0, j].astype(F32) + wide[c, 1, j].astype(F32)

    def half_copy(c, k, j, half, target, s_sem, r_sem):
        return copy_to(
            total.at[c, j, :, halves[half]], target.at[c, k], s_sem.at[c, k], r_sem.at[c, k],
            up if k == 0 else down, lat,
        )

    def relay2_copy(c, k):
        return half_copy(c, k, 0, k, relay2, relay2_s, relay2_r)

    def side2_copy(c, k):
        return half_copy(c, k, 1 + k, 1 - k, side2, side2_s, side2_r)

    def final2_copy(c, k):
        return half_copy(c, k, 1 + k, k, final2, final2_s, final2_r)

    def wide_relay(c):
        total[c, 0] = wide_sum(c, 0).astype(BF16)
        for k in range(2):
            relay2_copy(c, k).start()

    def wide_side(c):
        for k in range(2):
            total[c, 1 + k] = wide_sum(c, 1 + k).astype(BF16)
            side2_copy(c, k).start()

    def wide_final(c):
        for k in range(2):
            relay2_copy(c, k).wait_recv()
            both = wide[c, 0, 1 + k, :, halves[k]].astype(F32) + wide[c, 1, 1 + k, :, halves[k]].astype(F32)
            total[c, 1 + k, :, halves[k]] = (both + relay2[c, k].astype(F32)).astype(BF16)
            final2_copy(c, k).start()

    def wide_fold(c):
        mine = wide_sum(c, 3)
        for k in range(2):
            side2_copy(c, k).wait_recv()
            final2_copy(c, k).wait_recv()
        u = []
        for k in range(8):
            half, cols = k // 4, pl.ds(256 * (k % 4), 256)
            u.append(
                mine[:, 256 * k : 256 * k + 256]
                + final2[c, half, :, cols].astype(F32)
                + side2[c, 1 - half, :, cols].astype(F32)
            )
        keep(c, u)

    def first_copy(dest):
        return copy_to(send.at[dest], held.at[flip], first_s, first_r, shot, dest)

    def second_copy(dest):
        return copy_to(back.at[dest], got.at[lat], second_s, second_r, shot, dest)

    lane = lax.broadcasted_iota(jnp.int32, (1, 128), 1)
    low = lane < 64
    packed = (lax.broadcasted_iota(jnp.int32, (8, 128), 0) == 7) & (lat == 16)
    seventh = lax.broadcasted_iota(jnp.int32, (8, 128), 0) == 7

    partner = LAT - 1 - lat
    corner = jnp.where(lat == 0, 16, LAT - lat)

    def mirror_copy(k):
        some = pl.ds(8 * k, 8)
        return copy_to(
            mir_ids.at[some, pl.ds(0, 32), :], mir_in.at[some], wedge_s.at[2 + k], wedge_r.at[2 + k],
            shot if k == 0 else other, partner,
        )

    def corner_copy(k):
        src = (own_ids if k == 0 else mir_ids).at[:, pl.ds(32, 16), :]
        return copy_to(src, spec_in.at[k], wedge_s.at[k], wedge_r.at[k], shot, corner)

    def wedges_out():
        for k in range(3):
            tables[k].wait()
        ids = wedge[...].astype(F32).astype(BF16)
        chosen = jnp.dot(pick[...], ids, preferred_element_type=F32).astype(BF16)
        own, mir = chosen[:48], chosen[48:]
        tall = jnp.concatenate([own[:, 128 * t : 128 * t + 128] for t in range(16)], axis=0)
        moved = jnp.dot(tall, lanet[0:128, :], preferred_element_type=F32)
        for t, tile in enumerate(spread([moved[48 * t : 48 * t + 48] for t in range(16)], lane)):
            own_ids[t] = tile.astype(BF16)
        tall = jnp.concatenate(
            [
                jnp.concatenate(
                    [mir[:, 128 * (15 - t) : 128 * (16 - t)],
                     mir[:, 128 * ((16 - t) % 16) : 128 * ((16 - t) % 16) + 128]],
                    axis=1,
                )
                for t in range(16)
            ],
            axis=0,
        )
        moved = jnp.dot(tall, lanet[128:384, :], preferred_element_type=F32)
        for t, tile in enumerate(spread([moved[48 * t : 48 * t + 48] for t in range(16)], lane)):
            mir_ids[t] = tile.astype(BF16)

    def wedges_go():
        for k in range(2):
            mirror_copy(k).start()

        @pl.when(lat < 16)
        def _():
            for k in range(2):
                corner_copy(k).start()

    def look_up(ids):
        found = jnp.full(ids.shape, levels[0], F32)
        for w in range(1, 16):
            found = jnp.where(ids == float(w), levels[w], found)
        return found

    def wedges_in():
        for k in range(2):
            mirror_copy(k).wait_recv()

        @pl.when(lat >= 16)
        def _():
            for k in range(2):
                corner_copy(k).wait_recv()

        @pl.loop(0, 16)
        def _(kk):
            own = own_ids[kk].astype(F32)
            mir = mir_ids[kk].astype(F32)
            got_mir = mir_in[kk].astype(F32)
            spec_own = spec_in[0, kk].astype(F32)
            spec_mir = spec_in[1, kk].astype(F32)
            level1[kk, 0:8, :] = look_up(jnp.where(seventh & (lat >= 16), own[32:40], own[0:8]))
            level1[kk, 8:32, :] = look_up(own[8:32])
            level1[kk, 32:40, :] = look_up(spec_own[0:8])
            row = jnp.where(lat == 16, mir[32:40], spec_mir[0:8])
            level2[kk, 0:8, :] = look_up(jnp.where(seventh & (lat >= 16), row, got_mir[0:8]))
            level2[kk, 8:32, :] = look_up(got_mir[8:32])
            level2[kk, 32:40, :] = look_up(spec_mir[0:8])

    def stack():
        wide_prepare(0)
        pl.semaphore_wait(barrier, LAT + 3)
        wide_launch(0)
        begin(2)
        wide_prepare(1)
        wide_launch(1)
        begin(3)
        wedges_out()
        wedges_go()
        forward(2)
        forward(3)
        wide_relay(0)
        wide_side(0)
        across(2)
        across(3)
        wide_final(0)
        wide_relay(1)
        wide_side(1)
        wide_final(1)
        wide_fold(0)
        for k in range(3, 7):
            tables[k].wait()
        wide_fold(1)
        fold(2)
        fold(3)

    def columns():
        pieces = [
            lax.dot_general(ft[:, 0:1024], folded0[...], NT, preferred_element_type=F32).reshape(LAT, 8, 128)
        ]
        for s in range(3):
            pieces.append(
                lax.dot_general(
                    ft[:, 1024 + 512 * s : 1536 + 512 * s], folded1[s], NT, preferred_element_type=F32
                ).reshape(LAT, 8, 128)
            )
        for k in range(2):
            both = jnp.concatenate([pieces[2 * k], pieces[2 * k + 1]], axis=1)
            send[:, 16 * k : 16 * k + 16, :] = both.astype(BF16)

        @pl.loop(1, LAT)
        def _(k):
            first_copy((lat + k) % LAT).start()

        held[flip] = send[lat]
        wedges_in()
        all_but_one = held.at[pl.ds(0, LAT - 1)]
        pltpu.make_async_copy(all_but_one, all_but_one, first_r).wait()

    def unpack():
        nothing = jnp.zeros((8, 128), F32)
        for p in range(16):
            u0, u1 = held[2 * p].astype(F32), held[2 * p + 1].astype(F32)
            re = jnp.where(low, u0, pltpu.roll(u1, 64, 1))
            im = jnp.where(low, pltpu.roll(u0, 64, 1), u1)
            xr[p, 0:32, :] = re
            xi[p, 0:8, :] = jnp.where(packed, 0.0, im[0:8])
            xi[p, 8:32, :] = im[8:32]
            xr[p, 32:40, :] = im[0:8]
            xi[p, 32:40, :] = nothing

    def lateral(sign):
        base = 0 if sign < 0 else 2

        @pl.loop(0, 5)
        def _(g):
            at = pl.ds(pl.multiple_of(8 * g, 8), 8)
            values = []
            for p in range(16):
                value = (xr[p, at, :], xi[p, at, :])
                if sign > 0:
                    cos, sin = tw[base, p : p + 1, :], tw[base + 1, p : p + 1, :]
                    value = (value[0] * cos - value[1] * sin, value[1] * cos + value[0] * sin)
                values.append(value)
            for p, value in enumerate(short_transform(values, sign)):
                if sign < 0:
                    cos, sin = tw[base, p : p + 1, :], tw[base + 1, p : p + 1, :]
                    value = (value[0] * cos - value[1] * sin, value[1] * cos + value[0] * sin)
                xr[p, at, :] = value[0]
                xi[p, at, :] = value[1]

    def middle():
        lateral(-1)
        for b in range(4):
            some = pl.ds(4 * b, 4)
            both = jnp.concatenate([xr[some].reshape(160, 128), xi[some].reshape(160, 128)], axis=1)
            spectrum = jnp.dot(both.astype(BF16), xt[0:256, :], preferred_element_type=F32)
            re, im = spectrum[:, :128], spectrum[:, 128:]
            inverse = lax.rsqrt(jnp.maximum(re * re + im * im, 1e-30))
            factor = jnp.maximum(1.0 - level1[some].reshape(160, 128) * inverse, 0.0)
            factor += jnp.maximum(1.0 - level2[some].reshape(160, 128) * inverse, 0.0)
            both = jnp.concatenate([re * factor, im * factor], axis=1)
            inner = jnp.dot(both.astype(BF16), xt[256:512, :], preferred_element_type=F32)
            xr[some] = inner[:, :128].reshape(4, 40, 128)
            xi[some] = inner[:, 128:].reshape(4, 40, 128)
        lateral(1)

    def turn_back():
        for p in range(16):
            re, im = xr[p, 0:32, :], xi[p, 0:32, :]
            im = jnp.concatenate([jnp.where(packed, xr[p, 32:40, :], im[0:8]), im[8:32]], axis=0)
            back[2 * p] = jnp.where(low, re, pltpu.roll(im, 64, 1)).astype(BF16)
            back[2 * p + 1] = jnp.where(low, pltpu.roll(re, 64, 1), im).astype(BF16)

        @pl.loop(1, LAT)
        def _(k):
            second_copy((lat + k) % LAT).start()

        got[lat] = back[lat]
        all_but_one = got.at[pl.ds(0, LAT - 1)]
        pltpu.make_async_copy(all_but_one, all_but_one, second_r).wait()

    def columns_back():
        for s in range(4):
            tall = got[:, 16 * (s // 2) : 16 * (s // 2) + 16, :].astype(F32)
            flat = tall[:, 8 * (s % 2) : 8 * (s % 2) + 8, :].reshape(256, 128).T.astype(BF16)
            wide = jnp.concatenate([flat[:64], flat[64:]], axis=1)
            mid[s] = jnp.dot(wide, it[512 * s : 512 * s + 512, :], preferred_element_type=F32)

        @pl.loop(0, 8)
        def _(g):
            at = pl.ds(pl.multiple_of(8 * g, 8), 8)
            parts = [(mid[s, at, 0:256], mid[s, at, 256:512]) for s in range(4)]
            even, odd = real_eight_back(parts[0][0], parts[0][1], parts[1], parts[2], parts[3])
            for k in range(4):
                out[0, at, 256 * k : 256 * k + 256] = even[k] + odd[k]
                out[0, at, 1024 + 256 * k : 1280 + 256 * k] = even[k] - odd[k]

    def drain():
        for c in range(2, CHUNKS):
            for k in range(2):
                relay_copy(c, k).wait_send()
                side_copy(c, k).wait_send()
                final_copy(c, k).wait_send()
                cross_copy(c, k).wait_send()
        for c in range(2):
            for k in range(2):
                relay2_copy(c, k).wait_send()
                side2_copy(c, k).wait_send()
                final2_copy(c, k).wait_send()
                for j in range(4):
                    wide_copy(c, j, k).wait_send()
        sent = send.at[pl.ds(0, LAT - 1)]
        pltpu.make_async_copy(sent, sent, first_s).wait()
        sent = back.at[pl.ds(0, LAT - 1)]
        pltpu.make_async_copy(sent, sent, second_s).wait()
        for k in range(2):
            mirror_copy(k).wait_send()

        @pl.when(lat < 16)
        def _():
            for k in range(2):
                corner_copy(k).wait_send()


    stack()
    columns()
    unpack()
    middle()
    turn_back()
    columns_back()
    drain()


def on_device(partials, wedges, levels):
    tables = [
        jnp.asarray(t)
        for t in (
            forward_tables(), inverse_tables(), lateral_tables(), turn_tables(), pick_tables(), lane_tables()
        )
    ]
    anywhere = pl.BlockSpec(memory_space=pltpu.HBM)
    vmem, dma = pltpu.VMEM, pltpu.SemaphoreType.DMA
    two = dma((CHUNKS, 2))
    doubled = pl.pallas_call(
        kernel,
        out_shape=jax.ShapeDtypeStruct((1, ROWS, N), F32),
        in_specs=[anywhere, anywhere, pl.BlockSpec(memory_space=pltpu.SMEM)] + [anywhere] * 6,
        out_specs=pl.BlockSpec(memory_space=pltpu.VMEM),
        scratch_shapes=[
            vmem(partials.shape, BF16),
            vmem(wedges.shape, jnp.int32),
            *[vmem(t.shape, t.dtype) for t in tables],
            vmem((CHUNKS, 2, CROWS, N), BF16),
            vmem((CHUNKS, 2, CROWS, N), BF16),
            vmem((CHUNKS, 2, CROWS, N), BF16),
            vmem((CHUNKS, 2, CROWS, N), BF16),
            vmem((2, 2, 4, CROWS, N), BF16),
            vmem((2, 4, CROWS, N), BF16),
            vmem((2, 2, CROWS, N // 2), BF16),
            vmem((2, 2, CROWS, N // 2), BF16),
            vmem((2, 2, CROWS, N // 2), BF16),
            vmem((128, 1024), BF16),
            vmem((3, 128, 512), BF16),
            vmem((LAT, 32, 128), BF16),
            vmem((LAT, 32, 128), BF16),
            vmem((16, 40, 128), F32),
            vmem((16, 40, 128), F32),
            vmem((16, 40, 128), F32),
            vmem((16, 40, 128), F32),
            vmem((16, 48, 128), BF16),
            vmem((16, 48, 128), BF16),
            vmem((16, 32, 128), BF16),
            vmem((2, 16, 16, 128), BF16),
            vmem((LAT, 32, 128), BF16),
            vmem((LAT, 32, 128), BF16),
            vmem((4, ROWS, 512), F32),
            dma((CHUNKS,)),
            dma((7,)),
            two, two, two, two, two, two, two, two,
            dma, dma, dma, dma,
            dma((4,)),
            dma((4,)),
            dma((2, 4, 2)), dma((2, 4, 2)),
            dma((2, 2)), dma((2, 2)), dma((2, 2)), dma((2, 2)), dma((2, 2)), dma((2, 2)),
        ],
        compiler_params=pltpu.CompilerParams(
            collective_id=0, has_side_effects=True, vmem_limit_bytes=60 * 1024 * 1024
        ),
        name="stack_threshold",
    )(partials, wedges, levels, *tables)
    return doubled * 0.5


def solution(mesh):
    in_specs = (P("shot", None, "lat", None), P("lat", None), P())
    return jax.shard_map(
        on_device, mesh=mesh, in_specs=in_specs, out_specs=P("shot", "lat", None), check_vma=False
    )
```

```python
import functools
import math

import jax
import jax.numpy as jnp
import ml_dtypes
import numpy as np
from jax import lax
from jax.experimental import pallas as pl
from jax.experimental.pallas import tpu as pltpu
from jax.sharding import PartitionSpec as P

MESH = pl.DeviceIdType.MESH
F32 = jnp.float32
BF16 = jnp.bfloat16
N = 2048
LAT = 32
ROWS = N // LAT
CHUNKS = 4
CROWS = ROWS // CHUNKS
HALF = math.sqrt(0.5)
NT = (((1,), (1,)), ((), ()))


def owned():
    ky = np.zeros((LAT, 32), np.int64)
    for d in range(LAT):
        for i in range(8):
            for s in (1, 2, 3):
                ky[d, 8 * s + i] = 64 * d + 8 * i + s
        for i in range(4):
            ky[d, i] = 64 * d + 8 * i + 4
        for i in range(4, 7):
            ky[d, i] = 64 * d + 8 * (i - 3)
        ky[d, 7] = 64 * d + (32 if d < 16 else 0)
    return ky


def forward_tables():
    ky = owned()
    y2 = np.arange(256)
    scale = 1.0 / math.sqrt(N)
    parts = []
    for s in range(4):
        rows = ky[:, 8 * s : 8 * s + 8].reshape(-1)
        angle = 2.0 * np.pi * ((rows[:, None] * y2[None, :]) % N) / N
        re, im = np.cos(angle), -np.sin(angle)
        if s == 0:
            packed = 16 * 8 + 7
            re[packed] = np.where(y2 % 2, -1.0, 1.0)
            im[packed] = 1.0
            four = (rows % 8 == 4)[:, None]
            zero = np.zeros_like(re)
            parts += [
                np.where(four, zero, re),
                np.where(four, re, zero),
                np.where(four, zero, im),
                np.where(four, im, zero),
            ]
        else:
            parts += [re, im]
    return (np.concatenate(parts, axis=1) * scale).astype(ml_dtypes.bfloat16)


def inverse_tables():
    ky = owned()
    y2 = np.arange(256)
    scale = 2.0 / math.sqrt(N)
    parts = []
    for s in range(4):
        rows = ky[:, 8 * s : 8 * s + 8].reshape(-1)
        angle = 2.0 * np.pi * ((rows[:, None] * y2[None, :]) % N) / N
        cos, sin = 2.0 * np.cos(angle), 2.0 * np.sin(angle)
        if s == 0:
            packed = 16 * 8 + 7
            cos[packed] = np.where(y2 % 2, -1.0, 1.0)
            sin[packed] = -1.0
            four = (rows % 8 == 4)[:, None]
            zero = np.zeros_like(cos)
            top = np.concatenate([np.where(four, zero, cos), np.where(four, cos, zero)], axis=1)
            low = np.concatenate([np.where(four, zero, -sin), np.where(four, -sin, zero)], axis=1)
        else:
            top = np.concatenate([cos, sin], axis=1)
            low = np.concatenate([-sin, cos], axis=1)
        parts += [top, low]
    return (np.concatenate(parts, axis=0) * scale).astype(ml_dtypes.bfloat16)


def lateral_tables():
    index = np.arange(128)
    angle = 2.0 * np.pi * ((index[:, None] * index[None, :]) % 128) / 128
    cos, sin = np.cos(angle), np.sin(angle)
    forward = np.block([[cos, -sin], [sin, cos]])
    inverse = np.block([[cos, sin], [-sin, cos]])
    return np.concatenate([forward, inverse], axis=0).astype(ml_dtypes.bfloat16)


def turn_tables():
    angle = 2.0 * np.pi * (np.arange(16)[:, None] * np.arange(128)[None, :]) / N
    scale = 1.0 / math.sqrt(N)
    cos, sin = np.cos(angle) * scale, np.sin(angle) * scale
    return np.stack([cos, -sin, 0.5 * cos, 0.5 * sin]).astype(np.float32)


def pick_tables():
    own = np.zeros((48, 64))
    mirror = np.zeros((48, 64))
    for i in range(8):
        for s in (1, 2, 3):
            own[8 * s + i, 8 * i + s] = 1
            mirror[8 * s + i, 8 * (7 - i) + 8 - s] = 1
    for i in range(4):
        own[i, 8 * i + 4] = 1
        mirror[i, 8 * (7 - i) + 4] = 1
    for i in range(4, 7):
        own[i, 8 * (i - 3)] = 1
        mirror[i, 8 * (11 - i)] = 1
    own[7, 32] = mirror[7, 32] = 1
    own[39, 0] = mirror[39, 0] = 1
    return np.concatenate([own, mirror], axis=0).astype(ml_dtypes.bfloat16)


def lane_tables():
    lanes = np.arange(128)
    place = (lanes % 16) * 8 + lanes // 16
    own = np.zeros((128, 128))
    own[lanes, place] = 1
    mirror = np.zeros((256, 128))
    mirror[128 - lanes, place] = 1
    return np.concatenate([own, mirror], axis=0).astype(ml_dtypes.bfloat16)


def turn(pair, step, length, sign):
    re, im = pair
    step = step % length
    if step == 0:
        return pair
    if 4 * step == length:
        return (-im, re) if sign > 0 else (im, -re)
    if 8 * step == length:
        return ((re - sign * im) * HALF, (im + sign * re) * HALF)
    if 8 * step == 3 * length:
        return ((-re - sign * im) * HALF, (-im + sign * re) * HALF)
    cos = math.cos(2.0 * math.pi * step / length)
    sin = sign * math.sin(2.0 * math.pi * step / length)
    return (re * cos - im * sin, im * cos + re * sin)


def short_transform(values, sign):
    count = len(values)
    if count == 1:
        return values
    even = short_transform(values[0::2], sign)
    odd = short_transform(values[1::2], sign)
    low, high = [], []
    for k in range(count // 2):
        re, im = turn(odd[k], k, count, sign)
        low.append((even[k][0] + re, even[k][1] + im))
        high.append((even[k][0] - re, even[k][1] - im))
    return low + high


def real_eight(u):
    a = [u[k] + u[k + 4] for k in range(4)]
    b = [u[k] - u[k + 4] for k in range(4)]
    even, odd = a[0] + a[2], a[1] + a[3]
    minus, plus = (b[1] - b[3]) * HALF, (b[1] + b[3]) * HALF
    return (
        even + odd,
        even - odd,
        (b[0] + minus, -(b[2] + plus)),
        (a[0] - a[2], a[3] - a[1]),
        (b[0] - minus, b[2] - plus),
    )


def real_eight_back(zero, four, one, two, three):
    plus, minus = zero + four, zero - four
    (r1, i1), (r2, i2), (r3, i3) = one, two, three
    p0, p1 = plus + r2, plus - r2
    m0, m1 = minus - i2, minus + i2
    e0, e1 = r1 + r3, i3 - i1
    o0 = (r1 - i1 - r3 - i3) * HALF
    o1 = (r3 - i3 - r1 - i1) * HALF
    return (p0, m0, p1, m1), (e0, o0, e1, o1)


def spread(tiles, lane):
    for bit in (8, 4, 2, 1):
        high = (lane // 8) % (2 * bit) >= bit
        new = list(tiles)
        for t in range(16):
            if t & bit:
                continue
            first, second = tiles[t], tiles[t | bit]
            new[t] = jnp.where(high, pltpu.roll(second, 8 * bit, 1), first)
            new[t | bit] = jnp.where(high, second, pltpu.roll(first, 128 - 8 * bit, 1))
        tiles = new
    return tiles


def kernel(
    part_hbm, wedge_hbm, levels, ft_hbm, it_hbm, xt_hbm, tw_hbm, pick_hbm, lane_hbm,
    out,
    part, wedge, ft, it, xt, tw, pick, lanet,
    relay, side, final, cross, wide, total, relay2, side2, final2,
    folded0, folded1, send, held, xr, xi, level1, level2, own_ids, mir_ids, mir_in, spec_in, back, got, mid,
    load_sem, table_sem, relay_s, relay_r, side_s, side_r, final_s, final_r, cross_s, cross_r,
    first_s, first_r, second_s, second_r, wedge_s, wedge_r,
    wide_s, wide_r, relay2_s, relay2_r, side2_s, side2_r, final2_s, final2_r,
):
    shot = lax.axis_index("shot")
    lat = lax.axis_index("lat")
    n_shot = lax.axis_size("shot")
    y, xh = shot // 2, shot % 2
    up, down = (shot + 2) % n_shot, (shot + n_shot - 2) % n_shot
    y_up, y_down, y_far = (y + 1) % 4, (y + 3) % 4, (y + 2) % 4
    flip = lat + 2 - 4 * ((lat // 2) % 2)
    other = shot + 1 - 2 * xh

    def rows(c):
        return pl.ds(c * CROWS, CROWS)

    loads = [
        pltpu.make_async_copy(
            part_hbm.at[:, :, rows(c), :], part.at[:, :, rows(c), :], load_sem.at[c]
        )
        for c in range(CHUNKS)
    ]
    loads[0].start()
    tables = [
        pltpu.make_async_copy(src, dst, table_sem.at[k])
        for k, (src, dst) in enumerate(
            [(wedge_hbm, wedge), (pick_hbm, pick), (lane_hbm, lanet), (ft_hbm, ft),
             (xt_hbm, xt), (tw_hbm, tw), (it_hbm, it)]
        )
    ]
    for c in (2, 1, 3):
        loads[c].start()
    for copy in tables:
        copy.start()

    barrier = pltpu.get_barrier_semaphore()

    def greet(s, l):
        pl.semaphore_signal(barrier, inc=1, device_id=(s, l), device_id_type=MESH)

    greet(up, lat)
    greet(down, lat)
    greet(other, flip)
    greet(other, LAT - 1 - lat)

    @pl.loop(1, LAT)
    def _(k):
        greet(shot, (lat + k) % LAT)

    def copy_to(src, dst, s_sem, r_sem, s, l):
        return pltpu.make_async_remote_copy(
            src_ref=src, dst_ref=dst, send_sem=s_sem, recv_sem=r_sem, device_id=(s, l), device_id_type=MESH
        )

    def slab(q, c):
        return part.at[0, q, rows(c), :]

    def relay_copy(c, k):
        q = 2 * y_far + k
        return copy_to(
            slab(q, c), relay.at[c, k], relay_s.at[c, k], relay_r.at[c, k], up if k == 0 else down, lat
        )

    def side_copy(c, k):
        q = 2 * y_up + 1 if k == 0 else 2 * y_down
        return copy_to(
            slab(q, c), side.at[c, k], side_s.at[c, k], side_r.at[c, k], up if k == 0 else down, lat
        )

    def final_copy(c, k):
        q = 2 * y_up if k == 0 else 2 * y_down + 1
        return copy_to(
            slab(q, c), final.at[c, k], final_s.at[c, k], final_r.at[c, k], up if k == 0 else down, lat
        )

    def cross_copy(c, h):
        return copy_to(
            slab(2 * y + h, c), cross.at[c, xh], cross_s.at[c, h], cross_r.at[c, xh], 2 * y + h, flip
        )

    def pair(q, c):
        return part[0, q, rows(c), :].astype(F32) + part[1, q, rows(c), :].astype(F32)

    def prepare(c):
        loads[c].wait()
        for q in (2 * y_far, 2 * y_far + 1, 2 * y_up + 1, 2 * y_down):
            part[0, q, rows(c), :] = pair(q, c).astype(BF16)

    def launch(c):
        for k in range(2):
            relay_copy(c, k).start()
        for k in range(2):
            side_copy(c, k).start()

    def begin(c):
        prepare(c)
        launch(c)

    def forward(c):
        for k in range(2):
            q = 2 * y_up if k == 0 else 2 * y_down + 1
            relay_copy(c, k).wait_recv()
            part[0, q, rows(c), :] = (pair(q, c) + relay[c, k].astype(F32)).astype(BF16)
            final_copy(c, k).start()

    def across(c):
        for k in range(2):
            side_copy(c, k).wait_recv()
            final_copy(c, k).wait_recv()
        for h in range(2):
            q = 2 * y + h
            total = pair(q, c) + final[c, h].astype(F32) + side[c, 1 - h].astype(F32)
            part[0, q, rows(c), :] = total.astype(BF16)
            cross_copy(c, h).start()

    def fold(c):
        for h in range(2):
            pltpu.make_async_copy(cross.at[c, h], cross.at[c, h], cross_r.at[c, h]).wait()
        u = []
        for k in range(8):
            cols = pl.ds(256 * k, 256)
            u.append(cross[c, 0, :, cols].astype(F32) + cross[c, 1, :, cols].astype(F32))
        keep(c, u)

    def keep(c, u):
        top, low = pl.ds(c * CROWS, CROWS), pl.ds(ROWS + c * CROWS, CROWS)
        zero, four, one, two, three = real_eight(u)
        zero, four = zero.astype(BF16), four.astype(BF16)
        blank = jnp.zeros((CROWS, 512), BF16)
        folded0[top, 0:256] = zero
        folded0[top, 256:512] = four
        folded0[top, 512:1024] = blank
        folded0[low, 0:512] = blank
        folded0[low, 512:768] = zero
        folded0[low, 768:1024] = four
        for s, (re, im) in enumerate((one, two, three)):
            re, im, neg = re.astype(BF16), im.astype(BF16), (-im).astype(BF16)
            folded1[s, top, 0:256] = re
            folded1[s, top, 256:512] = neg
            folded1[s, low, 0:256] = im
            folded1[s, low, 256:512] = re

    halves = (pl.ds(0, N // 2), pl.ds(N // 2, N // 2))
    y_order = (y_far, y_up, y_down, y)

    def wide_copy(c, j, h):
        return copy_to(
            slab(2 * y_order[j] + h, c), wide.at[c, xh, j], wide_s.at[c, j, h], wide_r.at[c, j, xh],
            2 * y + h, flip,
        )

    def wide_prepare(c, j):
        for h in range(2):
            q = 2 * y_order[j] + h
            part[0, q, rows(c), :] = pair(q, c).astype(BF16)

    def wide_launch(c, j):
        for h in range(2):
            wide_copy(c, j, h).start()

    def wide_sum(c, j):
        for h in range(2):
            pltpu.make_async_copy(wide.at[c, h, j], wide.at[c, h, j], wide_r.at[c, j, h]).wait()
        return wide[c, 0, j].astype(F32) + wide[c, 1, j].astype(F32)

    def half_copy(c, k, j, half, target, s_sem, r_sem):
        return copy_to(
            total.at[c, j, :, halves[half]], target.at[c, k], s_sem.at[c, k], r_sem.at[c, k],
            up if k == 0 else down, lat,
        )

    def relay2_copy(c, k):
        return half_copy(c, k, 0, k, relay2, relay2_s, relay2_r)

    def side2_copy(c, k):
        return half_copy(c, k, 1 + k, 1 - k, side2, side2_s, side2_r)

    def final2_copy(c, k):
        return half_copy(c, k, 1 + k, k, final2, final2_s, final2_r)

    def wide_relay(c):
        total[c, 0] = wide_sum(c, 0).astype(BF16)
        for k in range(2):
            relay2_copy(c, k).start()

    def wide_side(c):
        for k in range(2):
            total[c, 1 + k] = wide_sum(c, 1 + k).astype(BF16)
            side2_copy(c, k).start()

    def wide_final(c):
        for k in range(2):
            relay2_copy(c, k).wait_recv()
            both = wide[c, 0, 1 + k, :, halves[k]].astype(F32) + wide[c, 1, 1 + k, :, halves[k]].astype(F32)
            total[c, 1 + k, :, halves[k]] = (both + relay2[c, k].astype(F32)).astype(BF16)
            final2_copy(c, k).start()

    def wide_fold(c):
        mine = wide_sum(c, 3)
        for k in range(2):
            side2_copy(c, k).wait_recv()
            final2_copy(c, k).wait_recv()
        u = []
        for k in range(8):
            half, cols = k // 4, pl.ds(256 * (k % 4), 256)
            u.append(
                mine[:, 256 * k : 256 * k + 256]
                + final2[c, half, :, cols].astype(F32)
                + side2[c, 1 - half, :, cols].astype(F32)
            )
        keep(c, u)

    def first_copy(dest):
        return copy_to(send.at[dest], held.at[flip], first_s, first_r, shot, dest)

    def second_copy(dest):
        return copy_to(back.at[dest], got.at[lat], second_s, second_r, shot, dest)

    lane = lax.broadcasted_iota(jnp.int32, (1, 128), 1)
    low = lane < 64
    packed = (lax.broadcasted_iota(jnp.int32, (8, 128), 0) == 7) & (lat == 16)
    seventh = lax.broadcasted_iota(jnp.int32, (8, 128), 0) == 7

    partner = LAT - 1 - lat
    corner = jnp.where(lat == 0, 16, LAT - lat)

    def mirror_copy(k):
        some = pl.ds(8 * k, 8)
        return copy_to(
            mir_ids.at[some, pl.ds(0, 32), :], mir_in.at[some], wedge_s.at[2 + k], wedge_r.at[2 + k],
            shot if k == 0 else other, partner,
        )

    def corner_copy():
        return copy_to(
            mir_ids.at[:, pl.ds(32, 16), :], spec_in, wedge_s.at[0], wedge_r.at[0], shot, corner
        )

    def wedges_out():
        for k in range(3):
            tables[k].wait()
        ids = wedge[...].astype(F32).astype(BF16)
        chosen = jnp.dot(pick[...], ids, preferred_element_type=F32).astype(BF16)
        own, mir = chosen[:48], chosen[48:]
        tall = jnp.concatenate([own[:, 128 * t : 128 * t + 128] for t in range(16)], axis=0)
        moved = jnp.dot(tall, lanet[0:128, :], preferred_element_type=F32)
        own_tiles = spread([moved[48 * t : 48 * t + 48] for t in range(16)], lane)
        for t, tile in enumerate(own_tiles):
            own_ids[t] = tile.astype(BF16)
        tall = jnp.concatenate(
            [
                jnp.concatenate(
                    [mir[:, 128 * (15 - t) : 128 * (16 - t)],
                     mir[:, 128 * ((16 - t) % 16) : 128 * ((16 - t) % 16) + 128]],
                    axis=1,
                )
                for t in range(16)
            ],
            axis=0,
        )
        moved = jnp.dot(tall, lanet[128:384, :], preferred_element_type=F32)
        for t, tile in enumerate(spread([moved[48 * t : 48 * t + 48] for t in range(16)], lane)):
            mir_ids[t] = jnp.concatenate([tile[:40], own_tiles[t][32:40]], axis=0).astype(BF16)

    def wedges_go():
        for k in range(2):
            mirror_copy(k).start()

        @pl.when(lat < 16)
        def _():
            corner_copy().start()

    def look_up(ids):
        found = jnp.full(ids.shape, levels[0], F32)
        for w in range(1, 16):
            found = jnp.where(ids == float(w), levels[w], found)
        return found

    def wedges_in():
        for k in range(2):
            mirror_copy(k).wait_recv()

        @pl.when(lat >= 16)
        def _():
            corner_copy().wait_recv()

        @pl.loop(0, 16)
        def _(kk):
            own = own_ids[kk].astype(F32)
            mir = mir_ids[kk].astype(F32)
            got_mir = mir_in[kk].astype(F32)
            spec = spec_in[kk].astype(F32)
            spec_mir, spec_own = spec[0:8], spec[8:16]
            level1[kk, 0:8, :] = look_up(jnp.where(seventh & (lat >= 16), own[32:40], own[0:8]))
            level1[kk, 8:32, :] = look_up(own[8:32])
            level1[kk, 32:40, :] = look_up(spec_own)
            row = jnp.where(lat == 16, mir[32:40], spec_mir)
            level2[kk, 0:8, :] = look_up(jnp.where(seventh & (lat >= 16), row, got_mir[0:8]))
            level2[kk, 8:32, :] = look_up(got_mir[8:32])
            level2[kk, 32:40, :] = look_up(spec_mir)

    def stack():
        loads[0].wait()
        wide_prepare(0, 0)
        pl.semaphore_wait(barrier, LAT + 3)
        wide_launch(0, 0)
        wide_prepare(0, 1)
        wide_launch(0, 1)
        begin(2)
        for j in (2, 3):
            wide_prepare(0, j)
            wide_launch(0, j)
        loads[1].wait()
        for j in range(4):
            wide_prepare(1, j)
            wide_launch(1, j)
        begin(3)
        wedges_out()
        wedges_go()
        forward(2)
        forward(3)
        wide_relay(0)
        wide_side(0)
        across(2)
        across(3)
        wide_final(0)
        wide_relay(1)
        wide_side(1)
        wide_final(1)
        wide_fold(0)
        for k in range(3, 7):
            tables[k].wait()
        wide_fold(1)
        fold(2)
        fold(3)

    def columns():
        pieces = [
            lax.dot_general(ft[:, 0:1024], folded0[...], NT, preferred_element_type=F32).reshape(LAT, 8, 128)
        ]
        for s in range(3):
            pieces.append(
                lax.dot_general(
                    ft[:, 1024 + 512 * s : 1536 + 512 * s], folded1[s], NT, preferred_element_type=F32
                ).reshape(LAT, 8, 128)
            )
        for k in range(2):
            both = jnp.concatenate([pieces[2 * k], pieces[2 * k + 1]], axis=1)
            send[:, 16 * k : 16 * k + 16, :] = both.astype(BF16)

        @pl.loop(1, LAT)
        def _(k):
            first_copy((lat + k) % LAT).start()

        held[flip] = send[lat]
        wedges_in()
        all_but_one = held.at[pl.ds(0, LAT - 1)]
        pltpu.make_async_copy(all_but_one, all_but_one, first_r).wait()

    def unpack():
        nothing = jnp.zeros((8, 128), F32)
        for p in range(16):
            u0, u1 = held[2 * p].astype(F32), held[2 * p + 1].astype(F32)
            re = jnp.where(low, u0, pltpu.roll(u1, 64, 1))
            im = jnp.where(low, pltpu.roll(u0, 64, 1), u1)
            xr[p, 0:32, :] = re
            xi[p, 0:8, :] = jnp.where(packed, 0.0, im[0:8])
            xi[p, 8:32, :] = im[8:32]
            xr[p, 32:40, :] = im[0:8]
            xi[p, 32:40, :] = nothing

    def lateral(sign):
        base = 0 if sign < 0 else 2

        @pl.loop(0, 5)
        def _(g):
            at = pl.ds(pl.multiple_of(8 * g, 8), 8)
            values = []
            for p in range(16):
                value = (xr[p, at, :], xi[p, at, :])
                if sign > 0:
                    cos, sin = tw[base, p : p + 1, :], tw[base + 1, p : p + 1, :]
                    value = (value[0] * cos - value[1] * sin, value[1] * cos + value[0] * sin)
                values.append(value)
            for p, value in enumerate(short_transform(values, sign)):
                if sign < 0:
                    cos, sin = tw[base, p : p + 1, :], tw[base + 1, p : p + 1, :]
                    value = (value[0] * cos - value[1] * sin, value[1] * cos + value[0] * sin)
                xr[p, at, :] = value[0]
                xi[p, at, :] = value[1]

    def middle():
        lateral(-1)
        for b in range(4):
            some = pl.ds(4 * b, 4)
            both = jnp.concatenate([xr[some].reshape(160, 128), xi[some].reshape(160, 128)], axis=1)
            spectrum = jnp.dot(both.astype(BF16), xt[0:256, :], preferred_element_type=F32)
            re, im = spectrum[:, :128], spectrum[:, 128:]
            inverse = lax.rsqrt(jnp.maximum(re * re + im * im, 1e-30))
            factor = jnp.maximum(1.0 - level1[some].reshape(160, 128) * inverse, 0.0)
            factor += jnp.maximum(1.0 - level2[some].reshape(160, 128) * inverse, 0.0)
            both = jnp.concatenate([re * factor, im * factor], axis=1)
            inner = jnp.dot(both.astype(BF16), xt[256:512, :], preferred_element_type=F32)
            xr[some] = inner[:, :128].reshape(4, 40, 128)
            xi[some] = inner[:, 128:].reshape(4, 40, 128)
        lateral(1)

    def turn_back():
        for p in range(16):
            re, im = xr[p, 0:32, :], xi[p, 0:32, :]
            im = jnp.concatenate([jnp.where(packed, xr[p, 32:40, :], im[0:8]), im[8:32]], axis=0)
            back[2 * p] = jnp.where(low, re, pltpu.roll(im, 64, 1)).astype(BF16)
            back[2 * p + 1] = jnp.where(low, pltpu.roll(re, 64, 1), im).astype(BF16)

        @pl.loop(1, LAT)
        def _(k):
            second_copy((lat + k) % LAT).start()

        got[lat] = back[lat]
        all_but_one = got.at[pl.ds(0, LAT - 1)]
        pltpu.make_async_copy(all_but_one, all_but_one, second_r).wait()

    def columns_back():
        for s in range(4):
            tall = got[:, 16 * (s // 2) : 16 * (s // 2) + 16, :].astype(F32)
            flat = tall[:, 8 * (s % 2) : 8 * (s % 2) + 8, :].reshape(256, 128).T.astype(BF16)
            wide = jnp.concatenate([flat[:64], flat[64:]], axis=1)
            mid[s] = jnp.dot(wide, it[512 * s : 512 * s + 512, :], preferred_element_type=F32)

        @pl.loop(0, 8)
        def _(g):
            at = pl.ds(pl.multiple_of(8 * g, 8), 8)
            parts = [(mid[s, at, 0:256], mid[s, at, 256:512]) for s in range(4)]
            even, odd = real_eight_back(parts[0][0], parts[0][1], parts[1], parts[2], parts[3])
            for k in range(4):
                out[0, at, 256 * k : 256 * k + 256] = even[k] + odd[k]
                out[0, at, 1024 + 256 * k : 1280 + 256 * k] = even[k] - odd[k]

    def drain():
        for c in range(2, CHUNKS):
            for k in range(2):
                relay_copy(c, k).wait_send()
                side_copy(c, k).wait_send()
                final_copy(c, k).wait_send()
                cross_copy(c, k).wait_send()
        for c in range(2):
            for k in range(2):
                relay2_copy(c, k).wait_send()
                side2_copy(c, k).wait_send()
                final2_copy(c, k).wait_send()
                for j in range(4):
                    wide_copy(c, j, k).wait_send()
        sent = send.at[pl.ds(0, LAT - 1)]
        pltpu.make_async_copy(sent, sent, first_s).wait()
        sent = back.at[pl.ds(0, LAT - 1)]
        pltpu.make_async_copy(sent, sent, second_s).wait()
        for k in range(2):
            mirror_copy(k).wait_send()

        @pl.when(lat < 16)
        def _():
            corner_copy().wait_send()


    stack()
    columns()
    unpack()
    middle()
    turn_back()
    columns_back()
    drain()


def on_device(partials, wedges, levels):
    tables = [
        jnp.asarray(t)
        for t in (
            forward_tables(), inverse_tables(), lateral_tables(), turn_tables(), pick_tables(), lane_tables()
        )
    ]
    anywhere = pl.BlockSpec(memory_space=pltpu.HBM)
    vmem, dma = pltpu.VMEM, pltpu.SemaphoreType.DMA
    two = dma((CHUNKS, 2))
    doubled = pl.pallas_call(
        kernel,
        out_shape=jax.ShapeDtypeStruct((1, ROWS, N), F32),
        in_specs=[anywhere, anywhere, pl.BlockSpec(memory_space=pltpu.SMEM)] + [anywhere] * 6,
        out_specs=pl.BlockSpec(memory_space=pltpu.VMEM),
        scratch_shapes=[
            vmem(partials.shape, BF16),
            vmem(wedges.shape, jnp.int32),
            *[vmem(t.shape, t.dtype) for t in tables],
            vmem((CHUNKS, 2, CROWS, N), BF16),
            vmem((CHUNKS, 2, CROWS, N), BF16),
            vmem((CHUNKS, 2, CROWS, N), BF16),
            vmem((CHUNKS, 2, CROWS, N), BF16),
            vmem((2, 2, 4, CROWS, N), BF16),
            vmem((2, 4, CROWS, N), BF16),
            vmem((2, 2, CROWS, N // 2), BF16),
            vmem((2, 2, CROWS, N // 2), BF16),
            vmem((2, 2, CROWS, N // 2), BF16),
            vmem((128, 1024), BF16),
            vmem((3, 128, 512), BF16),
            vmem((LAT, 32, 128), BF16),
            vmem((LAT, 32, 128), BF16),
            vmem((16, 40, 128), F32),
            vmem((16, 40, 128), F32),
            vmem((16, 40, 128), F32),
            vmem((16, 40, 128), F32),
            vmem((16, 48, 128), BF16),
            vmem((16, 48, 128), BF16),
            vmem((16, 32, 128), BF16),
            vmem((16, 16, 128), BF16),
            vmem((LAT, 32, 128), BF16),
            vmem((LAT, 32, 128), BF16),
            vmem((4, ROWS, 512), F32),
            dma((CHUNKS,)),
            dma((7,)),
            two, two, two, two, two, two, two, two,
            dma, dma, dma, dma,
            dma((4,)),
            dma((4,)),
            dma((2, 4, 2)), dma((2, 4, 2)),
            dma((2, 2)), dma((2, 2)), dma((2, 2)), dma((2, 2)), dma((2, 2)), dma((2, 2)),
        ],
        compiler_params=pltpu.CompilerParams(
            collective_id=0, has_side_effects=True, vmem_limit_bytes=60 * 1024 * 1024
        ),
        name="stack_threshold",
    )(partials, wedges, levels, *tables)
    return doubled * 0.5


def solution(mesh):
    in_specs = (P("shot", None, "lat", None), P("lat", None), P())
    return jax.shard_map(
        on_device, mesh=mesh, in_specs=in_specs, out_specs=P("shot", "lat", None), check_vma=False
    )
```

```python
import functools
import math

import jax
import jax.numpy as jnp
import ml_dtypes
import numpy as np
from jax import lax
from jax.experimental import pallas as pl
from jax.experimental.pallas import tpu as pltpu
from jax.sharding import PartitionSpec as P

MESH = pl.DeviceIdType.MESH
F32 = jnp.float32
BF16 = jnp.bfloat16
N = 2048
LAT = 32
ROWS = N // LAT
CHUNKS = 4
CROWS = ROWS // CHUNKS
HALF = math.sqrt(0.5)
NT = (((1,), (1,)), ((), ()))


def owned():
    ky = np.zeros((LAT, 32), np.int64)
    for d in range(LAT):
        for i in range(8):
            for s in (1, 2, 3):
                ky[d, 8 * s + i] = 64 * d + 8 * i + s
        for i in range(4):
            ky[d, i] = 64 * d + 8 * i + 4
        for i in range(4, 7):
            ky[d, i] = 64 * d + 8 * (i - 3)
        ky[d, 7] = 64 * d + (32 if d < 16 else 0)
    return ky


def forward_tables():
    ky = owned()
    y2 = np.arange(256)
    scale = 1.0 / math.sqrt(N)
    parts = []
    for s in range(4):
        rows = ky[:, 8 * s : 8 * s + 8].reshape(-1)
        angle = 2.0 * np.pi * ((rows[:, None] * y2[None, :]) % N) / N
        re, im = np.cos(angle), -np.sin(angle)
        if s == 0:
            packed = 16 * 8 + 7
            re[packed] = np.where(y2 % 2, -1.0, 1.0)
            im[packed] = 1.0
            four = (rows % 8 == 4)[:, None]
            zero = np.zeros_like(re)
            parts += [
                np.where(four, zero, re),
                np.where(four, re, zero),
                np.where(four, zero, im),
                np.where(four, im, zero),
            ]
        else:
            parts += [re, im]
    return (np.concatenate(parts, axis=1) * scale).astype(ml_dtypes.bfloat16)


def inverse_tables():
    ky = owned()
    y2 = np.arange(256)
    scale = 2.0 / math.sqrt(N)
    parts = []
    for s in range(4):
        rows = ky[:, 8 * s : 8 * s + 8].reshape(-1)
        angle = 2.0 * np.pi * ((rows[:, None] * y2[None, :]) % N) / N
        cos, sin = 2.0 * np.cos(angle), 2.0 * np.sin(angle)
        if s == 0:
            packed = 16 * 8 + 7
            cos[packed] = np.where(y2 % 2, -1.0, 1.0)
            sin[packed] = -1.0
            four = (rows % 8 == 4)[:, None]
            zero = np.zeros_like(cos)
            top = np.concatenate([np.where(four, zero, cos), np.where(four, cos, zero)], axis=1)
            low = np.concatenate([np.where(four, zero, -sin), np.where(four, -sin, zero)], axis=1)
        else:
            top = np.concatenate([cos, sin], axis=1)
            low = np.concatenate([-sin, cos], axis=1)
        parts += [top, low]
    return (np.concatenate(parts, axis=0) * scale).astype(ml_dtypes.bfloat16)


def lateral_tables():
    index = np.arange(128)
    angle = 2.0 * np.pi * ((index[:, None] * index[None, :]) % 128) / 128
    cos, sin = np.cos(angle), np.sin(angle)
    forward = np.block([[cos, -sin], [sin, cos]])
    inverse = np.block([[cos, sin], [-sin, cos]])
    return np.concatenate([forward, inverse], axis=0).astype(ml_dtypes.bfloat16)


def turn_tables():
    angle = 2.0 * np.pi * (np.arange(16)[:, None] * np.arange(128)[None, :]) / N
    scale = 1.0 / math.sqrt(N)
    cos, sin = np.cos(angle) * scale, np.sin(angle) * scale
    return np.stack([cos, -sin, 0.5 * cos, 0.5 * sin]).astype(np.float32)


def pick_tables():
    own = np.zeros((48, 64))
    mirror = np.zeros((48, 64))
    for i in range(8):
        for s in (1, 2, 3):
            own[8 * s + i, 8 * i + s] = 1
            mirror[8 * s + i, 8 * (7 - i) + 8 - s] = 1
    for i in range(4):
        own[i, 8 * i + 4] = 1
        mirror[i, 8 * (7 - i) + 4] = 1
    for i in range(4, 7):
        own[i, 8 * (i - 3)] = 1
        mirror[i, 8 * (11 - i)] = 1
    own[7, 32] = mirror[7, 32] = 1
    own[39, 0] = mirror[39, 0] = 1
    return np.concatenate([own, mirror], axis=0).astype(ml_dtypes.bfloat16)


def lane_tables():
    lanes = np.arange(128)
    place = (lanes % 16) * 8 + lanes // 16
    own = np.zeros((128, 128))
    own[lanes, place] = 1
    mirror = np.zeros((256, 128))
    mirror[128 - lanes, place] = 1
    return np.concatenate([own, mirror], axis=0).astype(ml_dtypes.bfloat16)


def turn(pair, step, length, sign):
    re, im = pair
    step = step % length
    if step == 0:
        return pair
    if 4 * step == length:
        return (-im, re) if sign > 0 else (im, -re)
    if 8 * step == length:
        return ((re - sign * im) * HALF, (im + sign * re) * HALF)
    if 8 * step == 3 * length:
        return ((-re - sign * im) * HALF, (-im + sign * re) * HALF)
    cos = math.cos(2.0 * math.pi * step / length)
    sin = sign * math.sin(2.0 * math.pi * step / length)
    return (re * cos - im * sin, im * cos + re * sin)


def short_transform(values, sign):
    count = len(values)
    if count == 1:
        return values
    even = short_transform(values[0::2], sign)
    odd = short_transform(values[1::2], sign)
    low, high = [], []
    for k in range(count // 2):
        re, im = turn(odd[k], k, count, sign)
        low.append((even[k][0] + re, even[k][1] + im))
        high.append((even[k][0] - re, even[k][1] - im))
    return low + high


def real_eight(u):
    a = [u[k] + u[k + 4] for k in range(4)]
    b = [u[k] - u[k + 4] for k in range(4)]
    even, odd = a[0] + a[2], a[1] + a[3]
    minus, plus = (b[1] - b[3]) * HALF, (b[1] + b[3]) * HALF
    return (
        even + odd,
        even - odd,
        (b[0] + minus, -(b[2] + plus)),
        (a[0] - a[2], a[3] - a[1]),
        (b[0] - minus, b[2] - plus),
    )


def real_eight_back(zero, four, one, two, three):
    plus, minus = zero + four, zero - four
    (r1, i1), (r2, i2), (r3, i3) = one, two, three
    p0, p1 = plus + r2, plus - r2
    m0, m1 = minus - i2, minus + i2
    e0, e1 = r1 + r3, i3 - i1
    o0 = (r1 - i1 - r3 - i3) * HALF
    o1 = (r3 - i3 - r1 - i1) * HALF
    return (p0, m0, p1, m1), (e0, o0, e1, o1)


def spread(tiles, lane):
    for bit in (8, 4, 2, 1):
        high = (lane // 8) % (2 * bit) >= bit
        new = list(tiles)
        for t in range(16):
            if t & bit:
                continue
            first, second = tiles[t], tiles[t | bit]
            new[t] = jnp.where(high, pltpu.roll(second, 8 * bit, 1), first)
            new[t | bit] = jnp.where(high, second, pltpu.roll(first, 128 - 8 * bit, 1))
        tiles = new
    return tiles


def kernel(
    part_hbm, wedge_hbm, levels, ft_hbm, it_hbm, xt_hbm, tw_hbm, pick_hbm, lane_hbm,
    out,
    part, wedge, ft, it, xt, tw, pick, lanet,
    relay, side, final, cross, wide, total, relay2, side2, final2,
    folded0, folded1, send, held, xr, xi, level1, level2, own_ids, mir_ids, mir_in, spec_in, back, got, mid,
    load_sem, table_sem, relay_s, relay_r, side_s, side_r, final_s, final_r, cross_s, cross_r,
    first_s, first_r, second_s, second_r, wedge_s, wedge_r,
    wide_s, wide_r, relay2_s, relay2_r, side2_s, side2_r, final2_s, final2_r,
):
    shot = lax.axis_index("shot")
    lat = lax.axis_index("lat")
    n_shot = lax.axis_size("shot")
    y, xh = shot // 2, shot % 2
    up, down = (shot + 2) % n_shot, (shot + n_shot - 2) % n_shot
    y_up, y_down, y_far = (y + 1) % 4, (y + 3) % 4, (y + 2) % 4
    flip = lat + 2 - 4 * ((lat // 2) % 2)
    other = shot + 1 - 2 * xh

    def rows(c):
        return pl.ds(c * CROWS, CROWS)

    loads = [
        pltpu.make_async_copy(
            part_hbm.at[:, :, rows(c), :], part.at[:, :, rows(c), :], load_sem.at[c]
        )
        for c in range(CHUNKS)
    ]
    loads[0].start()
    tables = [
        pltpu.make_async_copy(src, dst, table_sem.at[k])
        for k, (src, dst) in enumerate(
            [(wedge_hbm, wedge), (pick_hbm, pick), (lane_hbm, lanet), (ft_hbm, ft),
             (xt_hbm, xt), (tw_hbm, tw), (it_hbm, it)]
        )
    ]
    for c in (2, 1, 3):
        loads[c].start()
    for copy in tables:
        copy.start()

    barrier = pltpu.get_barrier_semaphore()

    def greet(s, l):
        pl.semaphore_signal(barrier, inc=1, device_id=(s, l), device_id_type=MESH)

    @pl.loop(1, LAT)
    def _(k):
        greet(shot, (lat + k) % LAT)

    greet(up, lat)
    greet(down, lat)
    greet(other, flip)

    def copy_to(src, dst, s_sem, r_sem, s, l):
        return pltpu.make_async_remote_copy(
            src_ref=src, dst_ref=dst, send_sem=s_sem, recv_sem=r_sem, device_id=(s, l), device_id_type=MESH
        )

    def slab(q, c):
        return part.at[0, q, rows(c), :]

    def relay_copy(c, k):
        q = 2 * y_far + k
        return copy_to(
            slab(q, c), relay.at[c, k], relay_s.at[c, k], relay_r.at[c, k], up if k == 0 else down, lat
        )

    def side_copy(c, k):
        q = 2 * y_up + 1 if k == 0 else 2 * y_down
        return copy_to(
            slab(q, c), side.at[c, k], side_s.at[c, k], side_r.at[c, k], up if k == 0 else down, lat
        )

    def final_copy(c, k):
        q = 2 * y_up if k == 0 else 2 * y_down + 1
        return copy_to(
            slab(q, c), final.at[c, k], final_s.at[c, k], final_r.at[c, k], up if k == 0 else down, lat
        )

    def cross_copy(c, h):
        return copy_to(
            slab(2 * y + h, c), cross.at[c, xh], cross_s.at[c, h], cross_r.at[c, xh], 2 * y + h, flip
        )

    def pair(q, c):
        return part[0, q, rows(c), :].astype(F32) + part[1, q, rows(c), :].astype(F32)

    def prepare(c):
        loads[c].wait()
        for q in (2 * y_far, 2 * y_far + 1, 2 * y_up + 1, 2 * y_down):
            part[0, q, rows(c), :] = pair(q, c).astype(BF16)

    def launch(c):
        for k in range(2):
            relay_copy(c, k).start()
        for k in range(2):
            side_copy(c, k).start()

    def begin(c):
        prepare(c)
        launch(c)

    def forward(c):
        for k in range(2):
            q = 2 * y_up if k == 0 else 2 * y_down + 1
            relay_copy(c, k).wait_recv()
            part[0, q, rows(c), :] = (pair(q, c) + relay[c, k].astype(F32)).astype(BF16)
            final_copy(c, k).start()

    def across(c):
        for k in range(2):
            side_copy(c, k).wait_recv()
            final_copy(c, k).wait_recv()
        for h in range(2):
            q = 2 * y + h
            total = pair(q, c) + final[c, h].astype(F32) + side[c, 1 - h].astype(F32)
            part[0, q, rows(c), :] = total.astype(BF16)
            cross_copy(c, h).start()

    def fold(c):
        for h in range(2):
            pltpu.make_async_copy(cross.at[c, h], cross.at[c, h], cross_r.at[c, h]).wait()
        u = []
        for k in range(8):
            cols = pl.ds(256 * k, 256)
            u.append(cross[c, 0, :, cols].astype(F32) + cross[c, 1, :, cols].astype(F32))
        keep(c, u)

    def keep(c, u):
        top, low = pl.ds(c * CROWS, CROWS), pl.ds(ROWS + c * CROWS, CROWS)
        zero, four, one, two, three = real_eight(u)
        zero, four = zero.astype(BF16), four.astype(BF16)
        blank = jnp.zeros((CROWS, 512), BF16)
        folded0[top, 0:256] = zero
        folded0[top, 256:512] = four
        folded0[top, 512:1024] = blank
        folded0[low, 0:512] = blank
        folded0[low, 512:768] = zero
        folded0[low, 768:1024] = four
        for s, (re, im) in enumerate((one, two, three)):
            re, im, neg = re.astype(BF16), im.astype(BF16), (-im).astype(BF16)
            folded1[s, top, 0:256] = re
            folded1[s, top, 256:512] = neg
            folded1[s, low, 0:256] = im
            folded1[s, low, 256:512] = re

    halves = (pl.ds(0, N // 2), pl.ds(N // 2, N // 2))
    y_order = (y_far, y_up, y_down, y)

    def wide_copy(c, j, h):
        return copy_to(
            slab(2 * y_order[j] + h, c), wide.at[c, xh, j], wide_s.at[c, j, h], wide_r.at[c, j, xh],
            2 * y + h, flip,
        )

    def wide_prepare(c, j):
        for h in range(2):
            q = 2 * y_order[j] + h
            part[0, q, rows(c), :] = pair(q, c).astype(BF16)

    def wide_launch(c, j):
        for h in range(2):
            wide_copy(c, j, h).start()

    def wide_sum(c, j):
        for h in range(2):
            pltpu.make_async_copy(wide.at[c, h, j], wide.at[c, h, j], wide_r.at[c, j, h]).wait()
        return wide[c, 0, j].astype(F32) + wide[c, 1, j].astype(F32)

    def half_copy(c, k, j, half, target, s_sem, r_sem):
        return copy_to(
            total.at[c, j, :, halves[half]], target.at[c, k], s_sem.at[c, k], r_sem.at[c, k],
            up if k == 0 else down, lat,
        )

    def relay2_copy(c, k):
        return half_copy(c, k, 0, k, relay2, relay2_s, relay2_r)

    def side2_copy(c, k):
        return half_copy(c, k, 1 + k, 1 - k, side2, side2_s, side2_r)

    def final2_copy(c, k):
        return half_copy(c, k, 1 + k, k, final2, final2_s, final2_r)

    def wide_relay(c):
        total[c, 0] = wide_sum(c, 0).astype(BF16)
        for k in range(2):
            relay2_copy(c, k).start()

    def wide_side(c):
        for k in range(2):
            total[c, 1 + k] = wide_sum(c, 1 + k).astype(BF16)
            side2_copy(c, k).start()

    def wide_final(c):
        for k in range(2):
            relay2_copy(c, k).wait_recv()
            both = wide[c, 0, 1 + k, :, halves[k]].astype(F32) + wide[c, 1, 1 + k, :, halves[k]].astype(F32)
            total[c, 1 + k, :, halves[k]] = (both + relay2[c, k].astype(F32)).astype(BF16)
            final2_copy(c, k).start()

    def wide_fold(c):
        mine = wide_sum(c, 3)
        for k in range(2):
            side2_copy(c, k).wait_recv()
            final2_copy(c, k).wait_recv()
        u = []
        for k in range(8):
            half, cols = k // 4, pl.ds(256 * (k % 4), 256)
            u.append(
                mine[:, 256 * k : 256 * k + 256]
                + final2[c, half, :, cols].astype(F32)
                + side2[c, 1 - half, :, cols].astype(F32)
            )
        keep(c, u)

    def first_copy(dest):
        return copy_to(send.at[dest], held.at[flip], first_s, first_r, shot, dest)

    def second_copy(dest):
        return copy_to(back.at[dest], got.at[lat], second_s, second_r, shot, dest)

    lane = lax.broadcasted_iota(jnp.int32, (1, 128), 1)
    low = lane < 64
    packed = (lax.broadcasted_iota(jnp.int32, (8, 128), 0) == 7) & (lat == 16)
    seventh = lax.broadcasted_iota(jnp.int32, (8, 128), 0) == 7

    partner = LAT - 1 - lat
    corner = jnp.where(lat == 0, 16, LAT - lat)

    def mirror_copy():
        return copy_to(
            mir_ids.at[:, pl.ds(0, 32), :], mir_in, wedge_s.at[1], wedge_r.at[1], shot, partner
        )

    def corner_copy():
        return copy_to(
            mir_ids.at[:, pl.ds(32, 16), :], spec_in, wedge_s.at[0], wedge_r.at[0], shot, corner
        )

    def wedges_out():
        for k in range(3):
            tables[k].wait()
        ids = wedge[...].astype(F32).astype(BF16)
        chosen = jnp.dot(pick[...], ids, preferred_element_type=F32).astype(BF16)
        own, mir = chosen[:48], chosen[48:]
        tall = jnp.concatenate([own[:, 128 * t : 128 * t + 128] for t in range(16)], axis=0)
        moved = jnp.dot(tall, lanet[0:128, :], preferred_element_type=F32)
        own_tiles = spread([moved[48 * t : 48 * t + 48] for t in range(16)], lane)
        for t, tile in enumerate(own_tiles):
            own_ids[t] = tile.astype(BF16)
        tall = jnp.concatenate(
            [
                jnp.concatenate(
                    [mir[:, 128 * (15 - t) : 128 * (16 - t)],
                     mir[:, 128 * ((16 - t) % 16) : 128 * ((16 - t) % 16) + 128]],
                    axis=1,
                )
                for t in range(16)
            ],
            axis=0,
        )
        moved = jnp.dot(tall, lanet[128:384, :], preferred_element_type=F32)
        for t, tile in enumerate(spread([moved[48 * t : 48 * t + 48] for t in range(16)], lane)):
            mir_ids[t] = jnp.concatenate([tile[:40], own_tiles[t][32:40]], axis=0).astype(BF16)

    def wedges_go():
        mirror_copy().start()

        @pl.when(lat < 16)
        def _():
            corner_copy().start()

    def look_up(ids):
        found = jnp.full(ids.shape, levels[0], F32)
        for w in range(1, 16):
            found = jnp.where(ids == float(w), levels[w], found)
        return found

    def wedges_in():
        mirror_copy().wait_recv()

        @pl.when(lat >= 16)
        def _():
            corner_copy().wait_recv()

        @pl.loop(0, 16)
        def _(kk):
            own = own_ids[kk].astype(F32)
            mir = mir_ids[kk].astype(F32)
            got_mir = mir_in[kk].astype(F32)
            spec = spec_in[kk].astype(F32)
            spec_mir, spec_own = spec[0:8], spec[8:16]
            level1[kk, 0:8, :] = look_up(jnp.where(seventh & (lat >= 16), own[32:40], own[0:8]))
            level1[kk, 8:32, :] = look_up(own[8:32])
            level1[kk, 32:40, :] = look_up(spec_own)
            row = jnp.where(lat == 16, mir[32:40], spec_mir)
            level2[kk, 0:8, :] = look_up(jnp.where(seventh & (lat >= 16), row, got_mir[0:8]))
            level2[kk, 8:32, :] = look_up(got_mir[8:32])
            level2[kk, 32:40, :] = look_up(spec_mir)

    def stack():
        loads[0].wait()
        wide_prepare(0, 0)
        pl.semaphore_wait(barrier, LAT + 2)
        wide_launch(0, 0)
        wide_prepare(0, 1)
        wide_launch(0, 1)
        begin(2)
        for j in (2, 3):
            wide_prepare(0, j)
            wide_launch(0, j)
        loads[1].wait()
        for j in range(4):
            wide_prepare(1, j)
            wide_launch(1, j)
        begin(3)
        wedges_out()
        wedges_go()
        forward(2)
        forward(3)
        wide_relay(0)
        wide_side(0)
        across(2)
        across(3)
        wide_final(0)
        wide_relay(1)
        wide_side(1)
        wide_final(1)
        wide_fold(0)
        for k in range(3, 7):
            tables[k].wait()
        wide_fold(1)
        fold(2)
        fold(3)

    def columns():
        pieces = [
            lax.dot_general(ft[:, 0:1024], folded0[...], NT, preferred_element_type=F32).reshape(LAT, 8, 128)
        ]
        for s in range(3):
            pieces.append(
                lax.dot_general(
                    ft[:, 1024 + 512 * s : 1536 + 512 * s], folded1[s], NT, preferred_element_type=F32
                ).reshape(LAT, 8, 128)
            )
        for k in range(2):
            both = jnp.concatenate([pieces[2 * k], pieces[2 * k + 1]], axis=1)
            send[:, 16 * k : 16 * k + 16, :] = both.astype(BF16)

        @pl.loop(1, LAT)
        def _(k):
            first_copy((lat + k) % LAT).start()

        held[flip] = send[lat]
        wedges_in()
        all_but_one = held.at[pl.ds(0, LAT - 1)]
        pltpu.make_async_copy(all_but_one, all_but_one, first_r).wait()

    def unpack():
        nothing = jnp.zeros((8, 128), F32)
        for p in range(16):
            u0, u1 = held[2 * p].astype(F32), held[2 * p + 1].astype(F32)
            re = jnp.where(low, u0, pltpu.roll(u1, 64, 1))
            im = jnp.where(low, pltpu.roll(u0, 64, 1), u1)
            xr[p, 0:32, :] = re
            xi[p, 0:8, :] = jnp.where(packed, 0.0, im[0:8])
            xi[p, 8:32, :] = im[8:32]
            xr[p, 32:40, :] = im[0:8]
            xi[p, 32:40, :] = nothing

    def lateral(sign):
        base = 0 if sign < 0 else 2

        @pl.loop(0, 5)
        def _(g):
            at = pl.ds(pl.multiple_of(8 * g, 8), 8)
            values = []
            for p in range(16):
                value = (xr[p, at, :], xi[p, at, :])
                if sign > 0:
                    cos, sin = tw[base, p : p + 1, :], tw[base + 1, p : p + 1, :]
                    value = (value[0] * cos - value[1] * sin, value[1] * cos + value[0] * sin)
                values.append(value)
            for p, value in enumerate(short_transform(values, sign)):
                if sign < 0:
                    cos, sin = tw[base, p : p + 1, :], tw[base + 1, p : p + 1, :]
                    value = (value[0] * cos - value[1] * sin, value[1] * cos + value[0] * sin)
                xr[p, at, :] = value[0]
                xi[p, at, :] = value[1]

    def middle():
        lateral(-1)
        for b in range(4):
            some = pl.ds(4 * b, 4)
            both = jnp.concatenate([xr[some].reshape(160, 128), xi[some].reshape(160, 128)], axis=1)
            spectrum = jnp.dot(both.astype(BF16), xt[0:256, :], preferred_element_type=F32)
            re, im = spectrum[:, :128], spectrum[:, 128:]
            inverse = lax.rsqrt(jnp.maximum(re * re + im * im, 1e-30))
            factor = jnp.maximum(1.0 - level1[some].reshape(160, 128) * inverse, 0.0)
            factor += jnp.maximum(1.0 - level2[some].reshape(160, 128) * inverse, 0.0)
            both = jnp.concatenate([re * factor, im * factor], axis=1)
            inner = jnp.dot(both.astype(BF16), xt[256:512, :], preferred_element_type=F32)
            xr[some] = inner[:, :128].reshape(4, 40, 128)
            xi[some] = inner[:, 128:].reshape(4, 40, 128)
        lateral(1)

    def turn_back():
        for p in range(16):
            re, im = xr[p, 0:32, :], xi[p, 0:32, :]
            im = jnp.concatenate([jnp.where(packed, xr[p, 32:40, :], im[0:8]), im[8:32]], axis=0)
            back[2 * p] = jnp.where(low, re, pltpu.roll(im, 64, 1)).astype(BF16)
            back[2 * p + 1] = jnp.where(low, pltpu.roll(re, 64, 1), im).astype(BF16)

        @pl.loop(1, LAT)
        def _(k):
            second_copy((lat + k) % LAT).start()

        got[lat] = back[lat]
        all_but_one = got.at[pl.ds(0, LAT - 1)]
        pltpu.make_async_copy(all_but_one, all_but_one, second_r).wait()

    def columns_back():
        for s in range(4):
            tall = got[:, 16 * (s // 2) : 16 * (s // 2) + 16, :].astype(F32)
            flat = tall[:, 8 * (s % 2) : 8 * (s % 2) + 8, :].reshape(256, 128).T.astype(BF16)
            wide = jnp.concatenate([flat[:64], flat[64:]], axis=1)
            mid[s] = jnp.dot(wide, it[512 * s : 512 * s + 512, :], preferred_element_type=F32)

        @pl.loop(0, 8)
        def _(g):
            at = pl.ds(pl.multiple_of(8 * g, 8), 8)
            parts = [(mid[s, at, 0:256], mid[s, at, 256:512]) for s in range(4)]
            even, odd = real_eight_back(parts[0][0], parts[0][1], parts[1], parts[2], parts[3])
            for k in range(4):
                out[0, at, 256 * k : 256 * k + 256] = even[k] + odd[k]
                out[0, at, 1024 + 256 * k : 1280 + 256 * k] = even[k] - odd[k]

    def drain():
        for c in range(2, CHUNKS):
            for k in range(2):
                relay_copy(c, k).wait_send()
                side_copy(c, k).wait_send()
                final_copy(c, k).wait_send()
                cross_copy(c, k).wait_send()
        for c in range(2):
            for k in range(2):
                relay2_copy(c, k).wait_send()
                side2_copy(c, k).wait_send()
                final2_copy(c, k).wait_send()
                for j in range(4):
                    wide_copy(c, j, k).wait_send()
        sent = send.at[pl.ds(0, LAT - 1)]
        pltpu.make_async_copy(sent, sent, first_s).wait()
        sent = back.at[pl.ds(0, LAT - 1)]
        pltpu.make_async_copy(sent, sent, second_s).wait()
        mirror_copy().wait_send()

        @pl.when(lat < 16)
        def _():
            corner_copy().wait_send()


    stack()
    columns()
    unpack()
    middle()
    turn_back()
    columns_back()
    drain()


def on_device(partials, wedges, levels):
    tables = [
        jnp.asarray(t)
        for t in (
            forward_tables(), inverse_tables(), lateral_tables(), turn_tables(), pick_tables(), lane_tables()
        )
    ]
    anywhere = pl.BlockSpec(memory_space=pltpu.HBM)
    vmem, dma = pltpu.VMEM, pltpu.SemaphoreType.DMA
    two = dma((CHUNKS, 2))
    doubled = pl.pallas_call(
        kernel,
        out_shape=jax.ShapeDtypeStruct((1, ROWS, N), F32),
        in_specs=[anywhere, anywhere, pl.BlockSpec(memory_space=pltpu.SMEM)] + [anywhere] * 6,
        out_specs=pl.BlockSpec(memory_space=pltpu.VMEM),
        scratch_shapes=[
            vmem(partials.shape, BF16),
            vmem(wedges.shape, jnp.int32),
            *[vmem(t.shape, t.dtype) for t in tables],
            vmem((CHUNKS, 2, CROWS, N), BF16),
            vmem((CHUNKS, 2, CROWS, N), BF16),
            vmem((CHUNKS, 2, CROWS, N), BF16),
            vmem((CHUNKS, 2, CROWS, N), BF16),
            vmem((2, 2, 4, CROWS, N), BF16),
            vmem((2, 4, CROWS, N), BF16),
            vmem((2, 2, CROWS, N // 2), BF16),
            vmem((2, 2, CROWS, N // 2), BF16),
            vmem((2, 2, CROWS, N // 2), BF16),
            vmem((128, 1024), BF16),
            vmem((3, 128, 512), BF16),
            vmem((LAT, 32, 128), BF16),
            vmem((LAT, 32, 128), BF16),
            vmem((16, 40, 128), F32),
            vmem((16, 40, 128), F32),
            vmem((16, 40, 128), F32),
            vmem((16, 40, 128), F32),
            vmem((16, 48, 128), BF16),
            vmem((16, 48, 128), BF16),
            vmem((16, 32, 128), BF16),
            vmem((16, 16, 128), BF16),
            vmem((LAT, 32, 128), BF16),
            vmem((LAT, 32, 128), BF16),
            vmem((4, ROWS, 512), F32),
            dma((CHUNKS,)),
            dma((7,)),
            two, two, two, two, two, two, two, two,
            dma, dma, dma, dma,
            dma((2,)),
            dma((2,)),
            dma((2, 4, 2)), dma((2, 4, 2)),
            dma((2, 2)), dma((2, 2)), dma((2, 2)), dma((2, 2)), dma((2, 2)), dma((2, 2)),
        ],
        compiler_params=pltpu.CompilerParams(
            collective_id=0, has_side_effects=True, vmem_limit_bytes=60 * 1024 * 1024
        ),
        name="stack_threshold",
    )(partials, wedges, levels, *tables)
    return doubled * 0.5


def solution(mesh):
    in_specs = (P("shot", None, "lat", None), P("lat", None), P())
    return jax.shard_map(
        on_device, mesh=mesh, in_specs=in_specs, out_specs=P("shot", "lat", None), check_vma=False
    )
```

```python
import functools
import math

import jax
import jax.numpy as jnp
import ml_dtypes
import numpy as np
from jax import lax
from jax.experimental import pallas as pl
from jax.experimental.pallas import tpu as pltpu
from jax.sharding import PartitionSpec as P

MESH = pl.DeviceIdType.MESH
F32 = jnp.float32
BF16 = jnp.bfloat16
N = 2048
LAT = 32
ROWS = N // LAT
CHUNKS = 4
CROWS = ROWS // CHUNKS
HALF = math.sqrt(0.5)
NT = (((1,), (1,)), ((), ()))


def owned():
    ky = np.zeros((LAT, 32), np.int64)
    for d in range(LAT):
        for i in range(8):
            for s in (1, 2, 3):
                ky[d, 8 * s + i] = 64 * d + 8 * i + s
        for i in range(4):
            ky[d, i] = 64 * d + 8 * i + 4
        for i in range(4, 7):
            ky[d, i] = 64 * d + 8 * (i - 3)
        ky[d, 7] = 64 * d + (32 if d < 16 else 0)
    return ky


def forward_tables():
    ky = owned()
    y2 = np.arange(256)
    scale = 1.0 / math.sqrt(N)
    parts = []
    for s in range(4):
        rows = ky[:, 8 * s : 8 * s + 8].reshape(-1)
        angle = 2.0 * np.pi * ((rows[:, None] * y2[None, :]) % N) / N
        re, im = np.cos(angle), -np.sin(angle)
        if s == 0:
            packed = 16 * 8 + 7
            re[packed] = np.where(y2 % 2, -1.0, 1.0)
            im[packed] = 1.0
            four = (rows % 8 == 4)[:, None]
            zero = np.zeros_like(re)
            parts += [
                np.where(four, zero, re),
                np.where(four, re, zero),
                np.where(four, zero, im),
                np.where(four, im, zero),
            ]
        else:
            parts += [re, im]
    return (np.concatenate(parts, axis=1) * scale).astype(ml_dtypes.bfloat16)


def inverse_tables():
    ky = owned()
    y2 = np.arange(256)
    scale = 2.0 / math.sqrt(N)
    parts = []
    for s in range(4):
        rows = ky[:, 8 * s : 8 * s + 8].reshape(-1)
        angle = 2.0 * np.pi * ((rows[:, None] * y2[None, :]) % N) / N
        cos, sin = 2.0 * np.cos(angle), 2.0 * np.sin(angle)
        if s == 0:
            packed = 16 * 8 + 7
            cos[packed] = np.where(y2 % 2, -1.0, 1.0)
            sin[packed] = -1.0
            four = (rows % 8 == 4)[:, None]
            zero = np.zeros_like(cos)
            top = np.concatenate([np.where(four, zero, cos), np.where(four, cos, zero)], axis=1)
            low = np.concatenate([np.where(four, zero, -sin), np.where(four, -sin, zero)], axis=1)
        else:
            top = np.concatenate([cos, sin], axis=1)
            low = np.concatenate([-sin, cos], axis=1)
        parts += [top, low]
    return (np.concatenate(parts, axis=0) * scale).astype(ml_dtypes.bfloat16)


def lateral_tables():
    index = np.arange(128)
    angle = 2.0 * np.pi * ((index[:, None] * index[None, :]) % 128) / 128
    cos, sin = np.cos(angle), np.sin(angle)
    forward = np.block([[cos, -sin], [sin, cos]])
    inverse = np.block([[cos, sin], [-sin, cos]])
    return np.concatenate([forward, inverse], axis=0).astype(ml_dtypes.bfloat16)


def turn_tables():
    angle = 2.0 * np.pi * (np.arange(16)[:, None] * np.arange(128)[None, :]) / N
    scale = 1.0 / math.sqrt(N)
    cos, sin = np.cos(angle) * scale, np.sin(angle) * scale
    return np.stack([cos, -sin, 0.5 * cos, 0.5 * sin]).astype(np.float32)


def pick_tables():
    own = np.zeros((48, 64))
    mirror = np.zeros((48, 64))
    for i in range(8):
        for s in (1, 2, 3):
            own[8 * s + i, 8 * i + s] = 1
            mirror[8 * s + i, 8 * (7 - i) + 8 - s] = 1
    for i in range(4):
        own[i, 8 * i + 4] = 1
        mirror[i, 8 * (7 - i) + 4] = 1
    for i in range(4, 7):
        own[i, 8 * (i - 3)] = 1
        mirror[i, 8 * (11 - i)] = 1
    own[7, 32] = mirror[7, 32] = 1
    own[39, 0] = mirror[39, 0] = 1
    return np.concatenate([own, mirror], axis=0).astype(ml_dtypes.bfloat16)


def lane_tables():
    lanes = np.arange(128)
    place = (lanes % 16) * 8 + lanes // 16
    own = np.zeros((128, 128))
    own[lanes, place] = 1
    mirror = np.zeros((256, 128))
    mirror[128 - lanes, place] = 1
    return np.concatenate([own, mirror], axis=0).astype(ml_dtypes.bfloat16)


def turn(pair, step, length, sign):
    re, im = pair
    step = step % length
    if step == 0:
        return pair
    if 4 * step == length:
        return (-im, re) if sign > 0 else (im, -re)
    if 8 * step == length:
        return ((re - sign * im) * HALF, (im + sign * re) * HALF)
    if 8 * step == 3 * length:
        return ((-re - sign * im) * HALF, (-im + sign * re) * HALF)
    cos = math.cos(2.0 * math.pi * step / length)
    sin = sign * math.sin(2.0 * math.pi * step / length)
    return (re * cos - im * sin, im * cos + re * sin)


def short_transform(values, sign):
    count = len(values)
    if count == 1:
        return values
    even = short_transform(values[0::2], sign)
    odd = short_transform(values[1::2], sign)
    low, high = [], []
    for k in range(count // 2):
        re, im = turn(odd[k], k, count, sign)
        low.append((even[k][0] + re, even[k][1] + im))
        high.append((even[k][0] - re, even[k][1] - im))
    return low + high


def real_eight(u):
    a = [u[k] + u[k + 4] for k in range(4)]
    b = [u[k] - u[k + 4] for k in range(4)]
    even, odd = a[0] + a[2], a[1] + a[3]
    minus, plus = (b[1] - b[3]) * HALF, (b[1] + b[3]) * HALF
    return (
        even + odd,
        even - odd,
        (b[0] + minus, -(b[2] + plus)),
        (a[0] - a[2], a[3] - a[1]),
        (b[0] - minus, b[2] - plus),
    )


def real_eight_back(zero, four, one, two, three):
    plus, minus = zero + four, zero - four
    (r1, i1), (r2, i2), (r3, i3) = one, two, three
    p0, p1 = plus + r2, plus - r2
    m0, m1 = minus - i2, minus + i2
    e0, e1 = r1 + r3, i3 - i1
    o0 = (r1 - i1 - r3 - i3) * HALF
    o1 = (r3 - i3 - r1 - i1) * HALF
    return (p0, m0, p1, m1), (e0, o0, e1, o1)


def spread(tiles, lane):
    for bit in (8, 4, 2, 1):
        high = (lane // 8) % (2 * bit) >= bit
        new = list(tiles)
        for t in range(16):
            if t & bit:
                continue
            first, second = tiles[t], tiles[t | bit]
            new[t] = jnp.where(high, pltpu.roll(second, 8 * bit, 1), first)
            new[t | bit] = jnp.where(high, second, pltpu.roll(first, 128 - 8 * bit, 1))
        tiles = new
    return tiles


def kernel(
    part_hbm, wedge_hbm, levels, ft_hbm, it_hbm, xt_hbm, tw_hbm, pick_hbm, lane_hbm,
    out,
    part, wedge, ft, it, xt, tw, pick, lanet,
    relay, side, final, cross, wide, total, relay2, side2, final2,
    folded0, folded1, send, held, xr, xi, level1, level2, own_ids, mir_ids, mir_in, spec_in, back, got, mid,
    load_sem, table_sem, relay_s, relay_r, side_s, side_r, final_s, final_r, cross_s, cross_r,
    first_s, first_r, second_s, second_r, wedge_s, wedge_r,
    wide_s, wide_r, relay2_s, relay2_r, side2_s, side2_r, final2_s, final2_r,
):
    shot = lax.axis_index("shot")
    lat = lax.axis_index("lat")
    n_shot = lax.axis_size("shot")
    y, xh = shot // 2, shot % 2
    up, down = (shot + 2) % n_shot, (shot + n_shot - 2) % n_shot
    y_up, y_down, y_far = (y + 1) % 4, (y + 3) % 4, (y + 2) % 4
    flip = lat + 2 - 4 * ((lat // 2) % 2)
    other = shot + 1 - 2 * xh

    def rows(c):
        return pl.ds(c * CROWS, CROWS)

    loads = [
        pltpu.make_async_copy(
            part_hbm.at[:, :, rows(c), :], part.at[:, :, rows(c), :], load_sem.at[c]
        )
        for c in range(CHUNKS)
    ]
    loads[0].start()
    tables = [
        pltpu.make_async_copy(src, dst, table_sem.at[k])
        for k, (src, dst) in enumerate(
            [(wedge_hbm, wedge), (pick_hbm, pick), (lane_hbm, lanet), (ft_hbm, ft),
             (xt_hbm, xt), (tw_hbm, tw), (it_hbm, it)]
        )
    ]
    for c in (2, 1, 3):
        loads[c].start()
    for copy in tables:
        copy.start()

    barrier = pltpu.get_barrier_semaphore()

    def greet(s, l):
        pl.semaphore_signal(barrier, inc=1, device_id=(s, l), device_id_type=MESH)

    @pl.loop(1, LAT)
    def _(k):
        greet(shot, (lat + k) % LAT)

    greet(up, lat)
    greet(down, lat)
    greet(other, flip)

    def copy_to(src, dst, s_sem, r_sem, s, l):
        return pltpu.make_async_remote_copy(
            src_ref=src, dst_ref=dst, send_sem=s_sem, recv_sem=r_sem, device_id=(s, l), device_id_type=MESH
        )

    def slab(q, c):
        return part.at[0, q, rows(c), :]

    def relay_copy(c, k):
        q = 2 * y_far + k
        return copy_to(
            slab(q, c), relay.at[c, k], relay_s.at[c, k], relay_r.at[c, k], up if k == 0 else down, lat
        )

    def side_copy(c, k):
        q = 2 * y_up + 1 if k == 0 else 2 * y_down
        return copy_to(
            slab(q, c), side.at[c, k], side_s.at[c, k], side_r.at[c, k], up if k == 0 else down, lat
        )

    def final_copy(c, k):
        q = 2 * y_up if k == 0 else 2 * y_down + 1
        return copy_to(
            slab(q, c), final.at[c, k], final_s.at[c, k], final_r.at[c, k], up if k == 0 else down, lat
        )

    def cross_copy(c, h):
        return copy_to(
            slab(2 * y + h, c), cross.at[c, xh], cross_s.at[c, h], cross_r.at[c, xh], 2 * y + h, flip
        )

    def pair(q, c):
        return part[0, q, rows(c), :].astype(F32) + part[1, q, rows(c), :].astype(F32)

    def prepare(c):
        loads[c].wait()
        for q in (2 * y_far, 2 * y_far + 1, 2 * y_up + 1, 2 * y_down):
            part[0, q, rows(c), :] = pair(q, c).astype(BF16)

    def launch(c):
        for k in range(2):
            relay_copy(c, k).start()
        for k in range(2):
            side_copy(c, k).start()

    def begin(c):
        prepare(c)
        launch(c)

    def forward(c):
        for k in range(2):
            q = 2 * y_up if k == 0 else 2 * y_down + 1
            relay_copy(c, k).wait_recv()
            part[0, q, rows(c), :] = (pair(q, c) + relay[c, k].astype(F32)).astype(BF16)
            final_copy(c, k).start()

    def across(c):
        for k in range(2):
            side_copy(c, k).wait_recv()
            final_copy(c, k).wait_recv()
        for h in range(2):
            q = 2 * y + h
            total = pair(q, c) + final[c, h].astype(F32) + side[c, 1 - h].astype(F32)
            part[0, q, rows(c), :] = total.astype(BF16)
            cross_copy(c, h).start()

    def fold(c):
        for h in range(2):
            pltpu.make_async_copy(cross.at[c, h], cross.at[c, h], cross_r.at[c, h]).wait()
        u = []
        for k in range(8):
            cols = pl.ds(256 * k, 256)
            u.append(cross[c, 0, :, cols].astype(F32) + cross[c, 1, :, cols].astype(F32))
        keep(c, u)

    def keep(c, u):
        top, low = pl.ds(c * CROWS, CROWS), pl.ds(ROWS + c * CROWS, CROWS)
        zero, four, one, two, three = real_eight(u)
        zero, four = zero.astype(BF16), four.astype(BF16)
        blank = jnp.zeros((CROWS, 512), BF16)
        folded0[top, 0:256] = zero
        folded0[top, 256:512] = four
        folded0[top, 512:1024] = blank
        folded0[low, 0:512] = blank
        folded0[low, 512:768] = zero
        folded0[low, 768:1024] = four
        for s, (re, im) in enumerate((one, two, three)):
            re, im, neg = re.astype(BF16), im.astype(BF16), (-im).astype(BF16)
            folded1[s, top, 0:256] = re
            folded1[s, top, 256:512] = neg
            folded1[s, low, 0:256] = im
            folded1[s, low, 256:512] = re

    halves = (pl.ds(0, N // 2), pl.ds(N // 2, N // 2))
    y_order = (y_far, y_up, y_down, y)

    def wide_copy(c, j, h):
        return copy_to(
            slab(2 * y_order[j] + h, c), wide.at[c, xh, j], wide_s.at[c, j, h], wide_r.at[c, j, xh],
            2 * y + h, flip,
        )

    def wide_prepare(c):
        loads[c].wait()
        for q in range(8):
            part[0, q, rows(c), :] = pair(q, c).astype(BF16)

    def wide_launch(c):
        for j in range(4):
            for h in range(2):
                wide_copy(c, j, h).start()

    def wide_sum(c, j):
        for h in range(2):
            pltpu.make_async_copy(wide.at[c, h, j], wide.at[c, h, j], wide_r.at[c, j, h]).wait()
        return wide[c, 0, j].astype(F32) + wide[c, 1, j].astype(F32)

    def half_copy(c, k, j, half, target, s_sem, r_sem):
        return copy_to(
            total.at[c, j, :, halves[half]], target.at[c, k], s_sem.at[c, k], r_sem.at[c, k],
            up if k == 0 else down, lat,
        )

    def relay2_copy(c, k):
        return half_copy(c, k, 0, k, relay2, relay2_s, relay2_r)

    def side2_copy(c, k):
        return half_copy(c, k, 1 + k, 1 - k, side2, side2_s, side2_r)

    def final2_copy(c, k):
        return half_copy(c, k, 1 + k, k, final2, final2_s, final2_r)

    def wide_relay(c):
        total[c, 0] = wide_sum(c, 0).astype(BF16)
        for k in range(2):
            relay2_copy(c, k).start()

    def wide_side(c):
        for k in range(2):
            total[c, 1 + k] = wide_sum(c, 1 + k).astype(BF16)
            side2_copy(c, k).start()

    def wide_final(c):
        for k in range(2):
            relay2_copy(c, k).wait_recv()
            both = wide[c, 0, 1 + k, :, halves[k]].astype(F32) + wide[c, 1, 1 + k, :, halves[k]].astype(F32)
            total[c, 1 + k, :, halves[k]] = (both + relay2[c, k].astype(F32)).astype(BF16)
            final2_copy(c, k).start()

    def wide_fold(c):
        mine = wide_sum(c, 3)
        for k in range(2):
            side2_copy(c, k).wait_recv()
            final2_copy(c, k).wait_recv()
        u = []
        for k in range(8):
            half, cols = k // 4, pl.ds(256 * (k % 4), 256)
            u.append(
                mine[:, 256 * k : 256 * k + 256]
                + final2[c, half, :, cols].astype(F32)
                + side2[c, 1 - half, :, cols].astype(F32)
            )
        keep(c, u)

    def first_copy(dest):
        return copy_to(send.at[dest], held.at[flip], first_s, first_r, shot, dest)

    def second_copy(dest):
        return copy_to(back.at[dest], got.at[lat], second_s, second_r, shot, dest)

    lane = lax.broadcasted_iota(jnp.int32, (1, 128), 1)
    low = lane < 64
    packed = (lax.broadcasted_iota(jnp.int32, (8, 128), 0) == 7) & (lat == 16)
    seventh = lax.broadcasted_iota(jnp.int32, (8, 128), 0) == 7

    partner = LAT - 1 - lat
    corner = jnp.where(lat == 0, 16, LAT - lat)

    def mirror_copy():
        return copy_to(
            mir_ids.at[:, pl.ds(0, 32), :], mir_in, wedge_s.at[0], wedge_r.at[0], shot, partner
        )

    def corner_copy(k):
        src = (own_ids if k == 0 else mir_ids).at[:, pl.ds(32, 16), :]
        return copy_to(src, spec_in.at[k], wedge_s.at[1 + k], wedge_r.at[1 + k], shot, corner)

    def wedges_out():
        for k in range(3):
            tables[k].wait()
        ids = wedge[...].astype(F32).astype(BF16)
        chosen = jnp.dot(pick[...], ids, preferred_element_type=F32).astype(BF16)
        own, mir = chosen[:48], chosen[48:]
        tall = jnp.concatenate([own[:, 128 * t : 128 * t + 128] for t in range(16)], axis=0)
        moved = jnp.dot(tall, lanet[0:128, :], preferred_element_type=F32)
        for t, tile in enumerate(spread([moved[48 * t : 48 * t + 48] for t in range(16)], lane)):
            own_ids[t] = tile.astype(BF16)
        tall = jnp.concatenate(
            [
                jnp.concatenate(
                    [mir[:, 128 * (15 - t) : 128 * (16 - t)],
                     mir[:, 128 * ((16 - t) % 16) : 128 * ((16 - t) % 16) + 128]],
                    axis=1,
                )
                for t in range(16)
            ],
            axis=0,
        )
        moved = jnp.dot(tall, lanet[128:384, :], preferred_element_type=F32)
        for t, tile in enumerate(spread([moved[48 * t : 48 * t + 48] for t in range(16)], lane)):
            mir_ids[t] = tile.astype(BF16)

    def wedges_go():
        mirror_copy().start()

        @pl.when(lat < 16)
        def _():
            for k in range(2):
                corner_copy(k).start()

    def look_up(ids):
        found = jnp.full(ids.shape, levels[0], F32)
        for w in range(1, 16):
            found = jnp.where(ids == float(w), levels[w], found)
        return found

    def wedges_in():
        mirror_copy().wait_recv()

        @pl.when(lat >= 16)
        def _():
            for k in range(2):
                corner_copy(k).wait_recv()

        @pl.loop(0, 16)
        def _(kk):
            own = own_ids[kk].astype(F32)
            mir = mir_ids[kk].astype(F32)
            got_mir = mir_in[kk].astype(F32)
            spec_own = spec_in[0, kk].astype(F32)
            spec_mir = spec_in[1, kk].astype(F32)
            level1[kk, 0:8, :] = look_up(jnp.where(seventh & (lat >= 16), own[32:40], own[0:8]))
            level1[kk, 8:32, :] = look_up(own[8:32])
            level1[kk, 32:40, :] = look_up(spec_own[0:8])
            row = jnp.where(lat == 16, mir[32:40], spec_mir[0:8])
            level2[kk, 0:8, :] = look_up(jnp.where(seventh & (lat >= 16), row, got_mir[0:8]))
            level2[kk, 8:32, :] = look_up(got_mir[8:32])
            level2[kk, 32:40, :] = look_up(spec_mir[0:8])

    def stack():
        wide_prepare(0)
        pl.semaphore_wait(barrier, LAT + 2)
        wide_launch(0)
        begin(2)
        wide_prepare(1)
        wide_launch(1)
        begin(3)
        wedges_out()
        wedges_go()
        forward(2)
        forward(3)
        wide_relay(0)
        wide_side(0)
        across(2)
        across(3)
        wide_final(0)
        wide_relay(1)
        wide_side(1)
        wide_final(1)
        wide_fold(0)
        for k in range(3, 7):
            tables[k].wait()
        wide_fold(1)
        fold(2)
        fold(3)

    def columns():
        pieces = [
            lax.dot_general(ft[:, 0:1024], folded0[...], NT, preferred_element_type=F32).reshape(LAT, 8, 128)
        ]
        for s in range(3):
            pieces.append(
                lax.dot_general(
                    ft[:, 1024 + 512 * s : 1536 + 512 * s], folded1[s], NT, preferred_element_type=F32
                ).reshape(LAT, 8, 128)
            )
        for k in range(2):
            both = jnp.concatenate([pieces[2 * k], pieces[2 * k + 1]], axis=1)
            send[:, 16 * k : 16 * k + 16, :] = both.astype(BF16)

        @pl.loop(1, LAT)
        def _(k):
            first_copy((lat + k) % LAT).start()

        held[flip] = send[lat]
        wedges_in()
        all_but_one = held.at[pl.ds(0, LAT - 1)]
        pltpu.make_async_copy(all_but_one, all_but_one, first_r).wait()

    def unpack():
        nothing = jnp.zeros((8, 128), F32)
        for p in range(16):
            u0, u1 = held[2 * p].astype(F32), held[2 * p + 1].astype(F32)
            re = jnp.where(low, u0, pltpu.roll(u1, 64, 1))
            im = jnp.where(low, pltpu.roll(u0, 64, 1), u1)
            xr[p, 0:32, :] = re
            xi[p, 0:8, :] = jnp.where(packed, 0.0, im[0:8])
            xi[p, 8:32, :] = im[8:32]
            xr[p, 32:40, :] = im[0:8]
            xi[p, 32:40, :] = nothing

    def lateral(sign):
        base = 0 if sign < 0 else 2

        @pl.loop(0, 5)
        def _(g):
            at = pl.ds(pl.multiple_of(8 * g, 8), 8)
            values = []
            for p in range(16):
                value = (xr[p, at, :], xi[p, at, :])
                if sign > 0:
                    cos, sin = tw[base, p : p + 1, :], tw[base + 1, p : p + 1, :]
                    value = (value[0] * cos - value[1] * sin, value[1] * cos + value[0] * sin)
                values.append(value)
            for p, value in enumerate(short_transform(values, sign)):
                if sign < 0:
                    cos, sin = tw[base, p : p + 1, :], tw[base + 1, p : p + 1, :]
                    value = (value[0] * cos - value[1] * sin, value[1] * cos + value[0] * sin)
                xr[p, at, :] = value[0]
                xi[p, at, :] = value[1]

    def middle():
        lateral(-1)
        for b in range(4):
            some = pl.ds(4 * b, 4)
            both = jnp.concatenate([xr[some].reshape(160, 128), xi[some].reshape(160, 128)], axis=1)
            spectrum = jnp.dot(both.astype(BF16), xt[0:256, :], preferred_element_type=F32)
            re, im = spectrum[:, :128], spectrum[:, 128:]
            inverse = lax.rsqrt(jnp.maximum(re * re + im * im, 1e-30))
            factor = jnp.maximum(1.0 - level1[some].reshape(160, 128) * inverse, 0.0)
            factor += jnp.maximum(1.0 - level2[some].reshape(160, 128) * inverse, 0.0)
            both = jnp.concatenate([re * factor, im * factor], axis=1)
            inner = jnp.dot(both.astype(BF16), xt[256:512, :], preferred_element_type=F32)
            xr[some] = inner[:, :128].reshape(4, 40, 128)
            xi[some] = inner[:, 128:].reshape(4, 40, 128)
        lateral(1)

    def turn_back():
        for p in range(16):
            re, im = xr[p, 0:32, :], xi[p, 0:32, :]
            im = jnp.concatenate([jnp.where(packed, xr[p, 32:40, :], im[0:8]), im[8:32]], axis=0)
            back[2 * p] = jnp.where(low, re, pltpu.roll(im, 64, 1)).astype(BF16)
            back[2 * p + 1] = jnp.where(low, pltpu.roll(re, 64, 1), im).astype(BF16)

        @pl.loop(1, LAT)
        def _(k):
            second_copy((lat + k) % LAT).start()

        got[lat] = back[lat]
        all_but_one = got.at[pl.ds(0, LAT - 1)]
        pltpu.make_async_copy(all_but_one, all_but_one, second_r).wait()

    def columns_back():
        for s in range(4):
            tall = got[:, 16 * (s // 2) : 16 * (s // 2) + 16, :].astype(F32)
            flat = tall[:, 8 * (s % 2) : 8 * (s % 2) + 8, :].reshape(256, 128).T.astype(BF16)
            wide = jnp.concatenate([flat[:64], flat[64:]], axis=1)
            mid[s] = jnp.dot(wide, it[512 * s : 512 * s + 512, :], preferred_element_type=F32)

        @pl.loop(0, 8)
        def _(g):
            at = pl.ds(pl.multiple_of(8 * g, 8), 8)
            parts = [(mid[s, at, 0:256], mid[s, at, 256:512]) for s in range(4)]
            even, odd = real_eight_back(parts[0][0], parts[0][1], parts[1], parts[2], parts[3])
            for k in range(4):
                out[0, at, 256 * k : 256 * k + 256] = even[k] + odd[k]
                out[0, at, 1024 + 256 * k : 1280 + 256 * k] = even[k] - odd[k]

    def drain():
        for c in range(2, CHUNKS):
            for k in range(2):
                relay_copy(c, k).wait_send()
                side_copy(c, k).wait_send()
                final_copy(c, k).wait_send()
                cross_copy(c, k).wait_send()
        for c in range(2):
            for k in range(2):
                relay2_copy(c, k).wait_send()
                side2_copy(c, k).wait_send()
                final2_copy(c, k).wait_send()
                for j in range(4):
                    wide_copy(c, j, k).wait_send()
        sent = send.at[pl.ds(0, LAT - 1)]
        pltpu.make_async_copy(sent, sent, first_s).wait()
        sent = back.at[pl.ds(0, LAT - 1)]
        pltpu.make_async_copy(sent, sent, second_s).wait()
        mirror_copy().wait_send()

        @pl.when(lat < 16)
        def _():
            for k in range(2):
                corner_copy(k).wait_send()


    stack()
    columns()
    unpack()
    middle()
    turn_back()
    columns_back()
    drain()


def on_device(partials, wedges, levels):
    tables = [
        jnp.asarray(t)
        for t in (
            forward_tables(), inverse_tables(), lateral_tables(), turn_tables(), pick_tables(), lane_tables()
        )
    ]
    anywhere = pl.BlockSpec(memory_space=pltpu.HBM)
    vmem, dma = pltpu.VMEM, pltpu.SemaphoreType.DMA
    two = dma((CHUNKS, 2))
    doubled = pl.pallas_call(
        kernel,
        out_shape=jax.ShapeDtypeStruct((1, ROWS, N), F32),
        in_specs=[anywhere, anywhere, pl.BlockSpec(memory_space=pltpu.SMEM)] + [anywhere] * 6,
        out_specs=pl.BlockSpec(memory_space=pltpu.VMEM),
        scratch_shapes=[
            vmem(partials.shape, BF16),
            vmem(wedges.shape, jnp.int32),
            *[vmem(t.shape, t.dtype) for t in tables],
            vmem((CHUNKS, 2, CROWS, N), BF16),
            vmem((CHUNKS, 2, CROWS, N), BF16),
            vmem((CHUNKS, 2, CROWS, N), BF16),
            vmem((CHUNKS, 2, CROWS, N), BF16),
            vmem((2, 2, 4, CROWS, N), BF16),
            vmem((2, 4, CROWS, N), BF16),
            vmem((2, 2, CROWS, N // 2), BF16),
            vmem((2, 2, CROWS, N // 2), BF16),
            vmem((2, 2, CROWS, N // 2), BF16),
            vmem((128, 1024), BF16),
            vmem((3, 128, 512), BF16),
            vmem((LAT, 32, 128), BF16),
            vmem((LAT, 32, 128), BF16),
            vmem((16, 40, 128), F32),
            vmem((16, 40, 128), F32),
            vmem((16, 40, 128), F32),
            vmem((16, 40, 128), F32),
            vmem((16, 48, 128), BF16),
            vmem((16, 48, 128), BF16),
            vmem((16, 32, 128), BF16),
            vmem((2, 16, 16, 128), BF16),
            vmem((LAT, 32, 128), BF16),
            vmem((LAT, 32, 128), BF16),
            vmem((4, ROWS, 512), F32),
            dma((CHUNKS,)),
            dma((7,)),
            two, two, two, two, two, two, two, two,
            dma, dma, dma, dma,
            dma((3,)),
            dma((3,)),
            dma((2, 4, 2)), dma((2, 4, 2)),
            dma((2, 2)), dma((2, 2)), dma((2, 2)), dma((2, 2)), dma((2, 2)), dma((2, 2)),
        ],
        compiler_params=pltpu.CompilerParams(
            collective_id=0, has_side_effects=True, vmem_limit_bytes=60 * 1024 * 1024
        ),
        name="stack_threshold",
    )(partials, wedges, levels, *tables)
    return doubled * 0.5


def solution(mesh):
    in_specs = (P("shot", None, "lat", None), P("lat", None), P())
    return jax.shard_map(
        on_device, mesh=mesh, in_specs=in_specs, out_specs=P("shot", "lat", None), check_vma=False
    )
```
